128 devices in a mesh: dp: 4 (over x), row: 4 (over y_hi, core), col: 8 (over y_lo, z).
Axes of the slice: x: 4, y: 4 (y_hi: 2, y_lo: 2; y = y_hi * 2 + y_lo), z: 4, core: 2. Of those that a mesh axis runs over, the one named last changes fastest.
Arguments:
- inputs: bfloat16 [16384, 1024], P(('dp', 'col'), 'row'), may hold values from -24 to 24
- scales: bfloat16 [2, 2, 1024], P(None, None, 'row'), may hold values from 0.5 to 1.5
- shifts: bfloat16 [2, 2, 1024], P(None, None, 'row'), may hold values from -1.5 to 1.5
- triples: bfloat16 [2, 1024, 3, 1024], P(None, 'row', None, 'col'), may hold values from -0.1875 to 0.1875
- offsets: bfloat16 [2, 3, 1024], P(None, None, 'col'), may hold values from -1.5 to 1.5
- merger: bfloat16 [2, 1024, 1024], P(None, 'col', 'row'), may hold values from -0.75 to 0.75
- expand: bfloat16 [2, 1024, 4096], P(None, 'row', 'col'), may hold values from -1 to 1
- uplift: bfloat16 [2, 4096], P(None, 'col'), may hold values from -1.5 to 1.5
- shrink: bfloat16 [2, 4096, 1024], P(None, 'col', 'row'), may hold values from -0.09375 to 0.09375
- closing: bfloat16 [2, 1024], P(None, 'row'), may hold values from -1.5 to 1.5
- cotangent: bfloat16 [16384, 1024], P(('dp', 'col'), 'row'), may hold values from -6 to 6
Outputs:
- outputs: bfloat16 [16384, 1024], P(('dp', 'col'), 'row')
- inputs_grad: float32 [16384, 1024], P(('dp', 'col'), 'row')
- scales_grad: float32 [2, 2, 1024], P(None, None, 'row')
- shifts_grad: float32 [2, 2, 1024], P(None, None, 'row')
- triples_grad: float32 [2, 1024, 3, 1024], P(None, 'row', None, 'col')
- offsets_grad: float32 [2, 3, 1024], P(None, None, 'col')
- merger_grad: float32 [2, 1024, 1024], P(None, 'col', 'row')
- expand_grad: float32 [2, 1024, 4096], P(None, 'row', 'col')
- uplift_grad: float32 [2, 4096], P(None, 'col')
- shrink_grad: float32 [2, 4096, 1024], P(None, 'col', 'row')
- closing_grad: float32 [2, 1024], P(None, 'row')
The draws below stay inside these ranges and needn't reach their ends.
All inputs are finite; a program needn't handle non-finite values.
Results may differ from the reference program's by a relative error of at most 0.03.
Values may be sent and summed in bfloat16 or wider, within the bound.
No kernel may reach another device: no remote copies, remote signals or barrier semaphores. Data moves between devices by JAX's collectives and lax.ppermute only.
A program may use at most 192 MiB of HBM per device.

```python
import math
import jax
import jax.numpy as jnp
from jax import lax

D = 1024
HEADS = 16
HEAD = 64
FF = 4096
ROT = 16
LAYERS = 2
LEN = 1024
SEQS = 16
TOKENS = 16384


def draw_inputs(key, part):
    key = jax.random.fold_in(key, 11)
    first_moment, second_moment, third, fourth = jax.random.split(key, 4)
    columns = jnp.exp(jnp.linspace(math.log(0.5), math.log(1.5), D))
    columns = columns * jax.random.uniform(first_moment, (D,), minval=0.7, maxval=1.4)
    rows = jnp.exp(jax.random.uniform(second_moment, (TOKENS, 1), minval=math.log(0.5), maxval=math.log(2.0)))
    base = jnp.clip(jax.random.normal(third, (TOKENS, D)), -5.0, 5.0)
    common = jnp.clip(0.3 * jax.random.normal(fourth, (1, D)), -0.6, 0.6)
    return ((base * columns[None, :] + common) * rows).astype(jnp.bfloat16)


def draw_expand(key, part):
    key = jax.random.fold_in(key, 23)
    first_key, second_key = jax.random.split(key, 2)
    factor = D ** (-0.5)
    entries = jnp.clip(jax.random.normal(first_key, (LAYERS, D, FF)), -6.0, 6.0) * factor
    shared = jnp.clip(jax.random.normal(second_key, (LAYERS, 1, FF)), -3.0, 3.0) * factor
    return jnp.clip(entries + shared, -1.0, 1.0).astype(jnp.bfloat16)


def steps_of(rng, shape, pieces, low, largest):
    def one(position, blocks):
        steps = jax.random.uniform(jax.random.fold_in(jax.random.fold_in(rng, 6), position), (blocks,), jnp.float32, low / len(pieces), largest / len(pieces))
        return jnp.repeat(jnp.exp(steps), shape[position] // blocks).reshape((-1,) + (1,) * (len(shape) - position - 1))

    factor_of = one(*pieces[0])
    for cut in pieces[1:]:
        factor_of = factor_of * one(*cut)
    return factor_of


def scatter_about(own_key, extent, spread, reach, pieces=(), dtype=jnp.bfloat16):
    values = jax.random.normal(own_key, extent, jnp.float32) * spread
    if len(pieces) > 0:
        values = steps_of(own_key, extent, pieces, -0.22, 0.18) * values
    return jnp.clip(values, min=-reach, max=reach).astype(dtype)


def setup_inputs(seed: int = 0) -> dict:
    key_list = jax.random.split(jax.random.key(seed), 12)
    inputs = draw_inputs(jax.random.fold_in(key_list[11], 71), 0)
    scales = jnp.clip(1.0 + 0.1 * jax.random.normal(key_list[1], (LAYERS, 2, D), jnp.float32), 0.5, 1.5).astype(jnp.bfloat16)
    shifts = scatter_about(key_list[2], (LAYERS, 2, D), 0.3, 1.5, ((2, 4),))
    triples = scatter_about(key_list[3], (LAYERS, D, 3, D), D ** -0.5, 0.1875, ((1, 4), (3, 8)))
    offsets = scatter_about(key_list[4], (LAYERS, 3, D), 0.3, 1.5, ((2, 8),))
    merger = scatter_about(key_list[5], (LAYERS, D, D), (D // 16) ** -0.5, 0.75, ((1, 8), (2, 4)))
    expand = draw_expand(jax.random.fold_in(key_list[11], 71), 0)
    uplift = scatter_about(key_list[7], (LAYERS, FF), 0.3, 1.5, ((1, 8),))
    shrink = scatter_about(key_list[8], (LAYERS, FF, D), FF ** -0.5, 0.09375, ((1, 8), (2, 4)))
    closing = scatter_about(key_list[9], (LAYERS, D), 0.3, 1.5, ((1, 4),))
    cotangent = scatter_about(key_list[10], (TOKENS, D), 1.0, 6.0, ((0, 32), (1, 4)))
    return dict(inputs=inputs, scales=scales, shifts=shifts, triples=triples, offsets=offsets, merger=merger, expand=expand, uplift=uplift, shrink=shrink, closing=closing, cotangent=cotangent)


NORM_EPSILON = 1e-05
HIGH = lax.Precision.HIGHEST

@jax.custom_vjp
def lower_precision(v):
    return lax.optimization_barrier(v.astype(jnp.bfloat16)).astype(jnp.float32)

@jax.custom_vjp
def low_back(v):
    return v

def low_keep(v):
    return (lower_precision(v), None)

def low_pass(kept, grad):
    return (grad,)

def back_keep(v):
    return (v, None)

def back_low(kept, grad):
    return (lower_precision(grad),)
lower_precision.defvjp(low_keep, low_pass)
low_back.defvjp(back_keep, back_low)

def tables(positions):
    inverse = 10000.0 ** (-jnp.arange(0, ROT, 2).astype(jnp.float32) / ROT)
    angles = positions.astype(jnp.float32)[:, None] * inverse[None, :]
    angles = jnp.concatenate([angles, angles], 1)
    return (jnp.cos(angles), jnp.sin(angles))

def rotate(field, cosine, sine):
    head = field[..., :ROT]
    turned = jnp.concatenate([-head[..., ROT // 2:], head[..., :ROT // 2]], -1)
    moved = head * cosine[:, None, :] + turned * sine[:, None, :]
    return jnp.concatenate([moved, field[..., ROT:]], -1)

def attend(parts):
    query, keys, values = parts
    scores = jnp.einsum('qhd,khd->hqk', query, keys, precision=HIGH) * HEAD ** (-0.5)
    scores = low_back(scores)
    allowed = jnp.arange(LEN)[:, None] >= jnp.arange(LEN)[None, :]
    scores = jnp.where(allowed[None], scores, -1e+30)
    probs = lower_precision(jax.nn.softmax(scores, -1))
    return jnp.einsum('hqk,khd->qhd', probs, values, precision=HIGH)

def layer(input_rows, norm_scale, norm_shift, triple, offset, merger, expand, uplift, shrink, closing, cosine, sine):
    groups = input_rows.shape[0]
    row_mean = lax.optimization_barrier(jnp.mean(input_rows, -1, keepdims=True))
    row_variance = lax.optimization_barrier(jnp.mean(input_rows * input_rows, -1, keepdims=True)) - row_mean * row_mean
    normalized_input = (input_rows - row_mean) * lax.rsqrt(row_variance + NORM_EPSILON)
    first_moment = lower_precision(normalized_input * norm_scale[0] + norm_shift[0])
    second_moment = lower_precision(normalized_input * norm_scale[1] + norm_shift[1])
    qkv = low_back(jnp.einsum('gld,dce->glce', first_moment, triple, precision=HIGH) + offset)
    split = qkv.reshape(groups, LEN, 3, HEADS, HEAD)
    query = lower_precision(rotate(split[:, :, 0], cosine, sine))
    keys = lower_precision(rotate(split[:, :, 1], cosine, sine))
    values = lower_precision(split[:, :, 2])
    mixed = lax.map(jax.checkpoint(attend), (query, keys, values)).reshape(groups, LEN, D)
    mixed = low_back(lower_precision(mixed))
    upper = low_back(jnp.einsum('gld,df->glf', second_moment, expand, precision=HIGH) + uplift)
    hidden = lower_precision(jax.nn.gelu(upper, approximate=False))
    out = jnp.einsum('gld,de->gle', mixed, merger, precision=HIGH)
    out = out + jnp.einsum('glf,fe->gle', hidden, shrink, precision=HIGH) + closing
    return input_rows + low_back(out)

def reference(inputs, scales, shifts, triples, offsets, merger, expand, uplift, shrink, closing, cotangent):
    params = (scales.astype(jnp.float32), shifts.astype(jnp.float32), triples.astype(jnp.float32), offsets.astype(jnp.float32), merger.astype(jnp.float32), expand.astype(jnp.float32), uplift.astype(jnp.float32), shrink.astype(jnp.float32), closing.astype(jnp.float32))
    cosine, sine = tables(jnp.arange(LEN))
    group = math.gcd(SEQS, max(1, 4096 // LEN))
    count = SEQS // group
    states = inputs.astype(jnp.float32).reshape(count, group, LEN, D)
    cotans = cotangent.astype(jnp.float32).reshape(count, group, LEN, D)

    def forward(input_rows, weights):
        for index in range(LAYERS):
            input_rows = layer(input_rows, *[w[index] for w in weights], cosine, sine)
        return input_rows

    def step(total, item):
        input_rows, ct = item
        y, pull = jax.vjp(forward, input_rows, params)
        dx, dparams = pull(ct)
        return (jax.tree.map(jnp.add, total, dparams), (y, dx))
    zeros = jax.tree.map(jnp.zeros_like, params)
    total, (ys, dxs) = lax.scan(step, zeros, (states, cotans))
    return (ys.reshape(TOKENS, D).astype(jnp.bfloat16), dxs.reshape(TOKENS, D), total[0], total[1], total[2], total[3], total[4], total[5], total[6], total[7], total[8])
```

```python
from functools import partial

import jax
import jax.numpy as jnp
import numpy as np
from jax import lax
from jax.experimental import pallas as pl
from jax.experimental.pallas import tpu as pltpu
from jax.sharding import Mesh
from jax.sharding import PartitionSpec as P

D = 1024
HEAD = 64
ROT = 16
LAYERS = 2
LEN = 1024
HEADS = 2
INNER = HEADS * HEAD
QKV = 3 * INNER
HID = 512
WIDE = QKV + HID
NORM_EPSILON = 1e-05
BF = jnp.bfloat16
F32 = jnp.float32
NN = (((1,), (0,)), ((), ()))
NT = (((1,), (1,)), ((), ()))


def dot(a, b, dims=NN):
    return lax.dot_general(a, b, dims, preferred_element_type=F32)


def call(kernel, out_shape, grid, in_specs, out_specs, flops=0, moved=0, scratch=()):
    return pl.pallas_call(
        kernel,
        out_shape=out_shape,
        grid=grid,
        in_specs=in_specs,
        out_specs=out_specs,
        scratch_shapes=scratch,
        compiler_params=pltpu.CompilerParams(vmem_limit_bytes=48 * 2**20),
        cost_estimate=pl.CostEstimate(flops=flops, bytes_accessed=moved, transcendentals=0),
    )


def rotary_tables():
    inverse = 10000.0 ** (-jnp.arange(0, ROT, 2).astype(F32) / ROT)
    angles = jnp.arange(LEN).astype(F32)[:, None] * inverse[None, :]
    cosine, sine = jnp.cos(angles), jnp.sin(angles)
    zero = jnp.zeros_like(sine)
    rest = jnp.zeros((LEN, HEAD - ROT), F32)
    keep = jnp.concatenate([cosine, cosine, rest + 1.0], 1)
    low = jnp.concatenate([-sine, zero, rest], 1)
    high = jnp.concatenate([zero, sine, rest], 1)
    return tuple(jnp.concatenate([t] * HEADS, 1) for t in (keep, low, high))


def turn(u, keep, low, high, sign):
    half = ROT // 2
    back = pltpu.roll(u, INNER - half, 1)
    ahead = pltpu.roll(u, half, 1)
    return u * keep + sign * (back * low + ahead * high)


def project_kernel(xhat, wide, norms, bias, keep, low, high, query, keys, values, hidden, slope):
    xh = xhat[...].astype(F32)
    n_a = (xh * norms[0:1] + norms[2:3]).astype(BF)
    n_f = (xh * norms[1:2] + norms[3:4]).astype(BF)
    qkv = dot(n_a, wide[:, :QKV]) + bias[0:1, :QKV]
    tables = (keep[...], low[...], high[...])
    query[...] = (turn(qkv[:, :INNER], *tables, 1.0).astype(BF) * 0.125).astype(BF)
    keys[...] = turn(qkv[:, INNER : 2 * INNER], *tables, 1.0).astype(BF)
    values[...] = qkv[:, 2 * INNER :].astype(BF)
    u = dot(n_f, wide[:, QKV:]) + bias[0:1, QKV:]
    cdf = 0.5 + 0.5 * lax.erf(u * (0.5**0.5))
    hidden[...] = (u * cdf).astype(BF)
    slope[...] = (cdf + u * (jnp.exp(u * u * -0.5) * (1.0 / (2.0 * np.pi) ** 0.5))).astype(BF)


def project(xhat, wide, norms, bias, tables):
    rows = 256
    block = lambda w: pl.BlockSpec((rows, w), lambda i: (i, 0))
    whole = lambda s: pl.BlockSpec(s, lambda i: (0, 0))
    shape = lambda w: jax.ShapeDtypeStruct((LEN, w), BF)
    return call(
        project_kernel,
        [shape(INNER), shape(INNER), shape(INNER), shape(HID), shape(HID)],
        (LEN // rows,),
        [block(D), whole((D, WIDE)), whole((4, D)), whole((1, WIDE))] + [block(INNER)] * 3,
        [block(INNER)] * 3 + [block(HID)] * 2,
        flops=2 * LEN * D * WIDE * 3,
        moved=LEN * D * 2 + D * WIDE * 2 + 4 * LEN * WIDE,
    )(xhat, wide, norms, bias, *tables)


BLOCK = 256


def head_mask(h, rows):
    lane = lax.broadcasted_iota(jnp.int32, (rows, INNER), 1)
    return (lane // HEAD) == h


def causal(n, start):
    key = lax.broadcasted_iota(jnp.int32, (n, BLOCK), 0)
    query = lax.broadcasted_iota(jnp.int32, (n, BLOCK), 1)
    return key <= query


def attend_kernel(query, keys, values, mixed, logs):
    for i in range(LEN // BLOCK):
        n = (i + 1) * BLOCK
        here = pl.ds(i * BLOCK, BLOCK)
        q = query[here, :]
        out = jnp.zeros((BLOCK, INNER), F32)
        for h in range(HEADS):
            mask = head_mask(h, BLOCK)
            qh = jnp.where(mask, q, jnp.zeros_like(q))
            s = dot(keys[:n, :], qh, NT)
            tail = jnp.where(causal(BLOCK, 0), s[n - BLOCK :], -1e30)
            s = jnp.concatenate([s[: n - BLOCK], tail], 0) if i else tail
            top = jnp.max(s, 0, keepdims=True)
            p = jnp.exp(s - top)
            total = jnp.sum(p, 0, keepdims=True)
            logs[h : h + 1, here] = top + jnp.log(total)
            part = lax.dot_general(
                values[:n, :], p.astype(BF), (((0,), (0,)), ((), ())), preferred_element_type=F32
            )
            part = jnp.transpose(part * (1.0 / total))
            out = jnp.where(mask, part, out)
        mixed[here, :] = out.astype(BF)


def attend(query, keys, values):
    return call(
        attend_kernel,
        [jax.ShapeDtypeStruct((LEN, INNER), BF), jax.ShapeDtypeStruct((8, LEN), F32)],
        (),
        [pl.BlockSpec(memory_space=pltpu.VMEM)] * 3,
        [pl.BlockSpec(memory_space=pltpu.VMEM)] * 2,
        flops=4 * HEADS * LEN * LEN * 256,
        moved=4 * LEN * INNER * 2,
    )(query, keys, values)


def attend_back_kernel(query, keys, values, dmixed, logs, keep, low, high, dqkv, sums, dkeys, dvalues):
    dkeys[...] = jnp.zeros_like(dkeys)
    dvalues[...] = jnp.zeros_like(dvalues)
    tables = lambda at: (keep[at, :], low[at, :], high[at, :])
    count = jnp.zeros((1, INNER), F32)
    for i in range(LEN // BLOCK):
        n = (i + 1) * BLOCK
        here = pl.ds(i * BLOCK, BLOCK)
        q, do = query[here, :], dmixed[here, :]
        dq = jnp.zeros((BLOCK, INNER), F32)
        for h in range(HEADS):
            mask = head_mask(h, BLOCK)
            qh = jnp.where(mask, q, jnp.zeros_like(q))
            doh = jnp.where(mask, do, jnp.zeros_like(do))
            s = dot(keys[:n, :], qh, NT)
            p = jnp.exp(s - logs[h : h + 1, here])
            tail = jnp.where(causal(BLOCK, 0), p[n - BLOCK :], 0.0)
            p = jnp.concatenate([p[: n - BLOCK], tail], 0) if i else tail
            dp = dot(values[:n, :], doh, NT)
            w = p * dp
            delta = jnp.sum(w, 0, keepdims=True)
            ds = (w - p * delta).astype(BF)
            dvalues[:n, :] += dot(p.astype(BF), doh)
            dkeys[:n, :] += dot(ds, qh)
            part = lax.dot_general(
                keys[:n, :], ds, (((0,), (0,)), ((), ())), preferred_element_type=F32
            )
            dq = jnp.where(mask, jnp.transpose(part), dq)
        dq = turn(dq * 0.125, *tables(here), -1.0).astype(BF)
        dqkv[here, :INNER] = dq
        count += jnp.sum(dq.astype(F32), 0, keepdims=True)
    sums[0:1, :INNER] = count
    every = pl.ds(0, LEN)
    dk = turn(dkeys[...], *tables(every), -1.0).astype(BF)
    dv = dvalues[...].astype(BF)
    dqkv[:, INNER : 2 * INNER] = dk
    dqkv[:, 2 * INNER :] = dv
    sums[0:1, INNER : 2 * INNER] = jnp.sum(dk.astype(F32), 0, keepdims=True)
    sums[0:1, 2 * INNER :] = jnp.sum(dv.astype(F32), 0, keepdims=True)


def attend_back(query, keys, values, dmixed, logs, tables):
    return call(
        attend_back_kernel,
        [jax.ShapeDtypeStruct((LEN, QKV), BF), jax.ShapeDtypeStruct((8, QKV), F32)],
        (),
        [pl.BlockSpec(memory_space=pltpu.VMEM)] * 8,
        [pl.BlockSpec(memory_space=pltpu.VMEM)] * 2,
        flops=10 * HEADS * LEN * LEN * 256,
        moved=8 * LEN * INNER * 2 + 3 * LEN * INNER * 4,
        scratch=[pltpu.VMEM((LEN, INNER), F32)] * 2,
    )(query, keys, values, dmixed, logs, *tables)


def merge_kernel(side, mixed, hidden, down, out):
    out[...] = (dot(mixed[...], down[:INNER]) + dot(hidden[...], down[INNER:])).astype(BF)


def merge(side, mixed, hidden, down):
    rows = LEN // 2
    return pl.pallas_call(
        merge_kernel,
        out_shape=jax.ShapeDtypeStruct((rows, D), BF),
        grid_spec=pltpu.PrefetchScalarGridSpec(
            num_scalar_prefetch=1,
            grid=(2,),
            in_specs=[
                pl.BlockSpec((rows // 2, INNER), lambda i, s: (s[0] * 2 + i, 0)),
                pl.BlockSpec((rows // 2, HID), lambda i, s: (s[0] * 2 + i, 0)),
                pl.BlockSpec((INNER + HID, D), lambda i, s: (0, 0)),
            ],
            out_specs=pl.BlockSpec((rows // 2, D), lambda i, s: (i, 0)),
        ),
        compiler_params=pltpu.CompilerParams(vmem_limit_bytes=48 * 2**20),
        cost_estimate=pl.CostEstimate(
            flops=2 * rows * D * (INNER + HID), bytes_accessed=rows * D * 4, transcendentals=0
        ),
    )(side, mixed, hidden, down)


def branch_kernel(dy, down, slope, dmixed, dupper, sums, total):
    @pl.when(pl.program_id(0) == 0)
    def _():
        sums[...] = jnp.zeros_like(sums)
        total[...] = jnp.zeros_like(total)

    g = dy[...]
    total[0:1] += jnp.sum(g.astype(F32), 0, keepdims=True)
    dmixed[...] = dot(g, down[:INNER], NT).astype(BF)
    du = (dot(g, down[INNER:], NT) * slope[...].astype(F32)).astype(BF)
    dupper[...] = du
    sums[0:1] += jnp.sum(du.astype(F32), 0, keepdims=True)


def branch(dy, down, slope):
    rows = 256
    block = lambda w: pl.BlockSpec((rows, w), lambda i: (i, 0))
    whole = lambda s: pl.BlockSpec(s, lambda i: (0, 0))
    return call(
        branch_kernel,
        [
            jax.ShapeDtypeStruct((LEN, INNER), BF),
            jax.ShapeDtypeStruct((LEN, HID), BF),
            jax.ShapeDtypeStruct((8, HID), F32),
            jax.ShapeDtypeStruct((8, D), F32),
        ],
        (LEN // rows,),
        [block(D), whole((INNER + HID, D)), block(HID)],
        [block(INNER), block(HID), whole((8, HID)), whole((8, D))],
        flops=2 * LEN * D * (INNER + HID),
        moved=LEN * D * 2 + 4 * LEN * HID,
    )(dy, down, slope)


def spread_kernel(side, dqkv, dupper, wide, norms, out):
    first = dot(dqkv[...], wide[:, :QKV], NT) * norms[0:1]
    out[...] = (first + dot(dupper[...], wide[:, QKV:], NT) * norms[1:2]).astype(BF)


def spread(side, dqkv, dupper, wide, norms):
    rows = LEN // 2
    return pl.pallas_call(
        spread_kernel,
        out_shape=jax.ShapeDtypeStruct((rows, D), BF),
        grid_spec=pltpu.PrefetchScalarGridSpec(
            num_scalar_prefetch=1,
            grid=(2,),
            in_specs=[
                pl.BlockSpec((rows // 2, QKV), lambda i, s: (s[0] * 2 + i, 0)),
                pl.BlockSpec((rows // 2, HID), lambda i, s: (s[0] * 2 + i, 0)),
                pl.BlockSpec((D, WIDE), lambda i, s: (0, 0)),
                pl.BlockSpec((4, D), lambda i, s: (0, 0)),
            ],
            out_specs=pl.BlockSpec((rows // 2, D), lambda i, s: (i, 0)),
        ),
        compiler_params=pltpu.CompilerParams(vmem_limit_bytes=48 * 2**20),
        cost_estimate=pl.CostEstimate(
            flops=2 * rows * D * WIDE, bytes_accessed=rows * D * 4, transcendentals=0
        ),
    )(side, dqkv, dupper, wide, norms)


AXES = ("x", "yh", "core", "yl", "zh", "zl")
LINE = ("zh", "zl")
RING = ("yh", "yl")
OWN = LEN // 8


def index(array, at):
    return lax.dynamic_index_in_dim(array, at, 0, False)


def across(array):
    return lax.ppermute(array, "core", [(0, 1), (1, 0)])


def around(array, axes, step):
    return lax.ppermute(array, axes, [(i, (i + step) % 4) for i in range(4)])


def place(pieces):
    shape = pieces[0][1].shape
    whole = jnp.zeros((len(pieces),) + shape, pieces[0][1].dtype)
    for at, piece in pieces:
        whole = lax.dynamic_update_index_in_dim(whole, piece, at, 0)
    return whole


def gather_line(own):
    z, core = lax.axis_index(LINE), lax.axis_index("core")
    pieces = [(z, own)] + [((z - k) % 4, around(own, LINE, k)) for k in (1, 3, 2)]
    half = place(pieces)
    whole = place([(core, half), (1 - core, across(half))])
    return whole.reshape(LEN, own.shape[1])


def scatter_line(mine, other):
    z = lax.axis_index(LINE)
    both = (mine.astype(F32) + across(other).astype(F32)).reshape(4, OWN, mine.shape[1])
    total = index(both, z)
    for k in (1, 3, 2):
        total = total + around(index(both, (z + k) % 4).astype(BF), LINE, k).astype(F32)
    return total


def exchange_perm(step, inward):
    pairs = []
    for q in range(4):
        for zh in range(2):
            for core in range(2):
                z = (q - step) % 4
                outer = ((q // 2) * 2 + q % 2) * 4 + zh * 2 + core
                inner = (zh * 2 + core) * 4 + z
                pairs.append((outer, inner) if inward else (inner, outer))
    return pairs


def inward(block):
    q = lax.axis_index(("yh", "core"))
    z = lax.axis_index(LINE)
    rows = block.reshape(4, OWN, block.shape[1])
    pieces = []
    for k in range(4):
        piece = index(rows, (q - k) % 4)
        piece = lax.ppermute(piece, ("yh", "core", "zh", "zl"), exchange_perm(k, True))
        pieces.append(((z + k) % 4, piece))
    return jnp.transpose(place(pieces), (1, 0, 2)).reshape(OWN, D)


def outward(own):
    q = lax.axis_index(("yh", "core"))
    z = lax.axis_index(LINE)
    columns = jnp.transpose(own.reshape(OWN, 4, D // 4), (1, 0, 2))
    pieces = []
    for k in range(4):
        piece = index(columns, (z + k) % 4)
        piece = lax.ppermute(piece, ("yh", "core", "zh", "zl"), exchange_perm(k, False))
        pieces.append(((q - k) % 4, piece))
    return place(pieces).reshape(4 * OWN, D // 4)


def fetch(shard):
    core = lax.axis_index("core")
    both = lax.all_gather(shard, RING, axis=0, tiled=False).reshape((2, 2) + shard.shape)
    kept = lax.dynamic_index_in_dim(both, core, 1, False)
    got = across(lax.dynamic_index_in_dim(both, 1 - core, 1, False))
    pair = place([(core, kept), (1 - core, got)])
    return jnp.swapaxes(pair, 0, 1).reshape((4,) + shard.shape)


def give(quarters):
    core = lax.axis_index("core")
    split = quarters.reshape((2, 2) + quarters.shape[1:])
    kept = lax.dynamic_index_in_dim(split, core, 1, False)
    got = across(lax.dynamic_index_in_dim(split, 1 - core, 1, False))
    pair = place([(core, kept), (1 - core, got)])
    chunks = jnp.swapaxes(pair, 0, 1).reshape((4,) + quarters.shape[1:])
    summed = lax.psum_scatter(chunks, RING, scatter_dimension=0, tiled=False)
    return lax.psum(summed, "x")


def normalize(x):
    mean = jnp.mean(x, 1, keepdims=True)
    r = lax.rsqrt(jnp.mean(x * x, 1, keepdims=True) - mean * mean + NORM_EPSILON)
    return (x - mean) * r, r


EXTRA = 16


def pack_wide(scales, shifts, triple, offset, expand, uplift):
    body = jnp.concatenate([triple.reshape(D // 4, QKV), expand], 1)
    bias = jnp.concatenate([offset.reshape(1, QKV), uplift.reshape(1, HID)], 1)
    norms = jnp.concatenate([scales, shifts], 0).reshape(1, 2, 2 * (D // 4))
    norms = jnp.pad(norms[0], ((0, 0), (0, WIDE - 2 * (D // 4))))
    rest = jnp.zeros((EXTRA - 3, WIDE), BF)
    return jnp.concatenate([body, bias, norms, rest], 0)


def unpack_wide(pieces):
    quarter = D // 4
    wide = pieces[:, :quarter].reshape(D, WIDE)
    bias = pieces[0, quarter : quarter + 1].astype(F32)
    norms = pieces[:, quarter + 1 : quarter + 3, : 2 * quarter].reshape(4, 4, quarter)
    norms = jnp.transpose(norms, (1, 0, 2)).reshape(4, D).astype(F32)
    return wide, bias, norms


def pack_down(merger, shrink, closing):
    rest = jnp.zeros((EXTRA - 1, D // 4), BF)
    return jnp.concatenate([merger, shrink, closing[None], rest], 0)


def unpack_down(pieces):
    joined = jnp.transpose(pieces, (1, 0, 2)).reshape(-1, D)
    return joined[: INNER + HID], joined[INNER + HID : INNER + HID + 1].astype(F32)


def weight_grad(left, right):
    return jnp.einsum("tc,td->cd", left, right, preferred_element_type=F32)


def shards(
    inputs, scales, shifts, triples, offsets, merger, expand, uplift, shrink, closing, cotangent
):
    core = lax.axis_index("core")
    here, there = core.reshape(1).astype(jnp.int32), (1 - core).reshape(1).astype(jnp.int32)
    tables = rotary_tables()
    x = inward(inputs).astype(F32)
    wides, downs = [], []
    for l in range(LAYERS):
        packed = pack_wide(scales[l], shifts[l], triples[l], offsets[l], expand[l], uplift[l])
        wides.append(unpack_wide(fetch(packed)))
        downs.append(unpack_down(fetch(pack_down(merger[l], shrink[l], closing[l]))))
    top = gather_line(inward(cotangent))
    saved = []
    for l in range(LAYERS):
        wide, bias, norms = wides[l]
        down, close = downs[l]
        xhat, r = normalize(x)
        full = gather_line(xhat.astype(BF))
        query, keys, values, hidden, slope = project(full, wide, norms, bias, tables)
        mixed, logs = attend(query, keys, values)
        other = merge(there, mixed, hidden, down)
        mine = merge(here, mixed, hidden, down)
        x = x + scatter_line(mine, other) + close
        saved.append((xhat, r, full, query, keys, values, hidden, slope, mixed, logs))
    outputs = outward(x.astype(BF))
    gradient = inward(cotangent).astype(F32)
    sums = [None] * LAYERS
    for l in reversed(range(LAYERS)):
        wide, bias, norms = wides[l]
        down, close = downs[l]
        xhat, r, full, query, keys, values, hidden, slope, mixed, logs = saved[l]
        dy = top if l == LAYERS - 1 else gather_line(gradient.astype(BF))
        dmixed, dupper, up_sum, close_sum = branch(dy, down, slope)
        down_grad = jnp.concatenate([weight_grad(mixed, dy), weight_grad(hidden, dy)], 0)
        down_grad = jnp.concatenate([down_grad, close_sum, jnp.zeros((EXTRA - 8, D), F32)], 0)
        down_grad = jnp.transpose(down_grad.astype(BF).reshape(-1, 4, D // 4), (1, 0, 2))
        dqkv, qkv_sum = attend_back(query, keys, values, dmixed, logs, tables)
        other = spread(there, dqkv, dupper, wide, norms)
        mine = spread(here, dqkv, dupper, wide, norms)
        wide_grad = jnp.concatenate([weight_grad(full, dqkv), weight_grad(full, dupper)], 1)
        wide_grad = wide_grad.astype(BF).reshape(4, D // 4, WIDE)
        bias_sum = jnp.concatenate([qkv_sum, up_sum], 1).astype(BF)
        bias_sum = jnp.broadcast_to(
            jnp.pad(bias_sum, ((0, EXTRA - 8), (0, 0)))[None], (4, EXTRA, WIDE)
        )
        wide_grad = jnp.concatenate([wide_grad, bias_sum], 1)
        dxhat = scatter_line(mine, other)
        gradient = gradient + r * (
            dxhat
            - jnp.mean(dxhat, 1, keepdims=True)
            - xhat * jnp.mean(dxhat * xhat, 1, keepdims=True)
        )
        sums[l] = (give(wide_grad), give(down_grad))
    inputs_grad = outward(gradient)
    quarter = D // 4
    grads = []
    for l in range(LAYERS):
        wide_sum, down_sum = (s.astype(F32) for s in sums[l])
        product, bias_sum = wide_sum[:quarter], wide_sum[quarter]
        scale, shift = scales[l].astype(F32), shifts[l].astype(F32)
        flat = triples[l].reshape(quarter, QKV).astype(F32)
        up = expand[l].astype(F32)
        first, second = product[:, :QKV], product[:, QKV:]
        offset_sum, uplift_sum = bias_sum[:QKV], bias_sum[QKV:]
        grads.append(
            (
                jnp.stack([jnp.sum(flat * first, 1), jnp.sum(up * second, 1)]),
                jnp.stack([jnp.sum(flat * offset_sum, 1), jnp.sum(up * uplift_sum, 1)]),
                (scale[0][:, None] * first + shift[0][:, None] * offset_sum).reshape(
                    quarter, 3, INNER
                ),
                offset_sum.reshape(3, INNER),
                down_sum[:INNER],
                scale[1][:, None] * second + shift[1][:, None] * uplift_sum,
                uplift_sum,
                down_sum[INNER : INNER + HID],
                down_sum[INNER + HID],
            )
        )
    stacked = [jnp.stack([g[member] for g in grads]) for member in range(9)]
    scales_grad, shifts_grad = lax.psum((stacked[0], stacked[1]), ("yl", "zh", "zl"))
    return (outputs, inputs_grad, scales_grad, shifts_grad) + tuple(stacked[2:])


def solution(mesh):
    grid = Mesh(mesh.devices.reshape(4, 2, 2, 2, 2, 2), AXES)
    row, col = ("yh", "core"), ("yl", "zh", "zl")
    tokens = P(("x",) + col, row)
    weights = (
        P(None, None, row),
        P(None, None, row),
        P(None, row, None, col),
        P(None, None, col),
        P(None, col, row),
        P(None, row, col),
        P(None, col),
        P(None, col, row),
        P(None, row),
    )
    return jax.shard_map(
        shards,
        mesh=grid,
        in_specs=(tokens,) + weights + (tokens,),
        out_specs=(tokens, tokens) + weights,
        check_vma=False,
    )
```

```python
from functools import partial

import jax
import jax.numpy as jnp
import numpy as np
from jax import lax
from jax.experimental import pallas as pl
from jax.experimental.pallas import tpu as pltpu
from jax.sharding import Mesh
from jax.sharding import PartitionSpec as P

D = 1024
QUARTER = D // 4
HEAD = 64
ROT = 16
LAYERS = 2
LEN = 1024
OWN = LEN // 8
HEADS = 2
INNER = HEADS * HEAD
QKV = 3 * INNER
HID = 512
WIDE = QKV + HID
DOWN = INNER + HID
EXTRA = 16
TALL = QUARTER + EXTRA
SHARE = (WIDE + DOWN) // 4
NORM_EPSILON = 1e-05
BF = jnp.bfloat16
F32 = jnp.float32
NN = (((1,), (0,)), ((), ()))
NT = (((1,), (1,)), ((), ()))
TN = (((0,), (0,)), ((), ()))
AXES = ("x", "yh", "core", "yl", "zh", "zl")
LINE = ("zh", "zl")
RING = ("yh", "yl")
STEPS = (0, 1, 3, 2)
ANY = pl.BlockSpec(memory_space=pl.ANY)
HBM = pltpu.MemorySpace.HBM
VMEM = pl.BlockSpec(memory_space=pltpu.VMEM)


def dot(a, b, dims=NN):
    return lax.dot_general(a, b, dims, preferred_element_type=F32)


def sds(shape, dtype=BF):
    return jax.ShapeDtypeStruct(shape, dtype)


def hbm(shape, dtype=BF):
    return HBM(shape, dtype)


def call(
    kernel, out_shape, grid, in_specs, out_specs, micros, scratch=(), scalars=0, aliases={}, after=()
):
    count, extra = scalars + len(in_specs), len(after)

    def body(*refs):
        kernel(*refs[:count], *refs[count + extra :])

    run = pl.pallas_call(
        body,
        out_shape=out_shape,
        grid_spec=pltpu.PrefetchScalarGridSpec(
            num_scalar_prefetch=scalars,
            grid=grid,
            in_specs=list(in_specs) + [ANY] * extra,
            out_specs=out_specs,
            scratch_shapes=scratch,
        ),
        input_output_aliases=aliases,
        compiler_params=pltpu.CompilerParams(vmem_limit_bytes=12 * 2**20),
        cost_estimate=pl.CostEstimate(
            flops=int(micros * 1e6), bytes_accessed=1024, transcendentals=0
        ),
    )
    return lambda *operands: run(*operands, *after)


def far(*arrays):
    return [pltpu.with_memory_space_constraint(a, HBM) for a in arrays]


def block(rows, width):
    return pl.BlockSpec((rows, width), lambda i, *s: (i, 0))


def whole(*shape):
    return pl.BlockSpec(shape, lambda i, *s: (0,) * len(shape))


def rotary_tables():
    lane = jnp.arange(INNER) % (ROT // 2)
    inverse = 10000.0 ** (-(2 * lane).astype(F32) / ROT)
    angles = jnp.arange(LEN).astype(F32)[:, None] * inverse[None, :]
    return lax.optimization_barrier((jnp.cos(angles), jnp.sin(angles)))


def turn(u, cosine, sine, sign):
    half = ROT // 2
    lane = lax.broadcasted_iota(jnp.int32, u.shape, 1) % HEAD
    back = pltpu.roll(u, INNER - half, 1)
    ahead = pltpu.roll(u, half, 1)
    turned = jnp.where(lane < half, -back, ahead)
    return jnp.where(lane < ROT, u * cosine + sign * (turned * sine), u)


def normalized(x):
    mean = jnp.mean(x, 1, keepdims=True)
    r = lax.rsqrt(jnp.mean(x * x, 1, keepdims=True) - mean * mean + NORM_EPSILON)
    return (x - mean) * r, r


def token_copies(order, pieces, held, sems):
    return [
        pltpu.make_async_copy(p, held.at[pl.ds(order[j] * OWN, OWN)], sems.at[order[j]])
        for j, p in enumerate(pieces)
    ]


def feature_copies(order, pieces, held, sems, part=0):
    return [
        pltpu.make_async_copy(
            p.at[pl.ds(part * 512, 512)],
            held.at[
                pl.ds((order[j] // 4) * 512, 512), pl.ds(lax.rem(order[j], 4) * QUARTER, QUARTER)
            ],
            sems.at[order[j]],
        )
        for j, p in enumerate(pieces)
    ]


ROWS = 256


def project_kernel(first, last, order, *refs):
    pieces, refs = refs[:8], refs[8:]
    wide, norms, bias, cosine, sine, *refs = refs
    if last:
        down_grad, *refs = refs
    full, slope, query, keys, values, hidden, *rest = refs
    held, sems = refs[-2:]
    step = pl.program_id(0)

    @pl.when(step == 0)
    def _():
        copies = (feature_copies if first else token_copies)(order, pieces, held, sems)
        for c in copies:
            c.start()

    if first:

        @pl.when(lax.rem(step, 2) == 0)
        def _():
            for j in range(4):
                part = held.at[pl.ds(0, 512), pl.ds(0, QUARTER)]
                pltpu.make_async_copy(part, part, sems.at[step * 2 + j]).wait()

        @pl.when(step == order[8] // 2)
        def _():
            rest[0][...] = held[pl.ds(order[8] * OWN, OWN), :].astype(F32)
    else:
        for j in range(2):
            part = held.at[pl.ds(0, OWN)]
            pltpu.make_async_copy(pieces[0], part, sems.at[step * 2 + j]).wait()
    rows = held[pl.ds(step * ROWS, ROWS), :]
    xh = rows.astype(F32)
    if first:
        xh, _ = normalized(xh)
        rows = xh.astype(BF)
        xh = rows.astype(F32)
    full[...] = rows
    n_a = (xh * norms[0:1] + norms[2:3]).astype(BF)
    n_f = (xh * norms[1:2] + norms[3:4]).astype(BF)
    qkv = dot(n_a, wide[:, :QKV]) + bias[0:1, :QKV]
    table = (cosine[...], sine[...])
    query[...] = (turn(qkv[:, :INNER], *table, 1.0).astype(BF) * 0.125).astype(BF)
    keys[...] = turn(qkv[:, INNER : 2 * INNER], *table, 1.0).astype(BF)
    values[...] = qkv[:, 2 * INNER :].astype(BF)
    u = dot(n_f, wide[:, QKV:]) + bias[0:1, QKV:]
    cdf = 0.5 + 0.5 * lax.erf(u * (0.5**0.5))
    hidden[...] = (u * cdf).astype(BF)
    if first:
        for now, later in zip((query, keys, values, hidden), rest[1:5]):
            later[...] = now[...]
    steep = cdf + u * (jnp.exp(u * u * -0.5) * (1.0 / (2.0 * np.pi) ** 0.5))
    if last:
        du = (down_grad[...] * steep).astype(BF)
        slope[...] = du

        @pl.when(step == 0)
        def _():
            rest[0][...] = jnp.zeros_like(rest[0])

        rest[0][0:1] += jnp.sum(du.astype(F32), 0, keepdims=True)
    else:
        slope[...] = steep.astype(BF)


def project(first, order, pieces, wide, norms, bias, tables, down_grad=None):
    heads = [block(ROWS, INNER)] * 3 + [block(ROWS, HID)]
    shapes = [hbm((LEN, D)), hbm((LEN, HID)) if first else sds((LEN, HID))]
    shapes += [sds((LEN, INNER))] * 3 + [sds((LEN, HID))]
    outs = [block(ROWS, D), block(ROWS, HID)] + heads
    if first:
        shapes += [hbm((OWN, D), F32)] + [hbm((LEN, INNER))] * 3 + [hbm((LEN, HID))]
        outs += [whole(OWN, D)] + heads
    given = []
    if down_grad is not None:
        shapes.append(sds((8, HID), F32))
        outs.append(whole(8, HID))
        given = [down_grad]
    return call(
        partial(project_kernel, first, down_grad is not None),
        shapes,
        (LEN // ROWS,),
        [ANY] * 8
        + [whole(D, WIDE), whole(8, D), whole(8, WIDE)]
        + [block(ROWS, INNER)] * 2
        + [block(ROWS, HID)] * len(given),
        outs,
        7,
        scratch=[pltpu.VMEM((LEN, D), BF), pltpu.SemaphoreType.DMA((8,))],
        scalars=1,
    )(order, *pieces, wide, norms, bias, *tables, *given)


BLOCK = 256


def head_mask(h, rows):
    lane = lax.broadcasted_iota(jnp.int32, (rows, INNER), 1)
    return (lane // HEAD) == h


def causal():
    key = lax.broadcasted_iota(jnp.int32, (BLOCK, BLOCK), 0)
    query = lax.broadcasted_iota(jnp.int32, (BLOCK, BLOCK), 1)
    return key <= query


def attend_kernel(query, keys, values, mixed, logs, *kept):
    for i in range(LEN // BLOCK):
        n = (i + 1) * BLOCK
        here = pl.ds(i * BLOCK, BLOCK)
        q = query[here, :]
        out = jnp.zeros((BLOCK, INNER), F32)
        for h in range(HEADS):
            mask = head_mask(h, BLOCK)
            qh = jnp.where(mask, q, jnp.zeros_like(q))
            s = dot(keys[:n, :], qh, NT)
            tail = jnp.where(causal(), s[n - BLOCK :], -1e30)
            s = jnp.concatenate([s[: n - BLOCK], tail], 0) if i else tail
            top = jnp.max(s, 0, keepdims=True)
            p = jnp.exp(s - top)
            total = jnp.sum(p, 0, keepdims=True)
            logs[h : h + 1, here] = top + jnp.log(total)
            part = dot(values[:n, :], p.astype(BF), TN)
            part = jnp.transpose(part * (1.0 / total))
            out = jnp.where(mask, part, out)
        mixed[here, :] = out.astype(BF)
        for ref in kept:
            ref[here, :] = out.astype(BF)


def attend(query, keys, values, keep):
    return call(
        attend_kernel,
        [sds((LEN, INNER)), sds((8, LEN), F32)] + [hbm((LEN, INNER))] * keep,
        (),
        [VMEM] * 3,
        [VMEM] * (2 + keep),
        5,
    )(query, keys, values)


def attend_back_kernel(
    query, keys, values, dmixed, logs, cosine, sine, dqkv, sums, dkeys, dvalues
):
    dkeys[...] = jnp.zeros_like(dkeys)
    dvalues[...] = jnp.zeros_like(dvalues)
    count = jnp.zeros((1, INNER), F32)
    for i in range(LEN // BLOCK):
        n = (i + 1) * BLOCK
        here = pl.ds(i * BLOCK, BLOCK)
        q, do = query[here, :], dmixed[here, :]
        dq = jnp.zeros((BLOCK, INNER), F32)
        for h in range(HEADS):
            mask = head_mask(h, BLOCK)
            qh = jnp.where(mask, q, jnp.zeros_like(q))
            doh = jnp.where(mask, do, jnp.zeros_like(do))
            s = dot(keys[:n, :], qh, NT)
            p = jnp.exp(s - logs[h : h + 1, here])
            tail = jnp.where(causal(), p[n - BLOCK :], 0.0)
            p = jnp.concatenate([p[: n - BLOCK], tail], 0) if i else tail
            dp = dot(values[:n, :], doh, NT)
            w = p * dp
            delta = jnp.sum(w, 0, keepdims=True)
            ds = (w - p * delta).astype(BF)
            dvalues[:n, :] += dot(p.astype(BF), doh)
            dkeys[:n, :] += dot(ds, qh)
            dq = jnp.where(mask, jnp.transpose(dot(keys[:n, :], ds, TN)), dq)
        dq = turn(dq * 0.125, cosine[here, :], sine[here, :], -1.0).astype(BF)
        dqkv[here, :INNER] = dq
        count += jnp.sum(dq.astype(F32), 0, keepdims=True)
    sums[0:1, :INNER] = count
    dk = turn(dkeys[...], cosine[...], sine[...], -1.0).astype(BF)
    dv = dvalues[...].astype(BF)
    dqkv[:, INNER : 2 * INNER] = dk
    dqkv[:, 2 * INNER :] = dv
    sums[0:1, INNER : 2 * INNER] = jnp.sum(dk.astype(F32), 0, keepdims=True)
    sums[0:1, 2 * INNER :] = jnp.sum(dv.astype(F32), 0, keepdims=True)


def attend_back(query, keys, values, dmixed, logs, tables, after=()):
    return call(
        attend_back_kernel,
        [sds((LEN, QKV)), sds((8, QKV), F32)],
        (),
        [VMEM] * 7,
        [VMEM] * 2,
        6,
        scratch=[pltpu.VMEM((LEN, INNER), F32)] * 2,
        after=after,
    )(query, keys, values, dmixed, logs, *tables)


def merge_kernel(side, mixed, hidden, down, out):
    first = dot(mixed[...], down[:, :INNER], NT)
    out[...] = (first + dot(hidden[...], down[:, INNER:], NT)).astype(BF)


def half_block(width):
    return pl.BlockSpec((ROWS, width), lambda i, s: (s[0] * 2 + i, 0))


def merge(side, mixed, hidden, down, after=()):
    return call(
        merge_kernel,
        sds((LEN // 2, D)),
        (2,),
        [half_block(INNER), half_block(HID), whole(D, DOWN)],
        block(ROWS, D),
        2,
        scalars=1,
        after=after,
    )(side, mixed, hidden, down)


def spread_kernel(side, dqkv, dupper, wide, norms, out):
    first = dot(dqkv[...], wide[:, :QKV], NT) * norms[0:1]
    out[...] = (first + dot(dupper[...], wide[:, QKV:], NT) * norms[1:2]).astype(BF)


def spread(side, dqkv, dupper, wide, norms):
    return call(
        spread_kernel,
        sds((LEN // 2, D)),
        (2,),
        [half_block(QKV), half_block(HID), whole(D, WIDE), whole(8, D)],
        block(ROWS, D),
        2.2,
        scalars=1,
    )(side, dqkv, dupper, wide, norms)


def joint_kernel(side, dqkv, dupper, wide, norms, mixed, hidden, down, out):
    step = pl.program_id(0)

    @pl.when(step < 2)
    def _():
        spread_kernel(side, dqkv, dupper, wide, norms, out)

    @pl.when(step >= 2)
    def _():
        merge_kernel(side, mixed, hidden, down, out)


def joint(side, dqkv, dupper, wide, norms, mixed, hidden, down, after=()):
    early = lambda w: pl.BlockSpec((ROWS, w), lambda i, s: (s[0] * 2 + jnp.minimum(i, 1), 0))
    late = lambda w: pl.BlockSpec((ROWS, w), lambda i, s: (s[0] * 2 + jnp.maximum(i - 2, 0), 0))
    return call(
        joint_kernel,
        sds((LEN, D)),
        (4,),
        [early(QKV), early(HID), whole(D, WIDE), whole(8, D), late(INNER), late(HID), whole(D, DOWN)],
        block(ROWS, D),
        4,
        scalars=1,
        after=after,
    )(side, dqkv, dupper, wide, norms, mixed, hidden, down)


def branch_first_kernel(dy, down, dmixed, dhidden, total):
    @pl.when(pl.program_id(0) == 0)
    def _():
        total[...] = jnp.zeros_like(total)

    g = dy[...]
    total[0:1] += jnp.sum(g.astype(F32), 0, keepdims=True)
    both = dot(g, down[...])
    dmixed[...] = both[:, :INNER].astype(BF)
    dhidden[...] = both[:, INNER:]


def branch_first(dy, down):
    return call(
        branch_first_kernel,
        [sds((LEN, INNER)), sds((LEN, HID), F32), sds((8, D), F32)],
        (LEN // ROWS,),
        [block(ROWS, D), whole(D, DOWN)],
        [block(ROWS, INNER), block(ROWS, HID), whole(8, D)],
        4,
    )(dy, down)


def branch_kernel(order, *refs):
    pieces, refs = refs[:8], refs[8:]
    down, slope, dmixed, dupper, sums, total, full, held, sems = refs
    step = pl.program_id(0)

    @pl.when(step == 0)
    def _():
        sums[...] = jnp.zeros_like(sums)
        total[...] = jnp.zeros_like(total)
        for c in token_copies(order, pieces, held, sems):
            c.start()

    for j in range(2):
        part = held.at[pl.ds(0, OWN)]
        pltpu.make_async_copy(pieces[0], part, sems.at[step * 2 + j]).wait()
    g = held[pl.ds(step * ROWS, ROWS), :]
    full[...] = g
    total[0:1] += jnp.sum(g.astype(F32), 0, keepdims=True)
    both = dot(g, down[...])
    dmixed[...] = both[:, :INNER].astype(BF)
    du = (both[:, INNER:] * slope[...].astype(F32)).astype(BF)
    dupper[...] = du
    sums[0:1] += jnp.sum(du.astype(F32), 0, keepdims=True)


def branch(order, pieces, down, slope, after=()):
    return call(
        branch_kernel,
        [
            sds((LEN, INNER)),
            sds((LEN, HID)),
            sds((8, HID), F32),
            sds((8, D), F32),
            sds((LEN, D)),
        ],
        (LEN // ROWS,),
        [ANY] * 8 + [whole(D, DOWN), block(ROWS, HID)],
        [block(ROWS, INNER), block(ROWS, HID), whole(8, HID), whole(8, D), block(ROWS, D)],
        4,
        scratch=[pltpu.VMEM((LEN, D), BF), pltpu.SemaphoreType.DMA((8,))],
        scalars=1,
        after=after,
    )(order, *pieces, down, slope)


def settle_kernel(order, *refs):
    count = len(refs) - 2
    copies = feature_copies(order, refs[:count], refs[count], refs[count + 1], 1)
    for c in copies:
        c.start()
    for c in copies:
        c.wait()


def settle(order, pieces, after=()):
    return call(
        settle_kernel,
        hbm((LEN, D)),
        (),
        [ANY] * len(pieces),
        VMEM,
        2,
        scratch=[pltpu.SemaphoreType.DMA((8,))],
        scalars=1,
        after=after,
    )(order, *pieces)


def pack_kernel(has_wide, has_down, layer, *refs):
    refs, out = list(refs[:-1]), refs[-1]
    start = 0
    out[QUARTER:, :] = jnp.zeros_like(out[QUARTER:, :])
    if has_wide:
        triples, expand, scales, shifts, offsets, uplift, closing = refs[:7]
        refs = refs[7:]
        for i in range(3):
            at = slice(i * INNER, (i + 1) * INNER)
            out[:QUARTER, at] = triples[0, :, i, :]
            out[QUARTER : QUARTER + 1, at] = offsets[layer, i : i + 1, :]
        out[:QUARTER, QKV:WIDE] = expand[0]
        out[QUARTER : QUARTER + 1, QKV:WIDE] = uplift[layer : layer + 1, :]
        for i in range(2):
            at = slice(i * QUARTER, (i + 1) * QUARTER)
            out[QUARTER + 1 : QUARTER + 2, at] = scales[layer, i : i + 1, :]
            out[QUARTER + 2 : QUARTER + 3, at] = shifts[layer, i : i + 1, :]
        out[QUARTER + 3 : QUARTER + 4, :QUARTER] = closing[layer : layer + 1, :]
        start = WIDE
    if has_down:
        merger, shrink = refs
        out[:QUARTER, start : start + INNER] = merger[0].T
        out[:QUARTER, start + INNER :] = shrink[0].T


def of_layer(layer, array):
    shape = array.shape[1:]
    return pl.BlockSpec((1,) + shape, lambda i, *s: (layer,) + (0,) * len(shape))


def pack(layer, wide, down, after=()):
    specs = []
    if wide:
        specs += [of_layer(layer, a) for a in wide[:2]] + [whole(*a.shape) for a in wide[2:]]
    specs += [of_layer(layer, a) for a in down]
    width = (WIDE if wide else 0) + (DOWN if down else 0)
    return call(
        partial(pack_kernel, bool(wide), bool(down), layer),
        hbm((QUARTER + EXTRA, width)),
        (1,),
        specs,
        whole(QUARTER + EXTRA, width),
        1,
        after=after,
    )(*wide, *down)


def pick_kernel(order, both, out, sems):
    copies = [
        pltpu.make_async_copy(both.at[2 * i + 1 - order[0]], out.at[i], sems.at[i])
        for i in range(2)
    ]
    for c in copies:
        c.start()
    for c in copies:
        c.wait()


def pick(order, both, after=()):
    return call(
        pick_kernel,
        sds((2,) + both.shape[1:]),
        (),
        [ANY],
        VMEM,
        1,
        scratch=[pltpu.SemaphoreType.DMA((2,))],
        scalars=1,
        after=after,
    )(order, both)


def halves(core, both, got, sems, places):
    copies = []
    for i in range(2):
        for j, (source, at) in enumerate(
            ((both.at[2 * i + core], 2 * i + core), (got.at[i], 2 * i + 1 - core))
        ):
            for n, (a, b) in enumerate(places(source, at)):
                copies.append(pltpu.make_async_copy(a, b, sems.at[2 * i + j, n]))
    for c in copies:
        c.start()
    for c in copies:
        c.wait()


def wide_places(wide, extra):
    def places(source, at):
        rows = pl.ds(at * QUARTER, QUARTER)
        return (
            (source.at[pl.ds(0, QUARTER), pl.ds(0, WIDE)], wide.at[rows]),
            (source.at[pl.ds(QUARTER, EXTRA), pl.ds(0, WIDE)], extra.at[at]),
        )

    return places


def down_places(down, start):
    def places(source, at):
        rows = pl.ds(at * QUARTER, QUARTER)
        return ((source.at[pl.ds(0, QUARTER), pl.ds(start, DOWN)], down.at[rows]),)

    return places


def vectors(extra, norms, bias):
    bias[...] = jnp.zeros_like(bias)
    norms[...] = jnp.zeros_like(norms)
    bias[0:1] = extra[0, 0:1].astype(F32)
    for q in range(4):
        cols = slice(q * QUARTER, (q + 1) * QUARTER)
        for n in range(5):
            row, at = 1 + n // 2, (n % 2) * QUARTER
            norms[n : n + 1, cols] = extra[q, row : row + 1, at : at + QUARTER].astype(F32)


def weights_kernel(has_wide, has_down, order, both, got, *refs):
    outs, (extra, sems) = list(refs[:-2]), refs[-2:]
    kept = []
    if has_wide:
        wide, wide_kept, norms, bias = outs[:4]
        outs = outs[4:]
        kept.append((wide, wide_kept))
    if has_down:
        down, down_kept = outs
        kept.append((down, down_kept))

    def places(source, at):
        found = ()
        if has_wide:
            found += wide_places(wide, extra)(source, at)
        if has_down:
            found += down_places(down, WIDE if has_wide else 0)(source, at)
        return found

    halves(order[0], both, got, sems, places)
    copies = [pltpu.make_async_copy(a, b, sems.at[i, 0]) for i, (a, b) in enumerate(kept)]
    for c in copies:
        c.start()
    if has_wide:
        vectors(extra, norms, bias)
    for c in copies:
        c.wait()


def settle_weights(order, both, got, has_wide, has_down):
    shapes, specs = [], []
    if has_wide:
        shapes += [sds((D, WIDE)), hbm((D, WIDE)), sds((8, D), F32), sds((8, WIDE), F32)]
        specs += [VMEM, ANY, VMEM, VMEM]
    if has_down:
        shapes += [sds((D, DOWN)), hbm((D, DOWN))]
        specs += [VMEM, ANY]
    return call(
        partial(weights_kernel, has_wide, has_down),
        shapes,
        (),
        [ANY] * 2,
        specs,
        2,
        scratch=[pltpu.VMEM((4, EXTRA, WIDE), BF), pltpu.SemaphoreType.DMA((4, 3))],
        scalars=1,
    )(order, both, got)


def combine_kernel(order, mine, got, own, *sent):
    for k, ref in zip(STEPS, (own,) + sent):
        for part in range(mine.shape[0] // 512):
            start = part * 512 + lax.rem(order[0] + k, 4) * OWN
            at = pl.ds(pl.multiple_of(start, OWN), OWN)
            total = mine[at, :].astype(F32) + got[at, :].astype(F32)
            ref[part * OWN : (part + 1) * OWN, :] = total.astype(ref.dtype)


def combine(order, mine, got):
    rows = mine.shape[0] // 4
    return call(
        combine_kernel,
        [sds((rows, D), F32)] + [hbm((rows, D))] * 3,
        (),
        [VMEM] * 2,
        [VMEM] * 4,
        1.5,
        scalars=1,
    )(order, mine, got)


def summed(own, others, rows):
    total = own[rows, :]
    for ref in others:
        total = total + ref[rows, :].astype(F32)
    return total


def back_through_norm(dxhat, x):
    xhat, r = normalized(x)
    mean = jnp.mean(dxhat, 1, keepdims=True)
    return r * (dxhat - mean - xhat * jnp.mean(dxhat * xhat, 1, keepdims=True))


EVERY = slice(0, OWN)


def finish_kernel(own, a, b, c, x, norms, new, xhat):
    value = x[...] + (summed(own, (a, b, c), EVERY) + norms[4:5])
    new[...] = value
    xhat[...] = normalized(value)[0].astype(BF)


def finish(parts, x, norms):
    return call(
        finish_kernel,
        [hbm((OWN, D), F32), hbm((OWN, D))],
        (),
        [VMEM] * 6,
        [VMEM] * 2,
        1.5,
    )(*parts, x, norms)


def finish_back_kernel(order, own, a, b, c, x, gradient, new, lowered, mark):
    mark[...] = jnp.zeros_like(mark)
    value = gradient[...].astype(F32) + back_through_norm(summed(own, (a, b, c), EVERY), x[...])
    new[...] = value
    lowered[...] = value.astype(BF)


def finish_back(order, parts, x, gradient):
    return call(
        finish_back_kernel,
        [hbm((OWN, D), F32), hbm((OWN, D)), sds((8, 128), F32)],
        (1,),
        [whole(OWN, D)] * 5 + [pl.BlockSpec((OWN, D), lambda i, s: (s[0], 0))],
        [whole(OWN, D)] * 2 + [whole(8, 128)],
        1.5,
        scalars=1,
    )(order, *parts, x, gradient)


def finish_last_kernel(order, own, a, b, c, x_back, gradient, x_front, norms, *refs):
    outs, mark, held = refs[:4], refs[4], refs[5]
    mark[...] = jnp.zeros_like(mark)
    others = (a, b, c)
    held[EVERY, :] = gradient[...] + back_through_norm(summed(own, others, EVERY), x_back[...])
    held[OWN:, :] = x_front[...] + (summed(own, others, slice(OWN, 2 * OWN)) + norms[4:5])
    for k, ref in enumerate(outs):
        q = lax.rem(order[0] + k, 4)
        ref[...] = held[:, pl.ds(pl.multiple_of(q * QUARTER, QUARTER), QUARTER)].astype(BF)


def finish_last(order, parts, x_back, gradient, x_front, norms):
    return call(
        finish_last_kernel,
        [hbm((2 * OWN, QUARTER))] * 4 + [sds((8, 128), F32)],
        (),
        [VMEM] * 8,
        [VMEM] * 5,
        2,
        scratch=[pltpu.VMEM((2 * OWN, D), F32)],
        scalars=1,
    )(order, *parts, x_back, gradient, x_front, norms)


def land_kernel(order, *refs):
    pieces, (back, front, mark) = refs[:4], refs[4:]
    mark[...] = jnp.zeros_like(mark)
    for k, p in enumerate(pieces):
        at = pl.ds(pl.multiple_of(lax.rem(order[0] - k + 4, 4) * OWN, OWN), OWN)
        back[at, :] = p[:OWN, :].astype(F32)
        front[at, :] = p[OWN:, :]


def land(order, pieces):
    shape = (4 * OWN, QUARTER)
    return call(
        land_kernel,
        [sds(shape, F32), sds(shape), sds((8, 128), F32)],
        (),
        [VMEM] * 4,
        [VMEM] * 3,
        1,
        scalars=1,
    )(order, *pieces)


def payload_kernel(pairs, marks, *refs):
    out, mark = refs[-2:]
    mark[...] = jnp.zeros_like(mark)
    at, width = 0, 0
    out[QUARTER:, :] = jnp.zeros_like(out[QUARTER:, :])
    for rights in pairs:
        lhs = refs[at][...]
        at += 1
        for w in rights:
            out[:QUARTER, width : width + w] = dot(lhs, refs[at][...], TN).astype(BF)
            at += 1
            width += w
    for row, start, w in marks:
        out[QUARTER + row : QUARTER + row + 1, start : start + w] = refs[at][0:1, :].astype(BF)
        at += 1


def payload(pairs, extras, after=()):
    operands, specs, shape, width = [], [], [], 0
    for left, rights in pairs:
        operands.append(left)
        specs.append(pl.BlockSpec((LEN, QUARTER), lambda i: (0, i)))
        for r in rights:
            operands.append(r)
            specs.append(whole(*r.shape))
            width += r.shape[1]
        shape.append(tuple(r.shape[1] for r in rights))
    marks = []
    for row, start, vector, sliced in extras:
        operands.append(vector)
        w = QUARTER if sliced else vector.shape[1]
        specs.append(pl.BlockSpec((8, w), lambda i: (0, i)) if sliced else whole(8, w))
        marks.append((row, start, w))
    return call(
        partial(payload_kernel, tuple(shape), tuple(marks)),
        [hbm((4 * TALL, width)), sds((8, 128), F32)],
        (4,),
        specs,
        [block(TALL, width), whole(8, 128)],
        4 * (0.3 + width / 1536),
        after=after,
    )(*operands)


def share_kernel(order, part, mine, *sent):
    for k, ref in zip(STEPS, (mine,) + sent):
        at = pl.multiple_of(lax.rem(order[0] + k, 4) * SHARE, SHARE)
        ref[...] = part[:, pl.ds(at, SHARE)]


def share(order, part, after=()):
    return call(
        share_kernel,
        [sds((TALL, SHARE))] + [hbm((TALL, SHARE))] * 3,
        (),
        [VMEM],
        [VMEM] * 4,
        1.5,
        scalars=1,
        after=after,
    )(order, part)


def last_sum_kernel(own, a, b, c, out, mark):
    mark[...] = jnp.zeros_like(mark)
    total = own[...].astype(F32) + a[...].astype(F32) + b[...].astype(F32) + c[...].astype(F32)
    out[...] = total.astype(BF)


def last_sum(parts):
    return call(
        last_sum_kernel,
        [hbm((TALL, SHARE)), sds((8, 128), F32)],
        (),
        [VMEM] * 4,
        [VMEM] * 2,
        1,
    )(*parts)


WIDTHS = {"triples": QKV, "expand": HID, "down": DOWN}
ROW = {"triples": 2, "expand": 0, "down": 1}


def final_kernel(layer, kinds, order, *refs):
    pieces, cols, refs = refs[:4], refs[4], refs[5:]
    shards_in = {}
    for kind in kinds:
        if kind != "down":
            shards_in[kind], refs = refs[0], refs[1:]
    if layer == 0:
        upper, refs = refs[0], refs[1 + sum(2 if k == "down" else 1 for k in kinds) :]
    held = refs[-1]
    for k, ref in zip(STEPS, pieces):
        at = pl.ds(pl.multiple_of(lax.rem(order[0] - k + 4, 4) * SHARE, SHARE), SHARE)
        held[:, at] = ref[...].astype(F32)
    start, lane = 0, lax.broadcasted_iota(jnp.int32, (QUARTER, 128), 1)
    stats = jnp.zeros((QUARTER, 128), F32)
    vectors, refs = refs[0], refs[1:]
    vectors[...] = jnp.zeros_like(vectors)
    for kind in kinds:
        w, row = WIDTHS[kind], ROW[kind]
        product = held[:QUARTER, start : start + w]
        if kind == "down":
            turned = jnp.transpose(product)
            refs[0][0] = turned[:INNER]
            refs[1][0] = turned[INNER:]
            refs = refs[2:]
            vectors[row : row + 1, :QUARTER] = held[QUARTER + row : QUARTER + row + 1, :QUARTER]
        else:
            sums = held[QUARTER + row : QUARTER + row + 1, start : start + w]
            vectors[row : row + 1, :w] = sums
            own = shards_in[kind]
            if kind == "triples":
                own = jnp.concatenate([own[0, :, i, :] for i in range(3)], 1)
            else:
                own = own[0]
            own = own.astype(F32)
            at = 0 if kind == "triples" else 1
            stats = jnp.where(lane == at, jnp.sum(own * product, 1, keepdims=True), stats)
            stats = jnp.where(lane == 2 + at, jnp.sum(own * sums, 1, keepdims=True), stats)
            value = cols[:, at : at + 1] * product + cols[:, 2 + at : 3 + at] * sums
            if kind == "triples":
                for i in range(3):
                    refs[0][0, :, i, :] = value[:, i * INNER : (i + 1) * INNER]
            else:
                refs[0][0] = value
            refs = refs[1:]
        start += w
    vectors[4:8, :QUARTER] = jnp.transpose(stats)[:4]
    if layer == 0:
        offsets, uplift, closing, joint_stats = refs[:4]
        for l, source in enumerate((vectors, upper)):
            offsets[l : l + 1] = source[2:3, :QKV]
            uplift[l : l + 1] = source[0:1]
            closing[l : l + 1] = source[1:2, :QUARTER]
            for n in range(2):
                at = 4 * n + 2 * l
                joint_stats[at : at + 2] = source[4 + 2 * n : 6 + 2 * n, :QUARTER]


GRADS = {
    "triples": [(LAYERS, QUARTER, 3, INNER)],
    "expand": [(LAYERS, QUARTER, HID)],
    "down": [(LAYERS, INNER, QUARTER), (LAYERS, HID, QUARTER)],
}


def final(layer, kinds, order, pieces, cols, weights, stacks, upper=None):
    width = WIDE + DOWN
    operands = list(pieces) + [cols] + [weights[k] for k in kinds if k != "down"]
    if layer == 0:
        operands.append(upper)
    specs = [VMEM] * len(operands)
    shapes, outs, aliases = [sds((8, HID), F32)], [VMEM], {}
    for kind in kinds:
        for place, shape in enumerate(GRADS[kind]):
            if layer == 0:
                aliases[1 + len(operands)] = len(shapes)
                operands.append(stacks[kind][place])
                specs.append(ANY)
            shapes.append(sds(shape, F32))
            outs.append(
                pl.BlockSpec(
                    (1,) + shape[1:], lambda i, s, n=len(shape) - 1: (layer,) + (0,) * n
                )
            )
    outs[0] = whole(8, HID)
    if layer == 0:
        for shape in ((LAYERS, QKV), (LAYERS, HID), (LAYERS, QUARTER), (8, QUARTER)):
            shapes.append(sds(shape, F32))
            outs.append(whole(*shape))
    fixed = [whole(*o.shape) if s is VMEM else s for o, s in zip(operands, specs)]
    for n, kind in enumerate(k for k in kinds if k != "down"):
        fixed[5 + n] = of_layer(layer, weights[kind])
    results = call(
        partial(final_kernel, layer, kinds),
        shapes,
        (1,),
        fixed,
        outs,
        2,
        scratch=[pltpu.VMEM((TALL, width), F32)],
        scalars=1,
        aliases=aliases,
    )(order, *operands)
    vectors, results = results[0], list(results[1:])
    grads = {}
    for kind in kinds:
        n = len(GRADS[kind])
        grads[kind], results = results[:n], results[n:]
    return (results if layer == 0 else vectors), grads


def across(array):
    return lax.ppermute(array, "core", [(0, 1), (1, 0)])


def around(array, axes, step):
    return lax.ppermute(array, axes, [(i, (i + step) % 4) for i in range(4)])


def exchanged(array, axes):
    return lax.ppermute(array, axes, [(0, 0), (1, 2), (2, 1), (3, 3)])


def gather_ring(own, axes):
    return [own] + [around(own, axes, k) for k in STEPS[1:]]


def gather_line(own):
    pieces = gather_ring(own, LINE)
    return pieces + [across(p) for p in pieces]


def scatter_line(order, other, mine):
    own, *sent = combine(order, mine, across(other))
    return [own] + [around(s, LINE, k) for s, k in zip(sent, STEPS[1:])]


def outward_pairs(step):
    pairs = []
    for q in range(4):
        for zh in range(2):
            for core in range(2):
                z = (q - step) % 4
                pairs.append(((zh * 2 + core) * 4 + z, q * 4 + zh * 2 + core))
    return pairs


def outward(pieces):
    axes = ("yh", "core", "zh", "zl")
    return [lax.ppermute(p, axes, outward_pairs(k)) for k, p in enumerate(pieces)]


def tiny(array):
    return array[:16, :128]


def fetch(core, both, after, has_wide, has_down):
    (both,) = far(both)
    return settle_weights(core, both, across(pick(core, both, after)), has_wide, has_down)


def reduce_ring(array):
    return lax.psum_scatter(array, RING, scatter_dimension=0, tiled=True)


def crossed(step):
    return [
        ((x * 2 + core) * 2 + yl, ((x + step) % 4 * 2 + yl) * 2 + core)
        for x in range(4)
        for core in range(2)
        for yl in range(2)
    ]


def reduce_x(x, part, after=()):
    mine, *sent = share(x.reshape(1), far(part)[0], after)
    total, mark = last_sum([mine] + far(*[around(s, "x", k) for s, k in zip(sent, STEPS[1:])]))
    return far(*[lax.ppermute(total, ("x", "core", "yl"), crossed(k)) for k in STEPS]), mark


def shards(
    inputs, scales, shifts, triples, offsets, merger, expand, uplift, shrink, closing, cotangent
):
    core, y, z = lax.axis_index("core"), lax.axis_index(RING), lax.axis_index(LINE)
    x_at, q_at = lax.axis_index("x"), lax.axis_index(("yh", "core"))
    here, there = core.reshape(1), (1 - core).reshape(1)
    chunk = core * 4 + z
    sources = [(z - k + 4) % 4 for k in STEPS]
    tokens = jnp.stack([core * 4 + s for s in sources] + [(1 - core) * 4 + s for s in sources])
    blocks = [(s % 2) * 4 + (s // 2) * 2 for s in sources]
    features = jnp.stack([b + core for b in blocks] + [b + 1 - core for b in blocks] + [chunk])
    z_one, x_one, q_one = z.reshape(1), x_at.reshape(1), q_at.reshape(1)

    moved = exchanged(jnp.concatenate([inputs, cotangent], 0), ("yh", "zh"))
    marker = [tiny(moved)]
    wide_args = (triples, expand, scales, shifts, offsets, uplift, closing)
    down_args = (merger, shrink)
    sent = lax.all_gather(pack(0, wide_args, down_args, marker), RING, axis=0, tiled=False)
    pieces = gather_line(moved)
    sent1 = lax.all_gather(pack(1, wide_args, down_args, marker), RING, axis=0, tiled=False)
    tables = rotary_tables()
    wide, wide_kept, norms, bias, down, down_kept = fetch(
        here, sent, [tiny(p) for p in pieces[1:4]], True, True
    )

    full0, slope0, query0, keys0, values0, hidden0, x0, *kept = project(
        True, features, far(*pieces), wide, norms, bias, tables
    )
    mixed0, logs0, mixed_kept = attend(query0, keys0, values0, 1)
    other = merge(there, mixed0, hidden0, down)
    mine = merge(here, mixed0, hidden0, down)
    query0, keys0, values0, hidden0, mixed0 = far(*kept, mixed_kept)
    parts = scatter_line(z_one, other, mine)
    marker = [tiny(p) for p in parts[1:]]
    top = settle(features, far(*pieces), marker)
    wide1, _, norms1, bias1, down1, down1_kept = fetch(here, sent1, marker, True, True)
    dmixed1, dhidden1, close_sum1 = branch_first(top, down1)
    x1, xhat = finish(parts[:1] + far(*parts[1:]), x0, norms)
    pieces = gather_line(xhat)

    full1, dupper1, query1, keys1, values1, hidden1, up_sum1 = project(
        False, tokens, pieces, wide1, norms1, bias1, tables, dhidden1
    )
    mixed1, logs1 = attend(query1, keys1, values1, 0)
    dqkv1, qkv_sum1 = attend_back(query1, keys1, values1, dmixed1, logs1, tables)
    other = spread(there, dqkv1, dupper1, wide1, norms1)
    mine = spread(here, dqkv1, dupper1, wide1, norms1)
    parts = scatter_line(z_one, other, mine)
    gradient, lowered, mark = finish_back(
        chunk.reshape(1), parts[:1] + far(*parts[1:]), *far(x1, top))
    grad1, done1 = payload(
        [(far(full1)[0], [dqkv1, dupper1]), (far(top)[0], [mixed1, hidden1])],
        [(2, 0, qkv_sum1, False), (0, QKV, up_sum1, False), (1, 0, close_sum1, True)],
        [mark],
    )
    grad1 = reduce_ring(grad1)
    pieces = gather_line(lowered)

    dmixed0, dupper0, up_sum0, close_sum0, dy0 = branch(
        tokens, pieces, *far(down_kept, slope0), [done1]
    )
    dqkv0, qkv_sum0 = attend_back(query0, keys0, values0, dmixed0, logs0, far(*tables))
    grad0, done0 = payload(
        [(far(full0)[0], [dupper0]), (dy0, [mixed0, hidden0]), (far(full0)[0], [dqkv0])],
        [(0, 0, up_sum0, False), (1, 0, close_sum0, True), (2, HID + DOWN, qkv_sum0, False)],
    )
    grad0 = reduce_ring(grad0)

    rest = (dqkv0, dupper0, far(wide_kept)[0], norms, mixed1, hidden1, far(down1_kept)[0])
    other = joint(there, *rest, [done0])
    mine = joint(here, *rest, [done0])
    parts = scatter_line(z_one, other, mine)
    *pieces, finished = finish_last(
        z_one, parts[:1] + far(*parts[1:]), *far(x0, gradient, x1), norms1)
    inputs_grad, outputs, landed = land(q_one, far(*outward(pieces)))
    cols = [
        jnp.concatenate([scales[l], shifts[l]], 0).astype(F32).T for l in range(LAYERS)
    ]
    weights = {"triples": triples, "expand": expand}
    reduced, summed1 = reduce_x(x_at, grad1, [tiny(dqkv0)])
    upper, stacks = final(
        1, ("triples", "expand", "down"), x_one, reduced, cols[1], weights, None
    )
    reduced, _ = reduce_x(x_at, grad0, [finished, summed1])
    (offsets_grad, uplift_grad, closing_grad, stats), stacks = final(
        0, ("expand", "down", "triples"), x_one, reduced, cols[0], weights, stacks, upper
    )
    stats = stats + lax.ppermute(stats, "yl", [(0, 1), (1, 0)])
    stats = sum(gather_ring(stats, LINE)).reshape(2, LAYERS, 2, QUARTER)
    offsets_grad = offsets_grad.reshape(LAYERS, 3, INNER)
    return (
        outputs,
        inputs_grad,
        stats[0],
        stats[1],
        stacks["triples"][0],
        offsets_grad,
        stacks["down"][0],
        stacks["expand"][0],
        uplift_grad,
        stacks["down"][1],
        closing_grad,
    )


def solution(mesh):
    grid = Mesh(mesh.devices.reshape(4, 2, 2, 2, 2, 2), AXES)
    row, col = ("yh", "core"), ("yl", "zh", "zl")
    tokens = P(("x",) + col, row)
    weights = (
        P(None, None, row),
        P(None, None, row),
        P(None, row, None, col),
        P(None, None, col),
        P(None, col, row),
        P(None, row, col),
        P(None, col),
        P(None, col, row),
        P(None, row),
    )
    return jax.shard_map(
        shards,
        mesh=grid,
        in_specs=(tokens,) + weights + (tokens,),
        out_specs=(tokens, tokens) + weights,
        check_vma=False,
    )
```

```python
from functools import partial

import jax
import jax.numpy as jnp
import numpy as np
from jax import lax
from jax.experimental import pallas as pl
from jax.experimental.pallas import tpu as pltpu
from jax.sharding import Mesh
from jax.sharding import PartitionSpec as P

D = 1024
QUARTER = D // 4
HEAD = 64
ROT = 16
LAYERS = 2
LEN = 1024
OWN = LEN // 8
HEADS = 2
INNER = HEADS * HEAD
QKV = 3 * INNER
HID = 512
WIDE = QKV + HID
DOWN = INNER + HID
EXTRA = 16
TALL = QUARTER + EXTRA
SHARE = (WIDE + DOWN) // 4
NORM_EPSILON = 1e-05
BF = jnp.bfloat16
F32 = jnp.float32
NN = (((1,), (0,)), ((), ()))
NT = (((1,), (1,)), ((), ()))
TN = (((0,), (0,)), ((), ()))
AXES = ("x", "yh", "core", "yl", "zh", "zl")
LINE = ("zh", "zl")
RING = ("yh", "yl")
STEPS = (0, 1, 3, 2)
ANY = pl.BlockSpec(memory_space=pl.ANY)
HBM = pltpu.MemorySpace.HBM
VMEM = pl.BlockSpec(memory_space=pltpu.VMEM)


def dot(a, b, dims=NN):
    return lax.dot_general(a, b, dims, preferred_element_type=F32)


def sds(shape, dtype=BF):
    return jax.ShapeDtypeStruct(shape, dtype)


def hbm(shape, dtype=BF):
    return HBM(shape, dtype)


def call(
    kernel, out_shape, grid, in_specs, out_specs, micros, scratch=(), scalars=0, aliases={}, after=()
):
    count, extra = scalars + len(in_specs), len(after)

    def body(*refs):
        kernel(*refs[:count], *refs[count + extra :])

    run = pl.pallas_call(
        body,
        out_shape=out_shape,
        grid_spec=pltpu.PrefetchScalarGridSpec(
            num_scalar_prefetch=scalars,
            grid=grid,
            in_specs=list(in_specs) + [ANY] * extra,
            out_specs=out_specs,
            scratch_shapes=scratch,
        ),
        input_output_aliases=aliases,
        compiler_params=pltpu.CompilerParams(vmem_limit_bytes=12 * 2**20),
        cost_estimate=pl.CostEstimate(
            flops=int(micros * 1e6), bytes_accessed=1024, transcendentals=0
        ),
    )
    return lambda *operands: run(*operands, *after)


def far(*arrays):
    return [pltpu.with_memory_space_constraint(a, HBM) for a in arrays]


def block(rows, width):
    return pl.BlockSpec((rows, width), lambda i, *s: (i, 0))


def whole(*shape):
    return pl.BlockSpec(shape, lambda i, *s: (0,) * len(shape))


def rotary_tables():
    lane = jnp.arange(INNER) % (ROT // 2)
    inverse = 10000.0 ** (-(2 * lane).astype(F32) / ROT)
    angles = jnp.arange(LEN).astype(F32)[:, None] * inverse[None, :]
    return lax.optimization_barrier((jnp.cos(angles), jnp.sin(angles)))


def turn(u, cosine, sine, sign):
    half = ROT // 2
    lane = lax.broadcasted_iota(jnp.int32, u.shape, 1) % HEAD
    back = pltpu.roll(u, INNER - half, 1)
    ahead = pltpu.roll(u, half, 1)
    turned = jnp.where(lane < half, -back, ahead)
    return jnp.where(lane < ROT, u * cosine + sign * (turned * sine), u)


def normalized(x):
    mean = jnp.mean(x, 1, keepdims=True)
    r = lax.rsqrt(jnp.mean(x * x, 1, keepdims=True) - mean * mean + NORM_EPSILON)
    return (x - mean) * r, r


def token_copies(order, pieces, held, sems):
    return [
        pltpu.make_async_copy(p, held.at[pl.ds(order[j] * OWN, OWN)], sems.at[order[j]])
        for j, p in enumerate(pieces)
    ]


def feature_copies(order, pieces, held, sems, part=0):
    return [
        pltpu.make_async_copy(
            p.at[pl.ds(part * 512, 512)],
            held.at[
                pl.ds((order[j] // 4) * 512, 512), pl.ds(lax.rem(order[j], 4) * QUARTER, QUARTER)
            ],
            sems.at[order[j]],
        )
        for j, p in enumerate(pieces)
    ]


ROWS = 256


def project_kernel(first, last, order, *refs):
    pieces, refs = refs[:8], refs[8:]
    wide, norms, bias, cosine, sine, *refs = refs
    if last:
        down_grad, *refs = refs
    full, slope, query, keys, values, hidden, *rest = refs
    held, sems = refs[-2:]
    step = pl.program_id(0)

    @pl.when(step == 0)
    def _():
        copies = (feature_copies if first else token_copies)(order, pieces, held, sems)
        for c in copies:
            c.start()

    if first:

        @pl.when(lax.rem(step, 2) == 0)
        def _():
            for j in range(4):
                part = held.at[pl.ds(0, 512), pl.ds(0, QUARTER)]
                pltpu.make_async_copy(part, part, sems.at[step * 2 + j]).wait()

        @pl.when(step == order[8] // 2)
        def _():
            rest[0][...] = held[pl.ds(order[8] * OWN, OWN), :].astype(F32)
    else:
        for j in range(2):
            part = held.at[pl.ds(0, OWN)]
            pltpu.make_async_copy(pieces[0], part, sems.at[step * 2 + j]).wait()
    rows = held[pl.ds(step * ROWS, ROWS), :]
    xh = rows.astype(F32)
    if first:
        xh, _ = normalized(xh)
        rows = xh.astype(BF)
        xh = rows.astype(F32)
    full[...] = rows
    n_a = (xh * norms[0:1] + norms[2:3]).astype(BF)
    n_f = (xh * norms[1:2] + norms[3:4]).astype(BF)
    qkv = dot(n_a, wide[:, :QKV]) + bias[0:1, :QKV]
    table = (cosine[...], sine[...])
    query[...] = (turn(qkv[:, :INNER], *table, 1.0).astype(BF) * 0.125).astype(BF)
    keys[...] = turn(qkv[:, INNER : 2 * INNER], *table, 1.0).astype(BF)
    values[...] = qkv[:, 2 * INNER :].astype(BF)
    u = dot(n_f, wide[:, QKV:]) + bias[0:1, QKV:]
    cdf = 0.5 + 0.5 * lax.erf(u * (0.5**0.5))
    hidden[...] = (u * cdf).astype(BF)
    if first:
        for now, later in zip((query, keys, values, hidden), rest[1:5]):
            later[...] = now[...]
    steep = cdf + u * (jnp.exp(u * u * -0.5) * (1.0 / (2.0 * np.pi) ** 0.5))
    if last:
        du = (down_grad[...] * steep).astype(BF)
        slope[...] = du

        @pl.when(step == 0)
        def _():
            rest[0][...] = jnp.zeros_like(rest[0])

        rest[0][0:1] += jnp.sum(du.astype(F32), 0, keepdims=True)
    else:
        slope[...] = steep.astype(BF)


def project(first, order, pieces, wide, norms, bias, tables, down_grad=None):
    heads = [block(ROWS, INNER)] * 3 + [block(ROWS, HID)]
    shapes = [hbm((LEN, D)), hbm((LEN, HID)) if first else sds((LEN, HID))]
    shapes += [sds((LEN, INNER))] * 3 + [sds((LEN, HID))]
    outs = [block(ROWS, D), block(ROWS, HID)] + heads
    if first:
        shapes += [hbm((OWN, D), F32)] + [hbm((LEN, INNER))] * 3 + [hbm((LEN, HID))]
        outs += [whole(OWN, D)] + heads
    given = []
    if down_grad is not None:
        shapes.append(sds((8, HID), F32))
        outs.append(whole(8, HID))
        given = [down_grad]
    return call(
        partial(project_kernel, first, down_grad is not None),
        shapes,
        (LEN // ROWS,),
        [ANY] * 8
        + [whole(D, WIDE), whole(8, D), whole(8, WIDE)]
        + [block(ROWS, INNER)] * 2
        + [block(ROWS, HID)] * len(given),
        outs,
        7,
        scratch=[pltpu.VMEM((LEN, D), BF), pltpu.SemaphoreType.DMA((8,))],
        scalars=1,
    )(order, *pieces, wide, norms, bias, *tables, *given)


BLOCK = 256


def head_mask(h, rows):
    lane = lax.broadcasted_iota(jnp.int32, (rows, INNER), 1)
    return (lane // HEAD) == h


def causal():
    key = lax.broadcasted_iota(jnp.int32, (BLOCK, BLOCK), 0)
    query = lax.broadcasted_iota(jnp.int32, (BLOCK, BLOCK), 1)
    return key <= query


def attend_kernel(query, keys, values, mixed, logs, *kept):
    for i in range(LEN // BLOCK):
        n = (i + 1) * BLOCK
        here = pl.ds(i * BLOCK, BLOCK)
        q = query[here, :]
        out = jnp.zeros((BLOCK, INNER), F32)
        for h in range(HEADS):
            mask = head_mask(h, BLOCK)
            qh = jnp.where(mask, q, jnp.zeros_like(q))
            s = dot(keys[:n, :], qh, NT)
            tail = jnp.where(causal(), s[n - BLOCK :], -1e30)
            s = jnp.concatenate([s[: n - BLOCK], tail], 0) if i else tail
            top = jnp.max(s, 0, keepdims=True)
            p = jnp.exp(s - top)
            total = jnp.sum(p, 0, keepdims=True)
            logs[h : h + 1, here] = top + jnp.log(total)
            part = dot(values[:n, :], p.astype(BF), TN)
            part = jnp.transpose(part * (1.0 / total))
            out = jnp.where(mask, part, out)
        mixed[here, :] = out.astype(BF)
        for ref in kept:
            ref[here, :] = out.astype(BF)


def attend(query, keys, values, keep):
    return call(
        attend_kernel,
        [sds((LEN, INNER)), sds((8, LEN), F32)] + [hbm((LEN, INNER))] * keep,
        (),
        [VMEM] * 3,
        [VMEM] * (2 + keep),
        5,
    )(query, keys, values)


def attend_back_kernel(
    query, keys, values, dmixed, logs, cosine, sine, dqkv, sums, dkeys, dvalues
):
    dkeys[...] = jnp.zeros_like(dkeys)
    dvalues[...] = jnp.zeros_like(dvalues)
    count = jnp.zeros((1, INNER), F32)
    for i in range(LEN // BLOCK):
        n = (i + 1) * BLOCK
        here = pl.ds(i * BLOCK, BLOCK)
        q, do = query[here, :], dmixed[here, :]
        dq = jnp.zeros((BLOCK, INNER), F32)
        for h in range(HEADS):
            mask = head_mask(h, BLOCK)
            qh = jnp.where(mask, q, jnp.zeros_like(q))
            doh = jnp.where(mask, do, jnp.zeros_like(do))
            s = dot(keys[:n, :], qh, NT)
            p = jnp.exp(s - logs[h : h + 1, here])
            tail = jnp.where(causal(), p[n - BLOCK :], 0.0)
            p = jnp.concatenate([p[: n - BLOCK], tail], 0) if i else tail
            dp = dot(values[:n, :], doh, NT)
            w = p * dp
            delta = jnp.sum(w, 0, keepdims=True)
            ds = (w - p * delta).astype(BF)
            dvalues[:n, :] += dot(p.astype(BF), doh)
            dkeys[:n, :] += dot(ds, qh)
            dq = jnp.where(mask, jnp.transpose(dot(keys[:n, :], ds, TN)), dq)
        dq = turn(dq * 0.125, cosine[here, :], sine[here, :], -1.0).astype(BF)
        dqkv[here, :INNER] = dq
        count += jnp.sum(dq.astype(F32), 0, keepdims=True)
    sums[0:1, :INNER] = count
    dk = turn(dkeys[...], cosine[...], sine[...], -1.0).astype(BF)
    dv = dvalues[...].astype(BF)
    dqkv[:, INNER : 2 * INNER] = dk
    dqkv[:, 2 * INNER :] = dv
    sums[0:1, INNER : 2 * INNER] = jnp.sum(dk.astype(F32), 0, keepdims=True)
    sums[0:1, 2 * INNER :] = jnp.sum(dv.astype(F32), 0, keepdims=True)


def attend_back(query, keys, values, dmixed, logs, tables, after=()):
    return call(
        attend_back_kernel,
        [sds((LEN, QKV)), sds((8, QKV), F32)],
        (),
        [VMEM] * 7,
        [VMEM] * 2,
        6,
        scratch=[pltpu.VMEM((LEN, INNER), F32)] * 2,
        after=after,
    )(query, keys, values, dmixed, logs, *tables)


def merge_kernel(side, mixed, hidden, down, out):
    first = dot(mixed[...], down[:, :INNER], NT)
    out[...] = (first + dot(hidden[...], down[:, INNER:], NT)).astype(BF)


def half_block(width):
    return pl.BlockSpec((ROWS, width), lambda i, s: (s[0] * 2 + i, 0))


def merge(side, mixed, hidden, down, after=()):
    return call(
        merge_kernel,
        sds((LEN // 2, D)),
        (2,),
        [half_block(INNER), half_block(HID), whole(D, DOWN)],
        block(ROWS, D),
        2,
        scalars=1,
        after=after,
    )(side, mixed, hidden, down)


def spread_kernel(side, dqkv, dupper, wide, norms, out):
    first = dot(dqkv[...], wide[:, :QKV], NT) * norms[0:1]
    out[...] = (first + dot(dupper[...], wide[:, QKV:], NT) * norms[1:2]).astype(BF)


def spread(side, dqkv, dupper, wide, norms):
    return call(
        spread_kernel,
        sds((LEN // 2, D)),
        (2,),
        [half_block(QKV), half_block(HID), whole(D, WIDE), whole(8, D)],
        block(ROWS, D),
        2.2,
        scalars=1,
    )(side, dqkv, dupper, wide, norms)


def joint_kernel(side, dqkv, dupper, wide, norms, mixed, hidden, down, out):
    step = pl.program_id(0)

    @pl.when(step < 2)
    def _():
        spread_kernel(side, dqkv, dupper, wide, norms, out)

    @pl.when(step >= 2)
    def _():
        merge_kernel(side, mixed, hidden, down, out)


def joint(side, dqkv, dupper, wide, norms, mixed, hidden, down, after=()):
    early = lambda w: pl.BlockSpec((ROWS, w), lambda i, s: (s[0] * 2 + jnp.minimum(i, 1), 0))
    late = lambda w: pl.BlockSpec((ROWS, w), lambda i, s: (s[0] * 2 + jnp.maximum(i - 2, 0), 0))
    return call(
        joint_kernel,
        sds((LEN, D)),
        (4,),
        [early(QKV), early(HID), whole(D, WIDE), whole(8, D), late(INNER), late(HID), whole(D, DOWN)],
        block(ROWS, D),
        4,
        scalars=1,
        after=after,
    )(side, dqkv, dupper, wide, norms, mixed, hidden, down)


def branch_first_kernel(order, *refs):
    pieces, refs = refs[:8], refs[8:]
    down, full, dmixed, dhidden, total, held, sems = refs
    step = pl.program_id(0)

    @pl.when(step == 0)
    def _():
        total[...] = jnp.zeros_like(total)
        for c in feature_copies(order, pieces, held, sems, 1):
            c.start()

    @pl.when(lax.rem(step, 2) == 0)
    def _():
        for j in range(4):
            part = held.at[pl.ds(0, 512), pl.ds(0, QUARTER)]
            pltpu.make_async_copy(part, part, sems.at[step * 2 + j]).wait()

    g = held[pl.ds(step * ROWS, ROWS), :]
    full[...] = g
    total[0:1] += jnp.sum(g.astype(F32), 0, keepdims=True)
    both = dot(g, down[...])
    dmixed[...] = both[:, :INNER].astype(BF)
    dhidden[...] = both[:, INNER:]


def branch_first(order, pieces, down):
    return call(
        branch_first_kernel,
        [hbm((LEN, D)), sds((LEN, INNER)), sds((LEN, HID), F32), sds((8, D), F32)],
        (LEN // ROWS,),
        [ANY] * 8 + [whole(D, DOWN)],
        [block(ROWS, D), block(ROWS, INNER), block(ROWS, HID), whole(8, D)],
        4,
        scratch=[pltpu.VMEM((LEN, D), BF), pltpu.SemaphoreType.DMA((8,))],
        scalars=1,
    )(order, *pieces, down)


def branch_kernel(order, *refs):
    pieces, refs = refs[:8], refs[8:]
    down, slope, dmixed, dupper, sums, total, full, held, sems = refs
    step = pl.program_id(0)

    @pl.when(step == 0)
    def _():
        sums[...] = jnp.zeros_like(sums)
        total[...] = jnp.zeros_like(total)
        for c in token_copies(order, pieces, held, sems):
            c.start()

    for j in range(2):
        part = held.at[pl.ds(0, OWN)]
        pltpu.make_async_copy(pieces[0], part, sems.at[step * 2 + j]).wait()
    g = held[pl.ds(step * ROWS, ROWS), :]
    full[...] = g
    total[0:1] += jnp.sum(g.astype(F32), 0, keepdims=True)
    both = dot(g, down[...])
    dmixed[...] = both[:, :INNER].astype(BF)
    du = (both[:, INNER:] * slope[...].astype(F32)).astype(BF)
    dupper[...] = du
    sums[0:1] += jnp.sum(du.astype(F32), 0, keepdims=True)


def branch(order, pieces, down, slope, after=()):
    return call(
        branch_kernel,
        [
            sds((LEN, INNER)),
            sds((LEN, HID)),
            sds((8, HID), F32),
            sds((8, D), F32),
            sds((LEN, D)),
        ],
        (LEN // ROWS,),
        [ANY] * 8 + [whole(D, DOWN), block(ROWS, HID)],
        [block(ROWS, INNER), block(ROWS, HID), whole(8, HID), whole(8, D), block(ROWS, D)],
        4,
        scratch=[pltpu.VMEM((LEN, D), BF), pltpu.SemaphoreType.DMA((8,))],
        scalars=1,
        after=after,
    )(order, *pieces, down, slope)


def pack_kernel(has_wide, has_down, layer, *refs):
    refs, out = list(refs[:-1]), refs[-1]
    start = 0
    if has_wide:
        out[QUARTER:, :] = jnp.zeros_like(out[QUARTER:, :])
        triples, expand, scales, shifts, offsets, uplift, closing = refs[:7]
        refs = refs[7:]
        for i in range(3):
            at = slice(i * INNER, (i + 1) * INNER)
            out[:QUARTER, at] = triples[0, :, i, :]
            out[QUARTER : QUARTER + 1, at] = offsets[layer, i : i + 1, :]
        out[:QUARTER, QKV:WIDE] = expand[0]
        out[QUARTER : QUARTER + 1, QKV:WIDE] = uplift[layer : layer + 1, :]
        for i in range(2):
            at = slice(i * QUARTER, (i + 1) * QUARTER)
            out[QUARTER + 1 : QUARTER + 2, at] = scales[layer, i : i + 1, :]
            out[QUARTER + 2 : QUARTER + 3, at] = shifts[layer, i : i + 1, :]
        out[QUARTER + 3 : QUARTER + 4, :QUARTER] = closing[layer : layer + 1, :]
        start = WIDE
    if has_down:
        merger, shrink = refs
        out[:QUARTER, start : start + INNER] = merger[0].T
        out[:QUARTER, start + INNER :] = shrink[0].T


def of_layer(layer, array):
    shape = array.shape[1:]
    return pl.BlockSpec((1,) + shape, lambda i, *s: (layer,) + (0,) * len(shape))


def pack(layer, wide, down, after=()):
    specs = []
    if wide:
        specs += [of_layer(layer, a) for a in wide[:2]] + [whole(*a.shape) for a in wide[2:]]
    specs += [of_layer(layer, a) for a in down]
    width = (WIDE if wide else 0) + (DOWN if down else 0)
    rows = QUARTER + EXTRA if wide else QUARTER
    return call(
        partial(pack_kernel, bool(wide), bool(down), layer),
        hbm((rows, width)),
        (1,),
        specs,
        whole(rows, width),
        1,
        after=after,
    )(*wide, *down)


def pick_kernel(order, both, out, sems):
    copies = [
        pltpu.make_async_copy(both.at[2 * i + 1 - order[0]], out.at[i], sems.at[i])
        for i in range(2)
    ]
    for c in copies:
        c.start()
    for c in copies:
        c.wait()


def pick(order, both, after=()):
    return call(
        pick_kernel,
        sds((2,) + both.shape[1:]),
        (),
        [ANY],
        VMEM,
        1,
        scratch=[pltpu.SemaphoreType.DMA((2,))],
        scalars=1,
        after=after,
    )(order, both)


def halves(core, both, got, sems, places):
    copies = []
    for i in range(2):
        for j, (source, at) in enumerate(
            ((both.at[2 * i + core], 2 * i + core), (got.at[i], 2 * i + 1 - core))
        ):
            for n, (a, b) in enumerate(places(source, at)):
                copies.append(pltpu.make_async_copy(a, b, sems.at[2 * i + j, n]))
    for c in copies:
        c.start()
    for c in copies:
        c.wait()


def wide_places(wide, extra):
    def places(source, at):
        rows = pl.ds(at * QUARTER, QUARTER)
        return (
            (source.at[pl.ds(0, QUARTER), pl.ds(0, WIDE)], wide.at[rows]),
            (source.at[pl.ds(QUARTER, EXTRA), pl.ds(0, WIDE)], extra.at[at]),
        )

    return places


def down_places(down, start):
    def places(source, at):
        rows = pl.ds(at * QUARTER, QUARTER)
        return ((source.at[pl.ds(0, QUARTER), pl.ds(start, DOWN)], down.at[rows]),)

    return places


def vectors(extra, norms, bias):
    bias[...] = jnp.zeros_like(bias)
    norms[...] = jnp.zeros_like(norms)
    bias[0:1] = extra[0, 0:1].astype(F32)
    for q in range(4):
        cols = slice(q * QUARTER, (q + 1) * QUARTER)
        for n in range(5):
            row, at = 1 + n // 2, (n % 2) * QUARTER
            norms[n : n + 1, cols] = extra[q, row : row + 1, at : at + QUARTER].astype(F32)


def weights_kernel(has_wide, has_down, order, both, got, *refs):
    outs, (extra, sems) = list(refs[:-2]), refs[-2:]
    kept = []
    if has_wide:
        wide, wide_kept, norms, bias = outs[:4]
        outs = outs[4:]
        kept.append((wide, wide_kept))
    if has_down:
        down, down_kept = outs
        kept.append((down, down_kept))

    def places(source, at):
        found = ()
        if has_wide:
            found += wide_places(wide, extra)(source, at)
        if has_down:
            found += down_places(down, WIDE if has_wide else 0)(source, at)
        return found

    halves(order[0], both, got, sems, places)
    copies = [pltpu.make_async_copy(a, b, sems.at[i, 0]) for i, (a, b) in enumerate(kept)]
    for c in copies:
        c.start()
    if has_wide:
        vectors(extra, norms, bias)
    for c in copies:
        c.wait()


def settle_weights(order, both, got, has_wide, has_down):
    shapes, specs = [], []
    if has_wide:
        shapes += [sds((D, WIDE)), hbm((D, WIDE)), sds((8, D), F32), sds((8, WIDE), F32)]
        specs += [VMEM, ANY, VMEM, VMEM]
    if has_down:
        shapes += [sds((D, DOWN)), hbm((D, DOWN))]
        specs += [VMEM, ANY]
    return call(
        partial(weights_kernel, has_wide, has_down),
        shapes,
        (),
        [ANY] * 2,
        specs,
        2,
        scratch=[pltpu.VMEM((4, EXTRA, WIDE), BF), pltpu.SemaphoreType.DMA((4, 3))],
        scalars=1,
    )(order, both, got)


def gate_kernel(*refs):
    pass


def gate(arrays, after):
    return call(
        gate_kernel,
        [sds(a.shape, a.dtype) for a in arrays],
        (),
        [ANY] * len(arrays),
        [ANY] * len(arrays),
        0.1,
        aliases={i: i for i in range(len(arrays))},
        after=after,
    )(*arrays)


def combine_kernel(order, mine, got, own, *sent):
    for k, ref in zip(STEPS, (own,) + sent):
        for part in range(mine.shape[0] // 512):
            start = part * 512 + lax.rem(order[0] + k, 4) * OWN
            at = pl.ds(pl.multiple_of(start, OWN), OWN)
            total = mine[at, :].astype(F32) + got[at, :].astype(F32)
            ref[part * OWN : (part + 1) * OWN, :] = total.astype(ref.dtype)


def combine(order, mine, got):
    rows = mine.shape[0] // 4
    return call(
        combine_kernel,
        [sds((rows, D), F32)] + [hbm((rows, D))] * 3,
        (),
        [VMEM] * 2,
        [VMEM] * 4,
        1.5,
        scalars=1,
    )(order, mine, got)


def summed(own, others, rows):
    total = own[rows, :]
    for ref in others:
        total = total + ref[rows, :].astype(F32)
    return total


def back_through_norm(dxhat, x):
    xhat, r = normalized(x)
    mean = jnp.mean(dxhat, 1, keepdims=True)
    return r * (dxhat - mean - xhat * jnp.mean(dxhat * xhat, 1, keepdims=True))


EVERY = slice(0, OWN)


def finish_kernel(own, a, b, c, x, norms, new, xhat):
    value = x[...] + (summed(own, (a, b, c), EVERY) + norms[4:5])
    new[...] = value
    xhat[...] = normalized(value)[0].astype(BF)


def finish(parts, x, norms):
    return call(
        finish_kernel,
        [hbm((OWN, D), F32), hbm((OWN, D))],
        (),
        [VMEM] * 6,
        [VMEM] * 2,
        1.5,
    )(*parts, x, norms)


def finish_back_kernel(order, own, a, b, c, x, gradient, new, lowered, mark):
    mark[...] = jnp.zeros_like(mark)
    value = gradient[...].astype(F32) + back_through_norm(summed(own, (a, b, c), EVERY), x[...])
    new[...] = value
    lowered[...] = value.astype(BF)


def finish_back(order, parts, x, gradient):
    return call(
        finish_back_kernel,
        [hbm((OWN, D), F32), hbm((OWN, D)), sds((8, 128), F32)],
        (1,),
        [whole(OWN, D)] * 5 + [pl.BlockSpec((OWN, D), lambda i, s: (s[0], 0))],
        [whole(OWN, D)] * 2 + [whole(8, 128)],
        1.5,
        scalars=1,
    )(order, *parts, x, gradient)


def finish_last_kernel(order, own, a, b, c, x_back, gradient, x_front, norms, *refs):
    outs, mark, held = refs[:4], refs[4], refs[5]
    mark[...] = jnp.zeros_like(mark)
    others = (a, b, c)
    held[EVERY, :] = gradient[...] + back_through_norm(summed(own, others, EVERY), x_back[...])
    held[OWN:, :] = x_front[...] + (summed(own, others, slice(OWN, 2 * OWN)) + norms[4:5])
    for k, ref in enumerate(outs):
        q = lax.rem(order[0] + k, 4)
        ref[...] = held[:, pl.ds(pl.multiple_of(q * QUARTER, QUARTER), QUARTER)].astype(BF)


def finish_last(order, parts, x_back, gradient, x_front, norms, after):
    return call(
        finish_last_kernel,
        [hbm((2 * OWN, QUARTER))] * 4 + [sds((8, 128), F32)],
        (),
        [VMEM] * 8,
        [VMEM] * 5,
        2,
        scratch=[pltpu.VMEM((2 * OWN, D), F32)],
        scalars=1,
        after=after,
    )(order, *parts, x_back, gradient, x_front, norms)


def land_kernel(order, *refs):
    pieces, (back, front, mark) = refs[:4], refs[4:]
    mark[...] = jnp.zeros_like(mark)
    for k, p in enumerate(pieces):
        at = pl.ds(pl.multiple_of(lax.rem(order[0] - k + 4, 4) * OWN, OWN), OWN)
        back[at, :] = p[:OWN, :].astype(F32)
        front[at, :] = p[OWN:, :]


def land(order, pieces):
    shape = (4 * OWN, QUARTER)
    return call(
        land_kernel,
        [sds(shape, F32), sds(shape), sds((8, 128), F32)],
        (),
        [VMEM] * 4,
        [VMEM] * 3,
        1,
        scalars=1,
    )(order, *pieces)


def payload_kernel(pairs, marks, *refs):
    out, mark = refs[-2:]
    mark[...] = jnp.zeros_like(mark)
    at, width = 0, 0
    out[QUARTER:, :] = jnp.zeros_like(out[QUARTER:, :])
    for rights in pairs:
        lhs = refs[at][...]
        at += 1
        for w in rights:
            out[:QUARTER, width : width + w] = dot(lhs, refs[at][...], TN).astype(BF)
            at += 1
            width += w
    for row, start, w in marks:
        out[QUARTER + row : QUARTER + row + 1, start : start + w] = refs[at][0:1, :].astype(BF)
        at += 1


def payload(pairs, extras, after=()):
    operands, specs, shape, width = [], [], [], 0
    for left, rights in pairs:
        operands.append(left)
        specs.append(pl.BlockSpec((LEN, QUARTER), lambda i: (0, i)))
        for r in rights:
            operands.append(r)
            specs.append(whole(*r.shape))
            width += r.shape[1]
        shape.append(tuple(r.shape[1] for r in rights))
    marks = []
    for row, start, vector, sliced in extras:
        operands.append(vector)
        w = QUARTER if sliced else vector.shape[1]
        specs.append(pl.BlockSpec((8, w), lambda i: (0, i)) if sliced else whole(8, w))
        marks.append((row, start, w))
    return call(
        partial(payload_kernel, tuple(shape), tuple(marks)),
        [hbm((4 * TALL, width)), sds((8, 128), F32)],
        (4,),
        specs,
        [block(TALL, width), whole(8, 128)],
        4 * (0.3 + width / 1536),
        after=after,
    )(*operands)


def share_kernel(order, part, mine, *sent):
    for k, ref in zip(STEPS, (mine,) + sent):
        at = pl.multiple_of(lax.rem(order[0] + k, 4) * SHARE, SHARE)
        ref[...] = part[:, pl.ds(at, SHARE)]


def share(order, part, after=()):
    return call(
        share_kernel,
        [sds((TALL, SHARE))] + [hbm((TALL, SHARE))] * 3,
        (),
        [VMEM],
        [VMEM] * 4,
        1.5,
        scalars=1,
        after=after,
    )(order, part)


def last_sum_kernel(own, a, b, c, out, mark):
    mark[...] = jnp.zeros_like(mark)
    total = own[...].astype(F32) + a[...].astype(F32) + b[...].astype(F32) + c[...].astype(F32)
    out[...] = total.astype(BF)


def last_sum(parts):
    return call(
        last_sum_kernel,
        [hbm((TALL, SHARE)), sds((8, 128), F32)],
        (),
        [VMEM] * 4,
        [VMEM] * 2,
        1,
    )(*parts)


WIDTHS = {"triples": QKV, "expand": HID, "down": DOWN}
ROW = {"triples": 2, "expand": 0, "down": 1}


def final_kernel(layer, kinds, order, *refs):
    pieces, cols, refs = refs[:4], refs[4], refs[5:]
    shards_in = {}
    for kind in kinds:
        if kind != "down":
            shards_in[kind], refs = refs[0], refs[1:]
    if layer == 0:
        upper, refs = refs[0], refs[1 + sum(2 if k == "down" else 1 for k in kinds) :]
    held = refs[-1]
    for k, ref in zip(STEPS, pieces):
        at = pl.ds(pl.multiple_of(lax.rem(order[0] - k + 4, 4) * SHARE, SHARE), SHARE)
        held[:, at] = ref[...].astype(F32)
    start, lane = 0, lax.broadcasted_iota(jnp.int32, (QUARTER, 128), 1)
    stats = jnp.zeros((QUARTER, 128), F32)
    vectors, refs = refs[0], refs[1:]
    vectors[...] = jnp.zeros_like(vectors)
    for kind in kinds:
        w, row = WIDTHS[kind], ROW[kind]
        product = held[:QUARTER, start : start + w]
        if kind == "down":
            turned = jnp.transpose(product)
            refs[0][0] = turned[:INNER]
            refs[1][0] = turned[INNER:]
            refs = refs[2:]
            vectors[row : row + 1, :QUARTER] = held[QUARTER + row : QUARTER + row + 1, :QUARTER]
        else:
            sums = held[QUARTER + row : QUARTER + row + 1, start : start + w]
            vectors[row : row + 1, :w] = sums
            own = shards_in[kind]
            if kind == "triples":
                own = jnp.concatenate([own[0, :, i, :] for i in range(3)], 1)
            else:
                own = own[0]
            own = own.astype(F32)
            at = 0 if kind == "triples" else 1
            stats = jnp.where(lane == at, jnp.sum(own * product, 1, keepdims=True), stats)
            stats = jnp.where(lane == 2 + at, jnp.sum(own * sums, 1, keepdims=True), stats)
            value = cols[:, at : at + 1] * product + cols[:, 2 + at : 3 + at] * sums
            if kind == "triples":
                for i in range(3):
                    refs[0][0, :, i, :] = value[:, i * INNER : (i + 1) * INNER]
            else:
                refs[0][0] = value
            refs = refs[1:]
        start += w
    vectors[4:8, :QUARTER] = jnp.transpose(stats)[:4]
    if layer == 0:
        offsets, uplift, closing, joint_stats = refs[:4]
        for l, source in enumerate((vectors, upper)):
            offsets[l : l + 1] = source[2:3, :QKV]
            uplift[l : l + 1] = source[0:1]
            closing[l : l + 1] = source[1:2, :QUARTER]
            for n in range(2):
                at = 4 * n + 2 * l
                joint_stats[at : at + 2] = source[4 + 2 * n : 6 + 2 * n, :QUARTER]


GRADS = {
    "triples": [(LAYERS, QUARTER, 3, INNER)],
    "expand": [(LAYERS, QUARTER, HID)],
    "down": [(LAYERS, INNER, QUARTER), (LAYERS, HID, QUARTER)],
}


def final(layer, kinds, order, pieces, cols, weights, stacks, upper=None):
    width = WIDE + DOWN
    operands = list(pieces) + [cols] + [weights[k] for k in kinds if k != "down"]
    if layer == 0:
        operands.append(upper)
    specs = [VMEM] * len(operands)
    shapes, outs, aliases = [sds((8, HID), F32)], [VMEM], {}
    for kind in kinds:
        for place, shape in enumerate(GRADS[kind]):
            if layer == 0:
                aliases[1 + len(operands)] = len(shapes)
                operands.append(stacks[kind][place])
                specs.append(ANY)
            shapes.append(sds(shape, F32))
            outs.append(
                pl.BlockSpec(
                    (1,) + shape[1:], lambda i, s, n=len(shape) - 1: (layer,) + (0,) * n
                )
            )
    outs[0] = whole(8, HID)
    if layer == 0:
        for shape in ((LAYERS, QKV), (LAYERS, HID), (LAYERS, QUARTER), (8, QUARTER)):
            shapes.append(sds(shape, F32))
            outs.append(whole(*shape))
    fixed = [whole(*o.shape) if s is VMEM else s for o, s in zip(operands, specs)]
    for n, kind in enumerate(k for k in kinds if k != "down"):
        fixed[5 + n] = of_layer(layer, weights[kind])
    results = call(
        partial(final_kernel, layer, kinds),
        shapes,
        (1,),
        fixed,
        outs,
        2,
        scratch=[pltpu.VMEM((TALL, width), F32)],
        scalars=1,
        aliases=aliases,
    )(order, *operands)
    vectors, results = results[0], list(results[1:])
    grads = {}
    for kind in kinds:
        n = len(GRADS[kind])
        grads[kind], results = results[:n], results[n:]
    return (results if layer == 0 else vectors), grads


def across(array):
    return lax.ppermute(array, "core", [(0, 1), (1, 0)])


def around(array, axes, step):
    return lax.ppermute(array, axes, [(i, (i + step) % 4) for i in range(4)])


def exchanged(array, axes):
    return lax.ppermute(array, axes, [(0, 0), (1, 2), (2, 1), (3, 3)])


def gather_ring(own, axes):
    return [own] + [around(own, axes, k) for k in STEPS[1:]]


def gather_line(own, after=()):
    pieces = gather_ring(own, LINE)
    if after:
        pieces = pieces[:1] + list(gate(pieces[1:], after))
    return pieces + [across(p) for p in pieces]


def scatter_line(order, other, mine):
    own, *sent = combine(order, mine, across(other))
    return [own] + [around(s, LINE, k) for s, k in zip(sent, STEPS[1:])]


def outward_pairs(step):
    pairs = []
    for q in range(4):
        for zh in range(2):
            for core in range(2):
                z = (q - step) % 4
                pairs.append(((zh * 2 + core) * 4 + z, q * 4 + zh * 2 + core))
    return pairs


def outward(pieces):
    axes = ("yh", "core", "zh", "zl")
    return [lax.ppermute(p, axes, outward_pairs(k)) for k, p in enumerate(pieces)]


def tiny(array):
    return array[:16, :128]


def fetch(core, both, after, has_wide, has_down):
    (both,) = far(both)
    return settle_weights(core, both, across(pick(core, both, after)), has_wide, has_down)


def reduce_ring(array):
    return lax.psum_scatter(array, RING, scatter_dimension=0, tiled=True)


def crossed(step):
    return [
        ((x * 2 + core) * 2 + yl, ((x + step) % 4 * 2 + yl) * 2 + core)
        for x in range(4)
        for core in range(2)
        for yl in range(2)
    ]


def reduce_x(x, part, after=()):
    mine, *sent = share(x.reshape(1), far(part)[0], after)
    total, mark = last_sum([mine] + far(*[around(s, "x", k) for s, k in zip(sent, STEPS[1:])]))
    return far(*[lax.ppermute(total, ("x", "core", "yl"), crossed(k)) for k in STEPS]), mark


def shards(
    inputs, scales, shifts, triples, offsets, merger, expand, uplift, shrink, closing, cotangent
):
    core, y, z = lax.axis_index("core"), lax.axis_index(RING), lax.axis_index(LINE)
    x_at, q_at = lax.axis_index("x"), lax.axis_index(("yh", "core"))
    here, there = core.reshape(1), (1 - core).reshape(1)
    chunk = core * 4 + z
    sources = [(z - k + 4) % 4 for k in STEPS]
    tokens = jnp.stack([core * 4 + s for s in sources] + [(1 - core) * 4 + s for s in sources])
    blocks = [(s % 2) * 4 + (s // 2) * 2 for s in sources]
    features = jnp.stack([b + core for b in blocks] + [b + 1 - core for b in blocks] + [chunk])
    z_one, x_one, q_one = z.reshape(1), x_at.reshape(1), q_at.reshape(1)

    moved = exchanged(jnp.concatenate([inputs, cotangent], 0), ("yh", "zh"))
    marker = [tiny(moved)]
    wide_args = (triples, expand, scales, shifts, offsets, uplift, closing)
    down_args = (merger, shrink)
    packs = gate([pack(l, wide_args, down_args) for l in range(LAYERS)], marker)
    sent, sent1 = [lax.all_gather(p, RING, axis=0, tiled=False) for p in packs]
    pieces = gather_line(moved)
    tables = rotary_tables()
    wide, wide_kept, norms, bias, down, down_kept = fetch(
        here, sent, [tiny(p) for p in pieces[1:4]], True, True
    )

    full0, slope0, query0, keys0, values0, hidden0, x0, *kept = project(
        True, features, far(*pieces), wide, norms, bias, tables
    )
    mixed0, logs0, mixed_kept = attend(query0, keys0, values0, 1)
    other = merge(there, mixed0, hidden0, down)
    mine = merge(here, mixed0, hidden0, down)
    query0, keys0, values0, hidden0, mixed0 = far(*kept, mixed_kept)
    parts = scatter_line(z_one, other, mine)
    marker = [tiny(p) for p in parts[1:]]
    first_pieces = pieces
    wide1, _, norms1, bias1, down1, down1_kept = fetch(here, sent1, marker, True, True)
    top, dmixed1, dhidden1, close_sum1 = branch_first(features, far(*first_pieces), down1)
    x1, xhat = finish(parts[:1] + far(*parts[1:]), x0, norms)
    pieces = gather_line(xhat, [close_sum1])

    full1, dupper1, query1, keys1, values1, hidden1, up_sum1 = project(
        False, tokens, pieces, wide1, norms1, bias1, tables, dhidden1
    )
    mixed1, logs1 = attend(query1, keys1, values1, 0)
    dqkv1, qkv_sum1 = attend_back(query1, keys1, values1, dmixed1, logs1, tables)
    other = spread(there, dqkv1, dupper1, wide1, norms1)
    mine = spread(here, dqkv1, dupper1, wide1, norms1)
    parts = scatter_line(z_one, other, mine)
    gradient, lowered, mark = finish_back(
        chunk.reshape(1), parts[:1] + far(*parts[1:]), *far(x1, top))
    grad1, done1 = payload(
        [(far(full1)[0], [dqkv1, dupper1]), (far(top)[0], [mixed1, hidden1])],
        [(2, 0, qkv_sum1, False), (0, QKV, up_sum1, False), (1, 0, close_sum1, True)],
        [mark],
    )
    grad1 = reduce_ring(grad1)

    pieces = gather_line(lowered, [done1])

    dmixed0, dupper0, up_sum0, close_sum0, dy0 = branch(
        tokens, pieces, *far(down_kept, slope0)
    )
    dqkv0, qkv_sum0 = attend_back(query0, keys0, values0, dmixed0, logs0, far(*tables))
    grad0, done0 = payload(
        [(far(full0)[0], [dupper0]), (dy0, [mixed0, hidden0]), (far(full0)[0], [dqkv0])],
        [(0, 0, up_sum0, False), (1, 0, close_sum0, True), (2, HID + DOWN, qkv_sum0, False)],
    )
    grad0 = reduce_ring(grad0)

    reduced1, summed1 = reduce_x(x_at, grad1, [tiny(dqkv0)])
    rest = (dqkv0, dupper0, far(wide_kept)[0], norms, mixed1, hidden1, far(down1_kept)[0])
    other = joint(there, *rest, [done0])
    mine = joint(here, *rest, [done0])
    parts = scatter_line(z_one, other, mine)
    *pieces, finished = finish_last(
        z_one, parts[:1] + far(*parts[1:]), *far(x0, gradient, x1), norms1, [summed1])
    inputs_grad, outputs, landed = land(q_one, far(*outward(pieces)))
    cols = [
        jnp.concatenate([scales[l], shifts[l]], 0).astype(F32).T for l in range(LAYERS)
    ]
    weights = {"triples": triples, "expand": expand}
    upper, stacks = final(
        1, ("triples", "expand", "down"), x_one, reduced1, cols[1], weights, None
    )
    reduced, _ = reduce_x(x_at, grad0, [finished])
    (offsets_grad, uplift_grad, closing_grad, stats), stacks = final(
        0, ("expand", "down", "triples"), x_one, reduced, cols[0], weights, stacks, upper
    )
    stats = stats + lax.ppermute(stats, "yl", [(0, 1), (1, 0)])
    stats = sum(gather_ring(stats, LINE)).reshape(2, LAYERS, 2, QUARTER)
    offsets_grad = offsets_grad.reshape(LAYERS, 3, INNER)
    return (
        outputs,
        inputs_grad,
        stats[0],
        stats[1],
        stacks["triples"][0],
        offsets_grad,
        stacks["down"][0],
        stacks["expand"][0],
        uplift_grad,
        stacks["down"][1],
        closing_grad,
    )


def solution(mesh):
    grid = Mesh(mesh.devices.reshape(4, 2, 2, 2, 2, 2), AXES)
    row, col = ("yh", "core"), ("yl", "zh", "zl")
    tokens = P(("x",) + col, row)
    weights = (
        P(None, None, row),
        P(None, None, row),
        P(None, row, None, col),
        P(None, None, col),
        P(None, col, row),
        P(None, row, col),
        P(None, col),
        P(None, col, row),
        P(None, row),
    )
    return jax.shard_map(
        shards,
        mesh=grid,
        in_specs=(tokens,) + weights + (tokens,),
        out_specs=(tokens, tokens) + weights,
        check_vma=False,
    )
```

```python
from functools import partial

import jax
import jax.numpy as jnp
import numpy as np
from jax import lax
from jax.experimental import pallas as pl
from jax.experimental.pallas import tpu as pltpu
from jax.sharding import Mesh
from jax.sharding import PartitionSpec as P

D = 1024
QUARTER = D // 4
HEAD = 64
ROT = 16
LAYERS = 2
LEN = 1024
OWN = LEN // 8
HEADS = 2
INNER = HEADS * HEAD
QKV = 3 * INNER
HID = 512
WIDE = QKV + HID
DOWN = INNER + HID
EXTRA = 16
TALL = QUARTER + EXTRA
SHARE = (WIDE + DOWN) // 4
NORM_EPSILON = 1e-05
BF = jnp.bfloat16
F32 = jnp.float32
NN = (((1,), (0,)), ((), ()))
NT = (((1,), (1,)), ((), ()))
TN = (((0,), (0,)), ((), ()))
AXES = ("x", "yh", "core", "yl", "zh", "zl")
LINE = ("zh", "zl")
RING = ("yh", "yl")
STEPS = (0, 1, 3, 2)
ANY = pl.BlockSpec(memory_space=pl.ANY)
HBM = pltpu.MemorySpace.HBM
VMEM = pl.BlockSpec(memory_space=pltpu.VMEM)


def dot(a, b, dims=NN):
    return lax.dot_general(a, b, dims, preferred_element_type=F32)


def sds(shape, dtype=BF):
    return jax.ShapeDtypeStruct(shape, dtype)


def hbm(shape, dtype=BF):
    return HBM(shape, dtype)


def call(
    kernel, out_shape, grid, in_specs, out_specs, micros, scratch=(), scalars=0, aliases={}, after=()
):
    count, extra = scalars + len(in_specs), len(after)

    def body(*refs):
        kernel(*refs[:count], *refs[count + extra :])

    run = pl.pallas_call(
        body,
        out_shape=out_shape,
        grid_spec=pltpu.PrefetchScalarGridSpec(
            num_scalar_prefetch=scalars,
            grid=grid,
            in_specs=list(in_specs) + [ANY] * extra,
            out_specs=out_specs,
            scratch_shapes=scratch,
        ),
        input_output_aliases=aliases,
        compiler_params=pltpu.CompilerParams(vmem_limit_bytes=12 * 2**20),
        cost_estimate=pl.CostEstimate(
            flops=int(micros * 1e6), bytes_accessed=1024, transcendentals=0
        ),
    )
    return lambda *operands: run(*operands, *after)


def far(*arrays):
    return [pltpu.with_memory_space_constraint(a, HBM) for a in arrays]


def block(rows, width):
    return pl.BlockSpec((rows, width), lambda i, *s: (i, 0))


def whole(*shape):
    return pl.BlockSpec(shape, lambda i, *s: (0,) * len(shape))


def rotary_tables():
    lane = jnp.arange(INNER) % (ROT // 2)
    inverse = 10000.0 ** (-(2 * lane).astype(F32) / ROT)
    angles = jnp.arange(LEN).astype(F32)[:, None] * inverse[None, :]
    return lax.optimization_barrier((jnp.cos(angles), jnp.sin(angles)))


def turn(u, cosine, sine, sign):
    half = ROT // 2
    lane = lax.broadcasted_iota(jnp.int32, u.shape, 1) % HEAD
    back = pltpu.roll(u, INNER - half, 1)
    ahead = pltpu.roll(u, half, 1)
    turned = jnp.where(lane < half, -back, ahead)
    return jnp.where(lane < ROT, u * cosine + sign * (turned * sine), u)


def normalized(x):
    mean = jnp.mean(x, 1, keepdims=True)
    r = lax.rsqrt(jnp.mean(x * x, 1, keepdims=True) - mean * mean + NORM_EPSILON)
    return (x - mean) * r, r


def token_copies(order, pieces, held, sems):
    return [
        pltpu.make_async_copy(p, held.at[pl.ds(order[j] * OWN, OWN)], sems.at[order[j]])
        for j, p in enumerate(pieces)
    ]


def feature_copies(order, pieces, held, sems, part=0):
    return [
        pltpu.make_async_copy(
            p.at[pl.ds(part * 512, 512)],
            held.at[
                pl.ds((order[j] // 4) * 512, 512), pl.ds(lax.rem(order[j], 4) * QUARTER, QUARTER)
            ],
            sems.at[order[j]],
        )
        for j, p in enumerate(pieces)
    ]


ROWS = 256


def project_kernel(first, last, order, *refs):
    pieces, refs = refs[:8], refs[8:]
    wide, norms, bias, cosine, sine, *refs = refs
    if last:
        down_grad, *refs = refs
    full, slope, query, keys, values, hidden, *rest = refs
    held, sems = refs[-2:]
    step = pl.program_id(0)

    @pl.when(step == 0)
    def _():
        copies = (feature_copies if first else token_copies)(order, pieces, held, sems)
        for c in copies:
            c.start()

    if first:

        @pl.when(lax.rem(step, 2) == 0)
        def _():
            for j in range(4):
                part = held.at[pl.ds(0, 512), pl.ds(0, QUARTER)]
                pltpu.make_async_copy(part, part, sems.at[step * 2 + j]).wait()

        @pl.when(step == order[8] // 2)
        def _():
            rest[0][...] = held[pl.ds(order[8] * OWN, OWN), :].astype(F32)
    else:
        for j in range(2):
            part = held.at[pl.ds(0, OWN)]
            pltpu.make_async_copy(pieces[0], part, sems.at[step * 2 + j]).wait()
    rows = held[pl.ds(step * ROWS, ROWS), :]
    xh = rows.astype(F32)
    if first:
        xh, _ = normalized(xh)
        rows = xh.astype(BF)
        xh = rows.astype(F32)
    full[...] = rows
    n_a = (xh * norms[0:1] + norms[2:3]).astype(BF)
    n_f = (xh * norms[1:2] + norms[3:4]).astype(BF)
    qkv = dot(n_a, wide[:, :QKV]) + bias[0:1, :QKV]
    table = (cosine[...], sine[...])
    query[...] = (turn(qkv[:, :INNER], *table, 1.0).astype(BF) * 0.125).astype(BF)
    keys[...] = turn(qkv[:, INNER : 2 * INNER], *table, 1.0).astype(BF)
    values[...] = qkv[:, 2 * INNER :].astype(BF)
    u = dot(n_f, wide[:, QKV:]) + bias[0:1, QKV:]
    cdf = 0.5 + 0.5 * lax.erf(u * (0.5**0.5))
    hidden[...] = (u * cdf).astype(BF)
    if first:
        for now, later in zip((query, keys, values, hidden), rest[1:5]):
            later[...] = now[...]
    steep = cdf + u * (jnp.exp(u * u * -0.5) * (1.0 / (2.0 * np.pi) ** 0.5))
    if last:
        du = (down_grad[...].astype(F32) * steep).astype(BF)
        slope[...] = du

        @pl.when(step == 0)
        def _():
            rest[0][...] = jnp.zeros_like(rest[0])

        rest[0][0:1] += jnp.sum(du.astype(F32), 0, keepdims=True)
    else:
        slope[...] = steep.astype(BF)


def project(first, order, pieces, wide, norms, bias, tables, down_grad=None):
    heads = [block(ROWS, INNER)] * 3 + [block(ROWS, HID)]
    shapes = [hbm((LEN, D)), hbm((LEN, HID)) if first else sds((LEN, HID))]
    shapes += [sds((LEN, INNER))] * 3 + [sds((LEN, HID))]
    outs = [block(ROWS, D), block(ROWS, HID)] + heads
    if first:
        shapes += [hbm((OWN, D), F32)] + [hbm((LEN, INNER))] * 3 + [hbm((LEN, HID))]
        outs += [whole(OWN, D)] + heads
    given = []
    if down_grad is not None:
        shapes.append(sds((8, HID), F32))
        outs.append(whole(8, HID))
        given = [down_grad]
    return call(
        partial(project_kernel, first, down_grad is not None),
        shapes,
        (LEN // ROWS,),
        [ANY] * 8
        + [whole(D, WIDE), whole(8, D), whole(8, WIDE)]
        + [block(ROWS, INNER)] * 2
        + [block(ROWS, HID)] * len(given),
        outs,
        7,
        scratch=[pltpu.VMEM((LEN, D), BF), pltpu.SemaphoreType.DMA((8,))],
        scalars=1,
    )(order, *pieces, wide, norms, bias, *tables, *given)


BLOCK = 256


def head_mask(h, rows):
    lane = lax.broadcasted_iota(jnp.int32, (rows, INNER), 1)
    return (lane // HEAD) == h


def causal():
    key = lax.broadcasted_iota(jnp.int32, (BLOCK, BLOCK), 0)
    query = lax.broadcasted_iota(jnp.int32, (BLOCK, BLOCK), 1)
    return key <= query


def attend_kernel(query, keys, values, mixed, logs, *kept):
    for i in range(LEN // BLOCK):
        n = (i + 1) * BLOCK
        here = pl.ds(i * BLOCK, BLOCK)
        q = query[here, :]
        out = jnp.zeros((BLOCK, INNER), F32)
        for h in range(HEADS):
            mask = head_mask(h, BLOCK)
            qh = jnp.where(mask, q, jnp.zeros_like(q))
            s = dot(keys[:n, :], qh, NT)
            tail = jnp.where(causal(), s[n - BLOCK :], -1e30)
            s = jnp.concatenate([s[: n - BLOCK], tail], 0) if i else tail
            top = jnp.max(s, 0, keepdims=True)
            p = jnp.exp(s - top)
            total = jnp.sum(p, 0, keepdims=True)
            logs[h : h + 1, here] = top + jnp.log(total)
            part = dot(values[:n, :], p.astype(BF), TN)
            part = jnp.transpose(part * (1.0 / total))
            out = jnp.where(mask, part, out)
        mixed[here, :] = out.astype(BF)
        for ref in kept:
            ref[here, :] = out.astype(BF)


def attend(query, keys, values, keep):
    return call(
        attend_kernel,
        [sds((LEN, INNER)), sds((8, LEN), F32)] + [hbm((LEN, INNER))] * keep,
        (),
        [VMEM] * 3,
        [VMEM] * (2 + keep),
        5,
    )(query, keys, values)


def attend_back_kernel(
    query, keys, values, dmixed, logs, cosine, sine, dqkv, sums, dkeys, dvalues
):
    dkeys[...] = jnp.zeros_like(dkeys)
    dvalues[...] = jnp.zeros_like(dvalues)
    count = jnp.zeros((1, INNER), F32)
    for i in range(LEN // BLOCK):
        n = (i + 1) * BLOCK
        here = pl.ds(i * BLOCK, BLOCK)
        q, do = query[here, :], dmixed[here, :]
        dq = jnp.zeros((BLOCK, INNER), F32)
        for h in range(HEADS):
            mask = head_mask(h, BLOCK)
            qh = jnp.where(mask, q, jnp.zeros_like(q))
            doh = jnp.where(mask, do, jnp.zeros_like(do))
            s = dot(keys[:n, :], qh, NT)
            p = jnp.exp(s - logs[h : h + 1, here])
            tail = jnp.where(causal(), p[n - BLOCK :], 0.0)
            p = jnp.concatenate([p[: n - BLOCK], tail], 0) if i else tail
            dp = dot(values[:n, :], doh, NT)
            w = p * dp
            delta = jnp.sum(w, 0, keepdims=True)
            ds = (w - p * delta).astype(BF)
            dvalues[:n, :] += dot(p.astype(BF), doh)
            dkeys[:n, :] += dot(ds, qh)
            dq = jnp.where(mask, jnp.transpose(dot(keys[:n, :], ds, TN)), dq)
        dq = turn(dq * 0.125, cosine[here, :], sine[here, :], -1.0).astype(BF)
        dqkv[here, :INNER] = dq
        count += jnp.sum(dq.astype(F32), 0, keepdims=True)
    sums[0:1, :INNER] = count
    dk = turn(dkeys[...], cosine[...], sine[...], -1.0).astype(BF)
    dv = dvalues[...].astype(BF)
    dqkv[:, INNER : 2 * INNER] = dk
    dqkv[:, 2 * INNER :] = dv
    sums[0:1, INNER : 2 * INNER] = jnp.sum(dk.astype(F32), 0, keepdims=True)
    sums[0:1, 2 * INNER :] = jnp.sum(dv.astype(F32), 0, keepdims=True)


def attend_back(query, keys, values, dmixed, logs, tables, after=()):
    return call(
        attend_back_kernel,
        [sds((LEN, QKV)), sds((8, QKV), F32)],
        (),
        [VMEM] * 7,
        [VMEM] * 2,
        6,
        scratch=[pltpu.VMEM((LEN, INNER), F32)] * 2,
        after=after,
    )(query, keys, values, dmixed, logs, *tables)


def merge_kernel(side, mixed, hidden, down, out):
    first = dot(mixed[...], down[:, :INNER], NT)
    out[...] = (first + dot(hidden[...], down[:, INNER:], NT)).astype(BF)


def half_block(width):
    return pl.BlockSpec((ROWS, width), lambda i, s: (s[0] * 2 + i, 0))


def merge(side, mixed, hidden, down, after=()):
    return call(
        merge_kernel,
        sds((LEN // 2, D)),
        (2,),
        [half_block(INNER), half_block(HID), whole(D, DOWN)],
        block(ROWS, D),
        2,
        scalars=1,
        after=after,
    )(side, mixed, hidden, down)


def spread_kernel(side, dqkv, dupper, wide, norms, out):
    first = dot(dqkv[...], wide[:, :QKV], NT) * norms[0:1]
    out[...] = (first + dot(dupper[...], wide[:, QKV:], NT) * norms[1:2]).astype(BF)


def spread(side, dqkv, dupper, wide, norms, after=()):
    return call(
        spread_kernel,
        sds((LEN // 2, D)),
        (2,),
        [half_block(QKV), half_block(HID), whole(D, WIDE), whole(8, D)],
        block(ROWS, D),
        2.2,
        scalars=1,
        after=after,
    )(side, dqkv, dupper, wide, norms)


def branch_first_kernel(order, *refs):
    pieces, refs = refs[:8], refs[8:]
    down, full, dmixed, dhidden, total, held, sems = refs
    step = pl.program_id(0)

    @pl.when(step == 0)
    def _():
        total[...] = jnp.zeros_like(total)
        for c in feature_copies(order, pieces, held, sems, 1):
            c.start()

    @pl.when(lax.rem(step, 2) == 0)
    def _():
        for j in range(4):
            part = held.at[pl.ds(0, 512), pl.ds(0, QUARTER)]
            pltpu.make_async_copy(part, part, sems.at[step * 2 + j]).wait()

    g = held[pl.ds(step * ROWS, ROWS), :]
    full[...] = g
    total[0:1] += jnp.sum(g.astype(F32), 0, keepdims=True)
    both = dot(g, down[...])
    dmixed[...] = both[:, :INNER].astype(BF)
    dhidden[...] = both[:, INNER:].astype(BF)


def branch_first(order, pieces, down):
    return call(
        branch_first_kernel,
        [hbm((LEN, D)), sds((LEN, INNER)), hbm((LEN, HID)), sds((8, D), F32)],
        (LEN // ROWS,),
        [ANY] * 8 + [whole(D, DOWN)],
        [block(ROWS, D), block(ROWS, INNER), block(ROWS, HID), whole(8, D)],
        4,
        scratch=[pltpu.VMEM((LEN, D), BF), pltpu.SemaphoreType.DMA((8,))],
        scalars=1,
    )(order, *pieces, down)


def branch_kernel(order, *refs):
    pieces, refs = refs[:8], refs[8:]
    down, slope, dmixed, dupper, sums, total, full, held, sems = refs
    step = pl.program_id(0)

    @pl.when(step == 0)
    def _():
        sums[...] = jnp.zeros_like(sums)
        total[...] = jnp.zeros_like(total)
        for c in token_copies(order, pieces, held, sems):
            c.start()

    for j in range(2):
        part = held.at[pl.ds(0, OWN)]
        pltpu.make_async_copy(pieces[0], part, sems.at[step * 2 + j]).wait()
    g = held[pl.ds(step * ROWS, ROWS), :]
    full[...] = g
    total[0:1] += jnp.sum(g.astype(F32), 0, keepdims=True)
    both = dot(g, down[...])
    dmixed[...] = both[:, :INNER].astype(BF)
    du = (both[:, INNER:] * slope[...].astype(F32)).astype(BF)
    dupper[...] = du
    sums[0:1] += jnp.sum(du.astype(F32), 0, keepdims=True)


def branch(order, pieces, down, slope, after=()):
    return call(
        branch_kernel,
        [
            sds((LEN, INNER)),
            sds((LEN, HID)),
            sds((8, HID), F32),
            sds((8, D), F32),
            sds((LEN, D)),
        ],
        (LEN // ROWS,),
        [ANY] * 8 + [whole(D, DOWN), block(ROWS, HID)],
        [block(ROWS, INNER), block(ROWS, HID), whole(8, HID), whole(8, D), block(ROWS, D)],
        4,
        scratch=[pltpu.VMEM((LEN, D), BF), pltpu.SemaphoreType.DMA((8,))],
        scalars=1,
        after=after,
    )(order, *pieces, down, slope)


def pack_kernel(has_wide, has_down, layer, *refs):
    refs, out = list(refs[:-1]), refs[-1]
    start = 0
    if has_wide:
        out[QUARTER:, :] = jnp.zeros_like(out[QUARTER:, :])
        triples, expand, scales, shifts, offsets, uplift, closing = refs[:7]
        refs = refs[7:]
        for i in range(3):
            at = slice(i * INNER, (i + 1) * INNER)
            out[:QUARTER, at] = triples[0, :, i, :]
            out[QUARTER : QUARTER + 1, at] = offsets[layer, i : i + 1, :]
        out[:QUARTER, QKV:WIDE] = expand[0]
        out[QUARTER : QUARTER + 1, QKV:WIDE] = uplift[layer : layer + 1, :]
        for i in range(2):
            at = slice(i * QUARTER, (i + 1) * QUARTER)
            out[QUARTER + 1 : QUARTER + 2, at] = scales[layer, i : i + 1, :]
            out[QUARTER + 2 : QUARTER + 3, at] = shifts[layer, i : i + 1, :]
        out[QUARTER + 3 : QUARTER + 4, :QUARTER] = closing[layer : layer + 1, :]
        start = WIDE
    if has_down:
        merger, shrink = refs
        out[:QUARTER, start : start + INNER] = merger[0].T
        out[:QUARTER, start + INNER :] = shrink[0].T


def of_layer(layer, array):
    shape = array.shape[1:]
    return pl.BlockSpec((1,) + shape, lambda i, *s: (layer,) + (0,) * len(shape))


def pack(layer, wide, down, after=()):
    specs = []
    if wide:
        specs += [of_layer(layer, a) for a in wide[:2]] + [whole(*a.shape) for a in wide[2:]]
    specs += [of_layer(layer, a) for a in down]
    width = (WIDE if wide else 0) + (DOWN if down else 0)
    rows = QUARTER + EXTRA if wide else QUARTER
    return call(
        partial(pack_kernel, bool(wide), bool(down), layer),
        hbm((rows, width)),
        (1,),
        specs,
        whole(rows, width),
        1,
        after=after,
    )(*wide, *down)


def pick_kernel(order, both, out, sems):
    copies = [
        pltpu.make_async_copy(both.at[2 * i + 1 - order[0]], out.at[i], sems.at[i])
        for i in range(2)
    ]
    for c in copies:
        c.start()
    for c in copies:
        c.wait()


def pick(order, both, after=()):
    return call(
        pick_kernel,
        sds((2,) + both.shape[1:]),
        (),
        [ANY],
        VMEM,
        1,
        scratch=[pltpu.SemaphoreType.DMA((2,))],
        scalars=1,
        after=after,
    )(order, both)


def halves(core, both, got, sems, places):
    copies = []
    for i in range(2):
        for j, (source, at) in enumerate(
            ((both.at[2 * i + core], 2 * i + core), (got.at[i], 2 * i + 1 - core))
        ):
            for n, (a, b) in enumerate(places(source, at)):
                copies.append(pltpu.make_async_copy(a, b, sems.at[2 * i + j, n]))
    for c in copies:
        c.start()
    for c in copies:
        c.wait()


def wide_places(wide, extra):
    def places(source, at):
        rows = pl.ds(at * QUARTER, QUARTER)
        return (
            (source.at[pl.ds(0, QUARTER), pl.ds(0, WIDE)], wide.at[rows]),
            (source.at[pl.ds(QUARTER, EXTRA), pl.ds(0, WIDE)], extra.at[at]),
        )

    return places


def down_places(down, start):
    def places(source, at):
        rows = pl.ds(at * QUARTER, QUARTER)
        return ((source.at[pl.ds(0, QUARTER), pl.ds(start, DOWN)], down.at[rows]),)

    return places


def vectors(extra, norms, bias):
    bias[...] = jnp.zeros_like(bias)
    norms[...] = jnp.zeros_like(norms)
    bias[0:1] = extra[0, 0:1].astype(F32)
    for q in range(4):
        cols = slice(q * QUARTER, (q + 1) * QUARTER)
        for n in range(5):
            row, at = 1 + n // 2, (n % 2) * QUARTER
            norms[n : n + 1, cols] = extra[q, row : row + 1, at : at + QUARTER].astype(F32)


def weights_kernel(order, both, got, wide, down, norms, bias, extra, sems):
    def places(source, at):
        return wide_places(wide, extra)(source, at) + down_places(down, WIDE)(source, at)

    halves(order[0], both, got, sems, places)
    vectors(extra, norms, bias)


def settle_weights(order, both, got):
    return call(
        weights_kernel,
        [sds((D, WIDE)), sds((D, DOWN)), sds((8, D), F32), hbm((8, WIDE), F32)],
        (),
        [ANY] * 2,
        [VMEM] * 4,
        2,
        scratch=[pltpu.VMEM((4, EXTRA, WIDE), BF), pltpu.SemaphoreType.DMA((4, 3))],
        scalars=1,
    )(order, both, got)


def keep_kernel(order, both, got, wide, down, mark, sems):
    mark[...] = jnp.zeros_like(mark)

    def places(source, at):
        rows = pl.ds(at * QUARTER, QUARTER)
        return (
            (source.at[pl.ds(0, QUARTER), pl.ds(0, WIDE)], wide.at[rows]),
        ) + down_places(down, WIDE)(source, at)

    halves(order[0], both, got, sems, places)


def keep_weights(order, both, got, after):
    return call(
        keep_kernel,
        [hbm((D, WIDE)), hbm((D, DOWN)), sds((8, 128), F32)],
        (),
        [ANY] * 2,
        [VMEM] * 3,
        2,
        scratch=[pltpu.SemaphoreType.DMA((4, 3))],
        scalars=1,
        after=after,
    )(order, both, got)


def gate_kernel(*refs):
    pass


def gate(arrays, after, shape=sds):
    return call(
        gate_kernel,
        [shape(a.shape, a.dtype) for a in arrays],
        (),
        [ANY] * len(arrays),
        [ANY] * len(arrays),
        0.1,
        aliases={i: i for i in range(len(arrays))},
        after=after,
    )(*(arrays if shape is sds else far(*arrays)))


def marked_gate_kernel(*refs):
    refs[-1][...] = jnp.zeros_like(refs[-1])


def marked_gate(arrays, after):
    *same, mark = call(
        marked_gate_kernel,
        [hbm(a.shape, a.dtype) for a in arrays] + [sds((8, 128), F32)],
        (),
        [ANY] * len(arrays),
        [ANY] * len(arrays) + [VMEM],
        0.1,
        aliases={i: i for i in range(len(arrays))},
        after=after,
    )(*far(*arrays))
    return same, mark


def combine_kernel(count, order, *refs):
    halves, (own, *sent), mark = refs[: 2 * count], refs[2 * count : -1], refs[-1]
    mark[...] = jnp.zeros_like(mark)
    for k, ref in zip(STEPS, [own] + sent):
        at = pl.ds(pl.multiple_of(lax.rem(order[0] + k, 4) * OWN, OWN), OWN)
        for part in range(count):
            mine, got = halves[2 * part : 2 * part + 2]
            total = mine[at, :].astype(F32) + got[at, :].astype(F32)
            ref[part * OWN : (part + 1) * OWN, :] = total.astype(ref.dtype)


def combine(order, halves, own=sds):
    count = len(halves) // 2
    rows = count * OWN
    return call(
        partial(combine_kernel, count),
        [own((rows, D), F32)] + [hbm((rows, D))] * 3 + [sds((8, 128), F32)],
        (),
        [VMEM] * len(halves),
        [VMEM] * 5,
        1.5,
        scalars=1,
    )(order, *halves)


def summed(own, others, rows):
    total = own[rows, :]
    for ref in others:
        total = total + ref[rows, :].astype(F32)
    return total


def back_through_norm(dxhat, x):
    xhat, r = normalized(x)
    mean = jnp.mean(dxhat, 1, keepdims=True)
    return r * (dxhat - mean - xhat * jnp.mean(dxhat * xhat, 1, keepdims=True))


EVERY = slice(0, OWN)


def finish_kernel(own, a, b, c, x, norms, new, xhat):
    value = x[...] + (summed(own, (a, b, c), EVERY) + norms[4:5])
    new[...] = value
    xhat[...] = normalized(value)[0].astype(BF)


def finish(parts, x, norms):
    return call(
        finish_kernel,
        [hbm((OWN, D), F32), hbm((OWN, D))],
        (),
        [VMEM] * 6,
        [VMEM] * 2,
        1.5,
    )(*parts, x, norms)


def finish_back_kernel(order, own, a, b, c, x, gradient, new, lowered, mark):
    mark[...] = jnp.zeros_like(mark)
    value = gradient[...].astype(F32) + back_through_norm(summed(own, (a, b, c), EVERY), x[...])
    new[...] = value
    lowered[...] = value.astype(BF)


def finish_back(order, parts, x, gradient):
    return call(
        finish_back_kernel,
        [hbm((OWN, D), F32), sds((OWN, D)), sds((8, 128), F32)],
        (1,),
        [whole(OWN, D)] * 5 + [pl.BlockSpec((OWN, D), lambda i, s: (s[0], 0))],
        [whole(OWN, D)] * 2 + [whole(8, 128)],
        1.5,
        scalars=1,
    )(order, *parts, x, gradient)


def finish_last_kernel(order, own, a, b, c, x_back, gradient, x_front, norms, *refs):
    outs, mark, held = refs[:4], refs[4], refs[5]
    mark[...] = jnp.zeros_like(mark)
    others = (a, b, c)
    held[EVERY, :] = gradient[...] + back_through_norm(summed(own, others, EVERY), x_back[...])
    held[OWN:, :] = x_front[...] + (summed(own, others, slice(OWN, 2 * OWN)) + norms[4:5])
    for k, ref in enumerate(outs):
        q = lax.rem(order[0] + k, 4)
        ref[...] = held[:, pl.ds(pl.multiple_of(q * QUARTER, QUARTER), QUARTER)].astype(BF)


def finish_last(order, parts, x_back, gradient, x_front, norms, after):
    return call(
        finish_last_kernel,
        [hbm((2 * OWN, QUARTER))] * 4 + [sds((8, 128), F32)],
        (),
        [VMEM] * 8,
        [VMEM] * 5,
        2,
        scratch=[pltpu.VMEM((2 * OWN, D), F32)],
        scalars=1,
        after=after,
    )(order, *parts, x_back, gradient, x_front, norms)


def land_kernel(order, *refs):
    pieces, (back, front, mark) = refs[:4], refs[4:]
    mark[...] = jnp.zeros_like(mark)
    for k, p in enumerate(pieces):
        at = pl.ds(pl.multiple_of(lax.rem(order[0] - k + 4, 4) * OWN, OWN), OWN)
        back[at, :] = p[:OWN, :].astype(F32)
        front[at, :] = p[OWN:, :]


def land(order, pieces):
    shape = (4 * OWN, QUARTER)
    return call(
        land_kernel,
        [sds(shape, F32), sds(shape), sds((8, 128), F32)],
        (),
        [VMEM] * 4,
        [VMEM] * 3,
        1,
        scalars=1,
    )(order, *pieces)


def payload_kernel(pairs, marks, *refs):
    out, mark = refs[-2:]
    mark[...] = jnp.zeros_like(mark)
    at, width = 0, 0
    out[QUARTER:, :] = jnp.zeros_like(out[QUARTER:, :])
    for rights in pairs:
        lhs = refs[at][...]
        at += 1
        for w in rights:
            out[:QUARTER, width : width + w] = dot(lhs, refs[at][...], TN).astype(BF)
            at += 1
            width += w
    for row, start, w in marks:
        out[QUARTER + row : QUARTER + row + 1, start : start + w] = refs[at][0:1, :].astype(BF)
        at += 1


def payload(pairs, extras, after=()):
    operands, specs, shape, width = [], [], [], 0
    for left, rights in pairs:
        operands.append(left)
        specs.append(pl.BlockSpec((LEN, QUARTER), lambda i: (0, i)))
        for r in rights:
            operands.append(r)
            specs.append(whole(*r.shape))
            width += r.shape[1]
        shape.append(tuple(r.shape[1] for r in rights))
    marks = []
    for row, start, vector, sliced in extras:
        operands.append(vector)
        w = QUARTER if sliced else vector.shape[1]
        specs.append(pl.BlockSpec((8, w), lambda i: (0, i)) if sliced else whole(8, w))
        marks.append((row, start, w))
    return call(
        partial(payload_kernel, tuple(shape), tuple(marks)),
        [hbm((4 * TALL, width)), sds((8, 128), F32)],
        (4,),
        specs,
        [block(TALL, width), whole(8, 128)],
        4 * (0.3 + width / 1536),
        after=after,
    )(*operands)


def share_kernel(order, part, mine, *sent):
    for k, ref in zip(STEPS, (mine,) + sent):
        at = pl.multiple_of(lax.rem(order[0] + k, 4) * SHARE, SHARE)
        ref[...] = part[:, pl.ds(at, SHARE)]


def share(order, part, after=()):
    return call(
        share_kernel,
        [sds((TALL, SHARE))] + [hbm((TALL, SHARE))] * 3,
        (),
        [VMEM],
        [VMEM] * 4,
        1.5,
        scalars=1,
        after=after,
    )(order, part)


def last_sum_kernel(own, a, b, c, out, mark):
    mark[...] = jnp.zeros_like(mark)
    total = own[...].astype(F32) + a[...].astype(F32) + b[...].astype(F32) + c[...].astype(F32)
    out[...] = total.astype(BF)


def last_sum(parts):
    return call(
        last_sum_kernel,
        [hbm((TALL, SHARE)), sds((8, 128), F32)],
        (),
        [VMEM] * 4,
        [VMEM] * 2,
        1,
    )(*parts)


def stats_kernel(a, b, c, d, scales, shifts):
    total = a[...] + b[...] + c[...] + d[...]
    for n, ref in enumerate((scales, shifts)):
        for l in range(LAYERS):
            ref[l] = total[4 * n + 2 * l : 4 * n + 2 * l + 2]


def stats_sum(parts):
    return call(
        stats_kernel,
        [sds((LAYERS, 2, QUARTER), F32)] * 2,
        (),
        [VMEM] * 4,
        [VMEM] * 2,
        1,
    )(*parts)


WIDTHS = {"triples": QKV, "expand": HID, "down": DOWN}
ROW = {"triples": 2, "expand": 0, "down": 1}


def final_kernel(layer, kinds, order, *refs):
    pieces, cols, refs = refs[:4], refs[4], refs[5:]
    shards_in = {}
    for kind in kinds:
        if kind != "down":
            shards_in[kind], refs = refs[0], refs[1:]
    if layer == 0:
        upper, refs = refs[0], refs[1 + sum(2 if k == "down" else 1 for k in kinds) :]
    held = refs[-1]
    for k, ref in zip(STEPS, pieces):
        at = pl.ds(pl.multiple_of(lax.rem(order[0] - k + 4, 4) * SHARE, SHARE), SHARE)
        held[:, at] = ref[...].astype(F32)
    start, lane = 0, lax.broadcasted_iota(jnp.int32, (QUARTER, 128), 1)
    stats = jnp.zeros((QUARTER, 128), F32)
    vectors, refs = refs[0], refs[1:]
    vectors[...] = jnp.zeros_like(vectors)
    for kind in kinds:
        w, row = WIDTHS[kind], ROW[kind]
        product = held[:QUARTER, start : start + w]
        if kind == "down":
            turned = jnp.transpose(product)
            refs[0][0] = turned[:INNER]
            refs[1][0] = turned[INNER:]
            refs = refs[2:]
            vectors[row : row + 1, :QUARTER] = held[QUARTER + row : QUARTER + row + 1, :QUARTER]
        else:
            sums = held[QUARTER + row : QUARTER + row + 1, start : start + w]
            vectors[row : row + 1, :w] = sums
            own = shards_in[kind]
            if kind == "triples":
                own = jnp.concatenate([own[0, :, i, :] for i in range(3)], 1)
            else:
                own = own[0]
            own = own.astype(F32)
            at = 0 if kind == "triples" else 1
            stats = jnp.where(lane == at, jnp.sum(own * product, 1, keepdims=True), stats)
            stats = jnp.where(lane == 2 + at, jnp.sum(own * sums, 1, keepdims=True), stats)
            value = cols[:, at : at + 1] * product + cols[:, 2 + at : 3 + at] * sums
            if kind == "triples":
                for i in range(3):
                    refs[0][0, :, i, :] = value[:, i * INNER : (i + 1) * INNER]
            else:
                refs[0][0] = value
            refs = refs[1:]
        start += w
    vectors[4:8, :QUARTER] = jnp.transpose(stats)[:4]
    if layer == 0:
        offsets, uplift, closing, joint_stats = refs[:4]
        for l, source in enumerate((vectors, upper)):
            for i in range(3):
                offsets[l, i : i + 1, :] = source[2:3, i * INNER : (i + 1) * INNER]
            uplift[l : l + 1] = source[0:1]
            closing[l : l + 1] = source[1:2, :QUARTER]
            for n in range(2):
                at = 4 * n + 2 * l
                joint_stats[at : at + 2] = source[4 + 2 * n : 6 + 2 * n, :QUARTER]


GRADS = {
    "triples": [(LAYERS, QUARTER, 3, INNER)],
    "expand": [(LAYERS, QUARTER, HID)],
    "down": [(LAYERS, INNER, QUARTER), (LAYERS, HID, QUARTER)],
}


def final(layer, kinds, order, pieces, cols, weights, stacks, upper=None):
    width = WIDE + DOWN
    operands = list(pieces) + [cols] + [weights[k] for k in kinds if k != "down"]
    if layer == 0:
        operands.append(upper)
    specs = [VMEM] * len(operands)
    shapes, outs, aliases = [sds((8, HID), F32)], [VMEM], {}
    for kind in kinds:
        for place, shape in enumerate(GRADS[kind]):
            if layer == 0:
                aliases[1 + len(operands)] = len(shapes)
                operands.append(stacks[kind][place])
                specs.append(ANY)
            shapes.append(sds(shape, F32))
            outs.append(
                pl.BlockSpec(
                    (1,) + shape[1:], lambda i, s, n=len(shape) - 1: (layer,) + (0,) * n
                )
            )
    outs[0] = whole(8, HID)
    if layer == 0:
        for shape in ((LAYERS, 3, INNER), (LAYERS, HID), (LAYERS, QUARTER), (8, QUARTER)):
            shapes.append(sds(shape, F32))
            outs.append(whole(*shape))
    fixed = [whole(*o.shape) if s is VMEM else s for o, s in zip(operands, specs)]
    for n, kind in enumerate(k for k in kinds if k != "down"):
        fixed[5 + n] = of_layer(layer, weights[kind])
    results = call(
        partial(final_kernel, layer, kinds),
        shapes,
        (1,),
        fixed,
        outs,
        2,
        scratch=[pltpu.VMEM((TALL, width), F32)],
        scalars=1,
        aliases=aliases,
    )(order, *operands)
    vectors, results = results[0], list(results[1:])
    grads = {}
    for kind in kinds:
        n = len(GRADS[kind])
        grads[kind], results = results[:n], results[n:]
    return (results if layer == 0 else vectors), grads


def across(array):
    return lax.ppermute(array, "core", [(0, 1), (1, 0)])


def around(array, axes, step):
    return lax.ppermute(array, axes, [(i, (i + step) % 4) for i in range(4)])


def exchanged(array, axes):
    return lax.ppermute(array, axes, [(0, 0), (1, 2), (2, 1), (3, 3)])


def gather_ring(own, axes):
    return [own] + [around(own, axes, k) for k in STEPS[1:]]


def gather_line(own, after=()):
    pieces = gather_ring(own, LINE)
    if after:
        pieces = pieces[:1] + list(gate(pieces[1:], after))
    return pieces + [across(p) for p in pieces]


def scatter_line(order, other, mine, early=(), own=sds):
    own, *sent, mark = combine(order, [mine, across(other), *early], own)
    return [own] + [around(s, LINE, k) for s, k in zip(sent, STEPS[1:])], mark


def outward_pairs(step):
    pairs = []
    for q in range(4):
        for zh in range(2):
            for core in range(2):
                z = (q - step) % 4
                pairs.append(((zh * 2 + core) * 4 + z, q * 4 + zh * 2 + core))
    return pairs


def outward(pieces):
    axes = ("yh", "core", "zh", "zl")
    return [lax.ppermute(p, axes, outward_pairs(k)) for k, p in enumerate(pieces)]


def tiny(array):
    return array[:16, :128]


def fetch(core, both, after):
    (both,) = far(both)
    got = across(pick(core, both, after))
    return settle_weights(core, both, got), got


def reduce_ring(array):
    return lax.psum_scatter(array, RING, scatter_dimension=0, tiled=True)


def crossed(step):
    return [
        ((x * 2 + core) * 2 + yl, ((x + step) % 4 * 2 + yl) * 2 + core)
        for x in range(4)
        for core in range(2)
        for yl in range(2)
    ]


def reduce_x(x, part, after=()):
    mine, *sent = share(x.reshape(1), far(part)[0], after)
    total, mark = last_sum([mine] + far(*[around(s, "x", k) for s, k in zip(sent, STEPS[1:])]))
    return far(*[lax.ppermute(total, ("x", "core", "yl"), crossed(k)) for k in STEPS]), mark


def shards(
    inputs, scales, shifts, triples, offsets, merger, expand, uplift, shrink, closing, cotangent
):
    core, y, z = lax.axis_index("core"), lax.axis_index(RING), lax.axis_index(LINE)
    x_at, q_at = lax.axis_index("x"), lax.axis_index(("yh", "core"))
    here, there = core.reshape(1), (1 - core).reshape(1)
    chunk = core * 4 + z
    sources = [(z - k + 4) % 4 for k in STEPS]
    tokens = jnp.stack([core * 4 + s for s in sources] + [(1 - core) * 4 + s for s in sources])
    blocks = [(s % 2) * 4 + (s // 2) * 2 for s in sources]
    features = jnp.stack([b + core for b in blocks] + [b + 1 - core for b in blocks] + [chunk])
    z_one, x_one, q_one = z.reshape(1), x_at.reshape(1), q_at.reshape(1)

    moved = exchanged(jnp.concatenate([inputs, cotangent], 0), ("yh", "zh"))
    marker = [tiny(moved)]
    wide_args = (triples, expand, scales, shifts, offsets, uplift, closing)
    down_args = (merger, shrink)
    packs = gate([pack(l, wide_args, down_args) for l in range(LAYERS)], marker)
    sent, sent1 = [lax.all_gather(p, RING, axis=0, tiled=False) for p in packs]
    pieces = gather_line(moved)
    first_pieces = pieces
    tables = rotary_tables()
    (wide, down, norms, bias), got = fetch(here, sent, [tiny(p) for p in pieces[1:4]])

    full0, slope0, query0, keys0, values0, hidden0, x0, *kept = project(
        True, features, far(*pieces), wide, norms, bias, tables
    )
    mixed0, logs0, mixed_kept = attend(query0, keys0, values0, 1)
    other = merge(there, mixed0, hidden0, down)
    mine = merge(here, mixed0, hidden0, down)
    query0, keys0, values0, hidden0, mixed0 = far(*kept, mixed_kept)
    parts, combined = scatter_line(z_one, other, mine)
    wide_kept, down_kept, kept_mark = keep_weights(here, *far(sent, got), [combined])
    late, arrived = marked_gate(parts[1:], [kept_mark])
    parts, marker = parts[:1] + late, [arrived]
    (wide1, down1, norms1, bias1), _ = fetch(here, sent1, marker)
    top, dmixed1, dhidden1, close_sum1 = branch_first(features, far(*first_pieces), down1)
    x1, xhat = finish(parts[:1] + far(*parts[1:]), x0, norms)
    pieces = gather_line(xhat, [close_sum1])

    full1, dupper1, query1, keys1, values1, hidden1, up_sum1 = project(
        False, tokens, far(pieces[0]) + pieces[1:], wide1, norms1, *far(bias1), tables, *far(dhidden1)
    )
    mixed1, logs1 = attend(query1, keys1, values1, 0)
    dqkv1, qkv_sum1 = attend_back(query1, keys1, values1, dmixed1, logs1, tables)
    other = spread(there, dqkv1, dupper1, wide1, norms1)
    mine = spread(here, dqkv1, dupper1, wide1, norms1)
    parts, combined = scatter_line(z_one, other, mine, own=hbm)
    grad1, done1 = payload(
        [(far(full1)[0], [dqkv1, dupper1]), (far(top)[0], [mixed1, hidden1])],
        [(2, 0, qkv_sum1, False), (0, QKV, up_sum1, False), (1, 0, close_sum1, True)],
        [combined],
    )
    late, arrived = marked_gate(parts[1:], [done1])
    gradient, lowered, mark = finish_back(
        chunk.reshape(1), far(parts[0], *late), *far(x1, top)
    )
    (grad1,) = gate([grad1], [arrived], hbm)
    grad1 = reduce_ring(grad1)

    other = merge(there, mixed1, hidden1, down1, [mark])
    mine = merge(here, mixed1, hidden1, down1, [mark])
    front = [mine, across(other)]
    pieces = gather_line(lowered, [tiny(mine)])

    dmixed0, dupper0, up_sum0, close_sum0, dy0 = branch(
        tokens, pieces, *far(down_kept, slope0)
    )
    dqkv0, qkv_sum0 = attend_back(query0, keys0, values0, dmixed0, logs0, far(*tables))
    grad0, done0 = payload(
        [(far(full0)[0], [dupper0]), (dy0, [mixed0, hidden0]), (far(full0)[0], [dqkv0])],
        [(0, 0, up_sum0, False), (1, 0, close_sum0, True), (2, HID + DOWN, qkv_sum0, False)],
    )
    grad0 = reduce_ring(grad0)

    reduced1, summed1 = reduce_x(x_at, grad1, [tiny(dqkv0)])
    rest = (dqkv0, dupper0, far(wide_kept)[0], norms, [done0])
    other = spread(there, *rest)
    mine = spread(here, *rest)
    parts, _ = scatter_line(z_one, other, mine, front)
    *pieces, finished = finish_last(
        z_one, parts[:1] + far(*parts[1:]), *far(x0, gradient, x1), norms1, [summed1])
    inputs_grad, outputs, landed = land(q_one, far(*outward(pieces)))
    cols = [
        jnp.concatenate([scales[l], shifts[l]], 0).astype(F32).T for l in range(LAYERS)
    ]
    weights = {"triples": triples, "expand": expand}
    upper, stacks = final(
        1, ("triples", "expand", "down"), x_one, reduced1, cols[1], weights, None
    )
    reduced, _ = reduce_x(x_at, grad0, [finished])
    (offsets_grad, uplift_grad, closing_grad, stats), stacks = final(
        0, ("expand", "down", "triples"), x_one, reduced, cols[0], weights, stacks, upper
    )
    stats = stats + lax.ppermute(stats, "yl", [(0, 1), (1, 0)])
    scales_grad, shifts_grad = stats_sum(gather_ring(stats, LINE))
    return (
        outputs,
        inputs_grad,
        scales_grad,
        shifts_grad,
        stacks["triples"][0],
        offsets_grad,
        stacks["down"][0],
        stacks["expand"][0],
        uplift_grad,
        stacks["down"][1],
        closing_grad,
    )


def solution(mesh):
    grid = Mesh(mesh.devices.reshape(4, 2, 2, 2, 2, 2), AXES)
    row, col = ("yh", "core"), ("yl", "zh", "zl")
    tokens = P(("x",) + col, row)
    weights = (
        P(None, None, row),
        P(None, None, row),
        P(None, row, None, col),
        P(None, None, col),
        P(None, col, row),
        P(None, row, col),
        P(None, col),
        P(None, col, row),
        P(None, row),
    )
    return jax.shard_map(
        shards,
        mesh=grid,
        in_specs=(tokens,) + weights + (tokens,),
        out_specs=(tokens, tokens) + weights,
        check_vma=False,
    )
```

```python
from functools import partial

import jax
import jax.numpy as jnp
import numpy as np
from jax import lax
from jax.experimental import pallas as pl
from jax.experimental.pallas import tpu as pltpu
from jax.sharding import Mesh
from jax.sharding import PartitionSpec as P

D = 1024
QUARTER = D // 4
HEAD = 64
ROT = 16
LAYERS = 2
LEN = 1024
OWN = LEN // 8
HEADS = 2
INNER = HEADS * HEAD
QKV = 3 * INNER
HID = 512
WIDE = QKV + HID
DOWN = INNER + HID
EXTRA = 16
TALL = QUARTER + EXTRA
SHARE = (WIDE + DOWN) // 4
NORM_EPSILON = 1e-05
BF = jnp.bfloat16
F32 = jnp.float32
NN = (((1,), (0,)), ((), ()))
NT = (((1,), (1,)), ((), ()))
TN = (((0,), (0,)), ((), ()))
AXES = ("x", "yh", "core", "yl", "zh", "zl")
LINE = ("zh", "zl")
RING = ("yh", "yl")
STEPS = (0, 1, 3, 2)
ANY = pl.BlockSpec(memory_space=pl.ANY)
HBM = pltpu.MemorySpace.HBM
VMEM = pl.BlockSpec(memory_space=pltpu.VMEM)


def dot(a, b, dims=NN):
    return lax.dot_general(a, b, dims, preferred_element_type=F32)


def sds(shape, dtype=BF):
    return jax.ShapeDtypeStruct(shape, dtype)


def hbm(shape, dtype=BF):
    return HBM(shape, dtype)


def call(
    kernel, out_shape, grid, in_specs, out_specs, micros, scratch=(), scalars=0, aliases={}, after=()
):
    count, extra = scalars + len(in_specs), len(after)

    def body(*refs):
        kernel(*refs[:count], *refs[count + extra :])

    run = pl.pallas_call(
        body,
        out_shape=out_shape,
        grid_spec=pltpu.PrefetchScalarGridSpec(
            num_scalar_prefetch=scalars,
            grid=grid,
            in_specs=list(in_specs) + [ANY] * extra,
            out_specs=out_specs,
            scratch_shapes=scratch,
        ),
        input_output_aliases=aliases,
        compiler_params=pltpu.CompilerParams(vmem_limit_bytes=12 * 2**20),
        cost_estimate=pl.CostEstimate(
            flops=int(micros * 1e6), bytes_accessed=1024, transcendentals=0
        ),
    )
    return lambda *operands: run(*operands, *after)


def far(*arrays):
    return [pltpu.with_memory_space_constraint(a, HBM) for a in arrays]


def block(rows, width):
    return pl.BlockSpec((rows, width), lambda i, *s: (i, 0))


def whole(*shape):
    return pl.BlockSpec(shape, lambda i, *s: (0,) * len(shape))


def rotary_tables():
    lane = jnp.arange(INNER) % (ROT // 2)
    inverse = 10000.0 ** (-(2 * lane).astype(F32) / ROT)
    angles = jnp.arange(LEN).astype(F32)[:, None] * inverse[None, :]
    return lax.optimization_barrier((jnp.cos(angles), jnp.sin(angles)))


def turn(u, cosine, sine, sign):
    half = ROT // 2
    lane = lax.broadcasted_iota(jnp.int32, u.shape, 1) % HEAD
    back = pltpu.roll(u, INNER - half, 1)
    ahead = pltpu.roll(u, half, 1)
    turned = jnp.where(lane < half, -back, ahead)
    return jnp.where(lane < ROT, u * cosine + sign * (turned * sine), u)


def normalized(x):
    mean = jnp.mean(x, 1, keepdims=True)
    r = lax.rsqrt(jnp.mean(x * x, 1, keepdims=True) - mean * mean + NORM_EPSILON)
    return (x - mean) * r, r


def token_copies(order, pieces, held, sems):
    return [
        pltpu.make_async_copy(p, held.at[pl.ds(order[j] * OWN, OWN)], sems.at[order[j]])
        for j, p in enumerate(pieces)
    ]


def feature_copies(order, pieces, held, sems, part=0):
    return [
        pltpu.make_async_copy(
            p.at[pl.ds(part * 512, 512)],
            held.at[
                pl.ds((order[j] // 4) * 512, 512), pl.ds(lax.rem(order[j], 4) * QUARTER, QUARTER)
            ],
            sems.at[order[j]],
        )
        for j, p in enumerate(pieces)
    ]


ROWS = 256


def project_kernel(first, last, order, *refs):
    pieces, refs = refs[:8], refs[8:]
    wide, norms, bias, cosine, sine, *refs = refs
    if last:
        down_grad, *refs = refs
    full, slope, query, keys, values, hidden, *rest = refs
    held, sems = refs[-2:]
    step = pl.program_id(0)

    @pl.when(step == 0)
    def _():
        copies = (feature_copies if first else token_copies)(order, pieces, held, sems)
        for c in copies:
            c.start()

    if first:

        @pl.when(lax.rem(step, 2) == 0)
        def _():
            for j in range(4):
                part = held.at[pl.ds(0, 512), pl.ds(0, QUARTER)]
                pltpu.make_async_copy(part, part, sems.at[step * 2 + j]).wait()

        @pl.when(step == order[8] // 2)
        def _():
            rest[0][...] = held[pl.ds(order[8] * OWN, OWN), :].astype(F32)
    else:
        for j in range(2):
            part = held.at[pl.ds(0, OWN)]
            pltpu.make_async_copy(pieces[0], part, sems.at[step * 2 + j]).wait()
    rows = held[pl.ds(step * ROWS, ROWS), :]
    xh = rows.astype(F32)
    if first:
        xh, _ = normalized(xh)
        rows = xh.astype(BF)
        xh = rows.astype(F32)
    full[...] = rows
    n_a = (xh * norms[0:1] + norms[2:3]).astype(BF)
    n_f = (xh * norms[1:2] + norms[3:4]).astype(BF)
    qkv = dot(n_a, wide[:, :QKV]) + bias[0:1, :QKV]
    table = (cosine[...], sine[...])
    query[...] = (turn(qkv[:, :INNER], *table, 1.0).astype(BF) * 0.125).astype(BF)
    keys[...] = turn(qkv[:, INNER : 2 * INNER], *table, 1.0).astype(BF)
    values[...] = qkv[:, 2 * INNER :].astype(BF)
    u = dot(n_f, wide[:, QKV:]) + bias[0:1, QKV:]
    cdf = 0.5 + 0.5 * lax.erf(u * (0.5**0.5))
    hidden[...] = (u * cdf).astype(BF)
    if first:
        for now, later in zip((query, keys, values, hidden), rest[1:5]):
            later[...] = now[...]
    steep = cdf + u * (jnp.exp(u * u * -0.5) * (1.0 / (2.0 * np.pi) ** 0.5))
    if last:
        du = (down_grad[...].astype(F32) * steep).astype(BF)
        slope[...] = du

        @pl.when(step == 0)
        def _():
            rest[0][...] = jnp.zeros_like(rest[0])

        rest[0][0:1] += jnp.sum(du.astype(F32), 0, keepdims=True)
    else:
        slope[...] = steep.astype(BF)


def project(first, order, pieces, wide, norms, bias, tables, down_grad=None):
    heads = [block(ROWS, INNER)] * 3 + [block(ROWS, HID)]
    shapes = [hbm((LEN, D)), hbm((LEN, HID)) if first else sds((LEN, HID))]
    shapes += [sds((LEN, INNER))] * 3 + [sds((LEN, HID))]
    outs = [block(ROWS, D), block(ROWS, HID)] + heads
    if first:
        shapes += [hbm((OWN, D), F32)] + [hbm((LEN, INNER))] * 3 + [hbm((LEN, HID))]
        outs += [whole(OWN, D)] + heads
    given = []
    if down_grad is not None:
        shapes.append(sds((8, HID), F32))
        outs.append(whole(8, HID))
        given = [down_grad]
    return call(
        partial(project_kernel, first, down_grad is not None),
        shapes,
        (LEN // ROWS,),
        [ANY] * 8
        + [whole(D, WIDE), whole(8, D), whole(8, WIDE)]
        + [block(ROWS, INNER)] * 2
        + [block(ROWS, HID)] * len(given),
        outs,
        7,
        scratch=[pltpu.VMEM((LEN, D), BF), pltpu.SemaphoreType.DMA((8,))],
        scalars=1,
    )(order, *pieces, wide, norms, bias, *tables, *given)


BLOCK = 256


def head_mask(h, rows):
    lane = lax.broadcasted_iota(jnp.int32, (rows, INNER), 1)
    return (lane // HEAD) == h


def causal():
    key = lax.broadcasted_iota(jnp.int32, (BLOCK, BLOCK), 0)
    query = lax.broadcasted_iota(jnp.int32, (BLOCK, BLOCK), 1)
    return key <= query


def attend_kernel(query, keys, values, mixed, logs, *kept):
    for i in range(LEN // BLOCK):
        n = (i + 1) * BLOCK
        here = pl.ds(i * BLOCK, BLOCK)
        q = query[here, :]
        out = jnp.zeros((BLOCK, INNER), F32)
        for h in range(HEADS):
            mask = head_mask(h, BLOCK)
            qh = jnp.where(mask, q, jnp.zeros_like(q))
            s = dot(keys[:n, :], qh, NT)
            tail = jnp.where(causal(), s[n - BLOCK :], -1e30)
            s = jnp.concatenate([s[: n - BLOCK], tail], 0) if i else tail
            top = jnp.max(s, 0, keepdims=True)
            p = jnp.exp(s - top)
            total = jnp.sum(p, 0, keepdims=True)
            logs[h : h + 1, here] = top + jnp.log(total)
            part = dot(values[:n, :], p.astype(BF), TN)
            part = jnp.transpose(part * (1.0 / total))
            out = jnp.where(mask, part, out)
        mixed[here, :] = out.astype(BF)
        for ref in kept:
            ref[here, :] = out.astype(BF)


def attend(query, keys, values, keep):
    return call(
        attend_kernel,
        [sds((LEN, INNER)), sds((8, LEN), F32)] + [hbm((LEN, INNER))] * keep,
        (),
        [VMEM] * 3,
        [VMEM] * (2 + keep),
        5,
    )(query, keys, values)


def attend_back_kernel(
    query, keys, values, dmixed, logs, cosine, sine, dqkv, sums, dkeys, dvalues
):
    dkeys[...] = jnp.zeros_like(dkeys)
    dvalues[...] = jnp.zeros_like(dvalues)
    count = jnp.zeros((1, INNER), F32)
    for i in range(LEN // BLOCK):
        n = (i + 1) * BLOCK
        here = pl.ds(i * BLOCK, BLOCK)
        q, do = query[here, :], dmixed[here, :]
        dq = jnp.zeros((BLOCK, INNER), F32)
        for h in range(HEADS):
            mask = head_mask(h, BLOCK)
            qh = jnp.where(mask, q, jnp.zeros_like(q))
            doh = jnp.where(mask, do, jnp.zeros_like(do))
            s = dot(keys[:n, :], qh, NT)
            p = jnp.exp(s - logs[h : h + 1, here])
            tail = jnp.where(causal(), p[n - BLOCK :], 0.0)
            p = jnp.concatenate([p[: n - BLOCK], tail], 0) if i else tail
            dp = dot(values[:n, :], doh, NT)
            w = p * dp
            delta = jnp.sum(w, 0, keepdims=True)
            ds = (w - p * delta).astype(BF)
            dvalues[:n, :] += dot(p.astype(BF), doh)
            dkeys[:n, :] += dot(ds, qh)
            dq = jnp.where(mask, jnp.transpose(dot(keys[:n, :], ds, TN)), dq)
        dq = turn(dq * 0.125, cosine[here, :], sine[here, :], -1.0).astype(BF)
        dqkv[here, :INNER] = dq
        count += jnp.sum(dq.astype(F32), 0, keepdims=True)
    sums[0:1, :INNER] = count
    dk = turn(dkeys[...], cosine[...], sine[...], -1.0).astype(BF)
    dv = dvalues[...].astype(BF)
    dqkv[:, INNER : 2 * INNER] = dk
    dqkv[:, 2 * INNER :] = dv
    sums[0:1, INNER : 2 * INNER] = jnp.sum(dk.astype(F32), 0, keepdims=True)
    sums[0:1, 2 * INNER :] = jnp.sum(dv.astype(F32), 0, keepdims=True)


def attend_back(query, keys, values, dmixed, logs, tables, after=()):
    return call(
        attend_back_kernel,
        [sds((LEN, QKV)), sds((8, QKV), F32)],
        (),
        [VMEM] * 7,
        [VMEM] * 2,
        6,
        scratch=[pltpu.VMEM((LEN, INNER), F32)] * 2,
        after=after,
    )(query, keys, values, dmixed, logs, *tables)


def merge_kernel(side, mixed, hidden, down, out):
    first = dot(mixed[...], down[:, :INNER], NT)
    out[...] = (first + dot(hidden[...], down[:, INNER:], NT)).astype(BF)


def half_block(width):
    return pl.BlockSpec((ROWS, width), lambda i, s: (s[0] * 2 + i, 0))


def merge(side, mixed, hidden, down, after=()):
    return call(
        merge_kernel,
        sds((LEN // 2, D)),
        (2,),
        [half_block(INNER), half_block(HID), whole(D, DOWN)],
        block(ROWS, D),
        2,
        scalars=1,
        after=after,
    )(side, mixed, hidden, down)


def spread_kernel(side, dqkv, dupper, wide, norms, out):
    first = dot(dqkv[...], wide[:, :QKV], NT) * norms[0:1]
    out[...] = (first + dot(dupper[...], wide[:, QKV:], NT) * norms[1:2]).astype(BF)


def spread(side, dqkv, dupper, wide, norms, after=()):
    return call(
        spread_kernel,
        sds((LEN // 2, D)),
        (2,),
        [half_block(QKV), half_block(HID), whole(D, WIDE), whole(8, D)],
        block(ROWS, D),
        2.2,
        scalars=1,
        after=after,
    )(side, dqkv, dupper, wide, norms)


def branch_first_kernel(order, *refs):
    pieces, refs = refs[:8], refs[8:]
    down, full, dmixed, dhidden, total, held, sems = refs
    step = pl.program_id(0)

    @pl.when(step == 0)
    def _():
        total[...] = jnp.zeros_like(total)
        for c in feature_copies(order, pieces, held, sems, 1):
            c.start()

    @pl.when(lax.rem(step, 2) == 0)
    def _():
        for j in range(4):
            part = held.at[pl.ds(0, 512), pl.ds(0, QUARTER)]
            pltpu.make_async_copy(part, part, sems.at[step * 2 + j]).wait()

    g = held[pl.ds(step * ROWS, ROWS), :]
    full[...] = g
    total[0:1] += jnp.sum(g.astype(F32), 0, keepdims=True)
    both = dot(g, down[...])
    dmixed[...] = both[:, :INNER].astype(BF)
    dhidden[...] = both[:, INNER:].astype(BF)


def branch_first(order, pieces, down):
    return call(
        branch_first_kernel,
        [hbm((LEN, D)), sds((LEN, INNER)), hbm((LEN, HID)), sds((8, D), F32)],
        (LEN // ROWS,),
        [ANY] * 8 + [whole(D, DOWN)],
        [block(ROWS, D), block(ROWS, INNER), block(ROWS, HID), whole(8, D)],
        4,
        scratch=[pltpu.VMEM((LEN, D), BF), pltpu.SemaphoreType.DMA((8,))],
        scalars=1,
    )(order, *pieces, down)


def branch_kernel(order, *refs):
    pieces, refs = refs[:8], refs[8:]
    down, slope, dmixed, dupper, sums, total, full, held, sems = refs
    step = pl.program_id(0)

    @pl.when(step == 0)
    def _():
        sums[...] = jnp.zeros_like(sums)
        total[...] = jnp.zeros_like(total)
        for c in token_copies(order, pieces, held, sems):
            c.start()

    for j in range(2):
        part = held.at[pl.ds(0, OWN)]
        pltpu.make_async_copy(pieces[0], part, sems.at[step * 2 + j]).wait()
    g = held[pl.ds(step * ROWS, ROWS), :]
    full[...] = g
    total[0:1] += jnp.sum(g.astype(F32), 0, keepdims=True)
    both = dot(g, down[...])
    dmixed[...] = both[:, :INNER].astype(BF)
    du = (both[:, INNER:] * slope[...].astype(F32)).astype(BF)
    dupper[...] = du
    sums[0:1] += jnp.sum(du.astype(F32), 0, keepdims=True)


def branch(order, pieces, down, slope, after=()):
    return call(
        branch_kernel,
        [
            sds((LEN, INNER)),
            sds((LEN, HID)),
            sds((8, HID), F32),
            sds((8, D), F32),
            sds((LEN, D)),
        ],
        (LEN // ROWS,),
        [ANY] * 8 + [whole(D, DOWN), block(ROWS, HID)],
        [block(ROWS, INNER), block(ROWS, HID), whole(8, HID), whole(8, D), block(ROWS, D)],
        4,
        scratch=[pltpu.VMEM((LEN, D), BF), pltpu.SemaphoreType.DMA((8,))],
        scalars=1,
        after=after,
    )(order, *pieces, down, slope)


def pack_kernel(has_wide, has_down, layer, *refs):
    refs, out = list(refs[:-1]), refs[-1]
    start = 0
    if has_wide:
        out[QUARTER:, :] = jnp.zeros_like(out[QUARTER:, :])
        triples, expand, scales, shifts, offsets, uplift, closing = refs[:7]
        refs = refs[7:]
        for i in range(3):
            at = slice(i * INNER, (i + 1) * INNER)
            out[:QUARTER, at] = triples[0, i]
            out[QUARTER : QUARTER + 1, at] = offsets[i, layer : layer + 1, :]
        out[:QUARTER, QKV:WIDE] = expand[0]
        out[QUARTER : QUARTER + 1, QKV:WIDE] = uplift[layer : layer + 1, :]
        for i in range(2):
            at = slice(i * QUARTER, (i + 1) * QUARTER)
            out[QUARTER + 1 : QUARTER + 2, at] = scales[layer, i : i + 1, :]
            out[QUARTER + 2 : QUARTER + 3, at] = shifts[layer, i : i + 1, :]
        out[QUARTER + 3 : QUARTER + 4, :QUARTER] = closing[layer : layer + 1, :]
        start = WIDE
    if has_down:
        merger, shrink = refs
        out[:QUARTER, start : start + INNER] = merger[0].T
        out[:QUARTER, start + INNER :] = shrink[0].T


def of_layer(layer, array):
    shape = array.shape[1:]
    return pl.BlockSpec((1,) + shape, lambda i, *s: (layer,) + (0,) * len(shape))


def pack(layer, wide, down, after=()):
    specs = []
    if wide:
        specs += [of_layer(layer, a) for a in wide[:2]] + [whole(*a.shape) for a in wide[2:]]
    specs += [of_layer(layer, a) for a in down]
    width = (WIDE if wide else 0) + (DOWN if down else 0)
    rows = QUARTER + EXTRA if wide else QUARTER
    return call(
        partial(pack_kernel, bool(wide), bool(down), layer),
        hbm((rows, width)),
        (1,),
        specs,
        whole(rows, width),
        1,
        after=after,
    )(*far(*wide), *far(*down))


def pick_kernel(order, both, out, sems):
    copies = [
        pltpu.make_async_copy(both.at[2 * i + 1 - order[0]], out.at[i], sems.at[i])
        for i in range(2)
    ]
    for c in copies:
        c.start()
    for c in copies:
        c.wait()


def pick(order, both, after=()):
    return call(
        pick_kernel,
        sds((2,) + both.shape[1:]),
        (),
        [ANY],
        VMEM,
        1,
        scratch=[pltpu.SemaphoreType.DMA((2,))],
        scalars=1,
        after=after,
    )(order, both)


def halves(core, both, got, sems, places):
    copies = []
    for i in range(2):
        for j, (source, at) in enumerate(
            ((both.at[2 * i + core], 2 * i + core), (got.at[i], 2 * i + 1 - core))
        ):
            for n, (a, b) in enumerate(places(source, at)):
                copies.append(pltpu.make_async_copy(a, b, sems.at[2 * i + j, n]))
    for c in copies:
        c.start()
    for c in copies:
        c.wait()


def wide_places(wide, extra):
    def places(source, at):
        rows = pl.ds(at * QUARTER, QUARTER)
        return (
            (source.at[pl.ds(0, QUARTER), pl.ds(0, WIDE)], wide.at[rows]),
            (source.at[pl.ds(QUARTER, EXTRA), pl.ds(0, WIDE)], extra.at[at]),
        )

    return places


def down_places(down, start):
    def places(source, at):
        rows = pl.ds(at * QUARTER, QUARTER)
        return ((source.at[pl.ds(0, QUARTER), pl.ds(start, DOWN)], down.at[rows]),)

    return places


def vectors(extra, norms, bias):
    bias[...] = jnp.zeros_like(bias)
    norms[...] = jnp.zeros_like(norms)
    bias[0:1] = extra[0, 0:1].astype(F32)
    for q in range(4):
        cols = slice(q * QUARTER, (q + 1) * QUARTER)
        for n in range(5):
            row, at = 1 + n // 2, (n % 2) * QUARTER
            norms[n : n + 1, cols] = extra[q, row : row + 1, at : at + QUARTER].astype(F32)


def weights_kernel(order, both, got, wide, down, norms, bias, extra, sems):
    def places(source, at):
        return wide_places(wide, extra)(source, at) + down_places(down, WIDE)(source, at)

    halves(order[0], both, got, sems, places)
    vectors(extra, norms, bias)


def settle_weights(order, both, got):
    return call(
        weights_kernel,
        [sds((D, WIDE)), sds((D, DOWN)), sds((8, D), F32), hbm((8, WIDE), F32)],
        (),
        [ANY] * 2,
        [VMEM] * 4,
        2,
        scratch=[pltpu.VMEM((4, EXTRA, WIDE), BF), pltpu.SemaphoreType.DMA((4, 3))],
        scalars=1,
    )(order, both, got)


def keep_kernel(order, both, got, wide, down, mark, sems):
    mark[...] = jnp.zeros_like(mark)

    def places(source, at):
        rows = pl.ds(at * QUARTER, QUARTER)
        return (
            (source.at[pl.ds(0, QUARTER), pl.ds(0, WIDE)], wide.at[rows]),
        ) + down_places(down, WIDE)(source, at)

    halves(order[0], both, got, sems, places)


def keep_weights(order, both, got, after):
    return call(
        keep_kernel,
        [hbm((D, WIDE)), hbm((D, DOWN)), sds((8, 128), F32)],
        (),
        [ANY] * 2,
        [VMEM] * 3,
        2,
        scratch=[pltpu.SemaphoreType.DMA((4, 3))],
        scalars=1,
        after=after,
    )(order, both, got)


def gate_kernel(*refs):
    pass


def gate(arrays, after, shape=sds):
    return call(
        gate_kernel,
        [shape(a.shape, a.dtype) for a in arrays],
        (),
        [ANY] * len(arrays),
        [ANY] * len(arrays),
        0.1,
        aliases={i: i for i in range(len(arrays))},
        after=after,
    )(*(arrays if shape is sds else far(*arrays)))


def marked_gate_kernel(*refs):
    refs[-1][...] = jnp.zeros_like(refs[-1])


def marked_gate(arrays, after):
    *same, mark = call(
        marked_gate_kernel,
        [hbm(a.shape, a.dtype) for a in arrays] + [sds((8, 128), F32)],
        (),
        [ANY] * len(arrays),
        [ANY] * len(arrays) + [VMEM],
        0.1,
        aliases={i: i for i in range(len(arrays))},
        after=after,
    )(*far(*arrays))
    return same, mark


def combine_kernel(count, order, *refs):
    halves, (own, *sent), mark = refs[: 2 * count], refs[2 * count : -1], refs[-1]
    mark[...] = jnp.zeros_like(mark)
    for k, ref in zip(STEPS, [own] + sent):
        at = pl.ds(pl.multiple_of(lax.rem(order[0] + k, 4) * OWN, OWN), OWN)
        for part in range(count):
            mine, got = halves[2 * part : 2 * part + 2]
            total = mine[at, :].astype(F32) + got[at, :].astype(F32)
            ref[part * OWN : (part + 1) * OWN, :] = total.astype(ref.dtype)


def combine(order, halves, own=sds):
    count = len(halves) // 2
    rows = count * OWN
    return call(
        partial(combine_kernel, count),
        [own((rows, D), F32)] + [hbm((rows, D))] * 3 + [sds((8, 128), F32)],
        (),
        [VMEM] * len(halves),
        [VMEM] * 5,
        1.5,
        scalars=1,
    )(order, *halves)


def summed(own, others, rows):
    total = own[rows, :]
    for ref in others:
        total = total + ref[rows, :].astype(F32)
    return total


def back_through_norm(dxhat, x):
    xhat, r = normalized(x)
    mean = jnp.mean(dxhat, 1, keepdims=True)
    return r * (dxhat - mean - xhat * jnp.mean(dxhat * xhat, 1, keepdims=True))


EVERY = slice(0, OWN)


def finish_kernel(own, a, b, c, x, norms, new, xhat):
    value = x[...] + (summed(own, (a, b, c), EVERY) + norms[4:5])
    new[...] = value
    xhat[...] = normalized(value)[0].astype(BF)


def finish(parts, x, norms):
    return call(
        finish_kernel,
        [hbm((OWN, D), F32), hbm((OWN, D))],
        (),
        [VMEM] * 6,
        [VMEM] * 2,
        1.5,
    )(*parts, x, norms)


def finish_back_kernel(order, own, a, b, c, x, gradient, new, lowered, mark):
    mark[...] = jnp.zeros_like(mark)
    value = gradient[...].astype(F32) + back_through_norm(summed(own, (a, b, c), EVERY), x[...])
    new[...] = value
    lowered[...] = value.astype(BF)


def finish_back(order, parts, x, gradient):
    return call(
        finish_back_kernel,
        [hbm((OWN, D), F32), sds((OWN, D)), sds((8, 128), F32)],
        (1,),
        [whole(OWN, D)] * 5 + [pl.BlockSpec((OWN, D), lambda i, s: (s[0], 0))],
        [whole(OWN, D)] * 2 + [whole(8, 128)],
        1.5,
        scalars=1,
    )(order, *parts, x, gradient)


def finish_last_kernel(order, own, a, b, c, x_back, gradient, x_front, norms, *refs):
    outs, mark, held = refs[:4], refs[4], refs[5]
    mark[...] = jnp.zeros_like(mark)
    others = (a, b, c)
    held[EVERY, :] = gradient[...] + back_through_norm(summed(own, others, EVERY), x_back[...])
    held[OWN:, :] = x_front[...] + (summed(own, others, slice(OWN, 2 * OWN)) + norms[4:5])
    for k, ref in enumerate(outs):
        q = lax.rem(order[0] + k, 4)
        ref[...] = held[:, pl.ds(pl.multiple_of(q * QUARTER, QUARTER), QUARTER)].astype(BF)


def finish_last(order, parts, x_back, gradient, x_front, norms, after):
    return call(
        finish_last_kernel,
        [hbm((2 * OWN, QUARTER))] * 4 + [sds((8, 128), F32)],
        (),
        [VMEM] * 8,
        [VMEM] * 5,
        2,
        scratch=[pltpu.VMEM((2 * OWN, D), F32)],
        scalars=1,
        after=after,
    )(order, *parts, x_back, gradient, x_front, norms)


def land_kernel(order, *refs):
    pieces, (back, front, mark) = refs[:4], refs[4:]
    mark[...] = jnp.zeros_like(mark)
    for k, p in enumerate(pieces):
        at = pl.ds(pl.multiple_of(lax.rem(order[0] - k + 4, 4) * OWN, OWN), OWN)
        back[at, :] = p[:OWN, :].astype(F32)
        front[at, :] = p[OWN:, :]


def land(order, pieces):
    shape = (4 * OWN, QUARTER)
    return call(
        land_kernel,
        [sds(shape, F32), sds(shape), sds((8, 128), F32)],
        (),
        [VMEM] * 4,
        [VMEM] * 3,
        1,
        scalars=1,
    )(order, *pieces)


def payload_kernel(pairs, marks, *refs):
    out, mark = refs[-2:]
    mark[...] = jnp.zeros_like(mark)
    at, width = 0, 0
    out[QUARTER:, :] = jnp.zeros_like(out[QUARTER:, :])
    for rights in pairs:
        lhs = refs[at][...]
        at += 1
        for w in rights:
            out[:QUARTER, width : width + w] = dot(lhs, refs[at][...], TN).astype(BF)
            at += 1
            width += w
    for row, start, w in marks:
        out[QUARTER + row : QUARTER + row + 1, start : start + w] = refs[at][0:1, :].astype(BF)
        at += 1


def payload(pairs, extras, after=()):
    operands, specs, shape, width = [], [], [], 0
    for left, rights in pairs:
        operands.append(left)
        specs.append(pl.BlockSpec((LEN, QUARTER), lambda i: (0, i)))
        for r in rights:
            operands.append(r)
            specs.append(whole(*r.shape))
            width += r.shape[1]
        shape.append(tuple(r.shape[1] for r in rights))
    marks = []
    for row, start, vector, sliced in extras:
        operands.append(vector)
        w = QUARTER if sliced else vector.shape[1]
        specs.append(pl.BlockSpec((8, w), lambda i: (0, i)) if sliced else whole(8, w))
        marks.append((row, start, w))
    return call(
        partial(payload_kernel, tuple(shape), tuple(marks)),
        [hbm((4 * TALL, width)), sds((8, 128), F32)],
        (4,),
        specs,
        [block(TALL, width), whole(8, 128)],
        4 * (0.3 + width / 1536),
        after=after,
    )(*operands)


def share_kernel(order, part, mine, *sent):
    for k, ref in zip(STEPS, (mine,) + sent):
        at = pl.multiple_of(lax.rem(order[0] + k, 4) * SHARE, SHARE)
        ref[...] = part[:, pl.ds(at, SHARE)]


def share(order, part, after=()):
    return call(
        share_kernel,
        [sds((TALL, SHARE))] + [hbm((TALL, SHARE))] * 3,
        (),
        [VMEM],
        [VMEM] * 4,
        1.5,
        scalars=1,
        after=after,
    )(order, part)


def last_sum_kernel(own, a, b, c, out, mark):
    mark[...] = jnp.zeros_like(mark)
    total = own[...].astype(F32) + a[...].astype(F32) + b[...].astype(F32) + c[...].astype(F32)
    out[...] = total.astype(BF)


def last_sum(parts):
    return call(
        last_sum_kernel,
        [hbm((TALL, SHARE)), sds((8, 128), F32)],
        (),
        [VMEM] * 4,
        [VMEM] * 2,
        1,
    )(*parts)


def stats_kernel(a, b, c, d, scales, shifts):
    total = a[...] + b[...] + c[...] + d[...]
    for n, ref in enumerate((scales, shifts)):
        for l in range(LAYERS):
            ref[l] = total[4 * n + 2 * l : 4 * n + 2 * l + 2]


def stats_sum(parts):
    return call(
        stats_kernel,
        [sds((LAYERS, 2, QUARTER), F32)] * 2,
        (),
        [VMEM] * 4,
        [VMEM] * 2,
        1,
    )(*parts)


WIDTHS = {"triples": QKV, "expand": HID, "down": DOWN}
ROW = {"triples": 2, "expand": 0, "down": 1}


def final_kernel(layer, kinds, order, *refs):
    pieces, cols, refs = refs[:4], refs[4], refs[5:]
    shards_in = {}
    for kind in kinds:
        if kind != "down":
            shards_in[kind], refs = refs[0], refs[1:]
    if layer == 0:
        upper, refs = refs[0], refs[1 + sum(2 if k == "down" else 1 for k in kinds) :]
    held = refs[-1]
    for k, ref in zip(STEPS, pieces):
        at = pl.ds(pl.multiple_of(lax.rem(order[0] - k + 4, 4) * SHARE, SHARE), SHARE)
        held[:, at] = ref[...].astype(F32)
    start, lane = 0, lax.broadcasted_iota(jnp.int32, (QUARTER, 128), 1)
    stats = jnp.zeros((QUARTER, 128), F32)
    vectors, refs = refs[0], refs[1:]
    vectors[...] = jnp.zeros_like(vectors)
    for kind in kinds:
        w, row = WIDTHS[kind], ROW[kind]
        product = held[:QUARTER, start : start + w]
        if kind == "down":
            turned = jnp.transpose(product)
            refs[0][0] = turned[:INNER]
            refs[1][0] = turned[INNER:]
            refs = refs[2:]
            vectors[row : row + 1, :QUARTER] = held[QUARTER + row : QUARTER + row + 1, :QUARTER]
        else:
            sums = held[QUARTER + row : QUARTER + row + 1, start : start + w]
            vectors[row : row + 1, :w] = sums
            own = shards_in[kind]
            if kind == "triples":
                own = jnp.concatenate([own[0, i] for i in range(3)], 1)
            else:
                own = own[0]
            own = own.astype(F32)
            at = 0 if kind == "triples" else 1
            stats = jnp.where(lane == at, jnp.sum(own * product, 1, keepdims=True), stats)
            stats = jnp.where(lane == 2 + at, jnp.sum(own * sums, 1, keepdims=True), stats)
            value = cols[:, at : at + 1] * product + cols[:, 2 + at : 3 + at] * sums
            if kind == "triples":
                for i in range(3):
                    refs[0][0, i] = value[:, i * INNER : (i + 1) * INNER]
            else:
                refs[0][0] = value
            refs = refs[1:]
        start += w
    vectors[4:8, :QUARTER] = jnp.transpose(stats)[:4]
    if layer == 0:
        offsets, uplift, closing, joint_stats = refs[:4]
        for l, source in enumerate((vectors, upper)):
            for i in range(3):
                offsets[i, l : l + 1, :] = source[2:3, i * INNER : (i + 1) * INNER]
            uplift[l : l + 1] = source[0:1]
            closing[l : l + 1] = source[1:2, :QUARTER]
            for n in range(2):
                at = 4 * n + 2 * l
                joint_stats[at : at + 2] = source[4 + 2 * n : 6 + 2 * n, :QUARTER]


GRADS = {
    "triples": [(LAYERS, 3, QUARTER, INNER)],
    "expand": [(LAYERS, QUARTER, HID)],
    "down": [(LAYERS, INNER, QUARTER), (LAYERS, HID, QUARTER)],
}


def final(layer, kinds, order, pieces, cols, weights, stacks, upper=None, after=()):
    width = WIDE + DOWN
    operands = list(pieces) + [cols] + [weights[k] for k in kinds if k != "down"]
    if layer == 0:
        operands.append(upper)
    specs = [VMEM] * len(operands)
    shapes, outs, aliases = [sds((8, HID), F32)], [VMEM], {}
    for kind in kinds:
        for place, shape in enumerate(GRADS[kind]):
            if layer == 0:
                aliases[1 + len(operands)] = len(shapes)
                operands.append(stacks[kind][place])
                specs.append(ANY)
            shapes.append(sds(shape, F32))
            outs.append(
                pl.BlockSpec(
                    (1,) + shape[1:], lambda i, s, n=len(shape) - 1: (layer,) + (0,) * n
                )
            )
    outs[0] = whole(8, HID)
    if layer == 0:
        for shape in ((3, LAYERS, INNER), (LAYERS, HID), (LAYERS, QUARTER), (8, QUARTER)):
            shapes.append(sds(shape, F32))
            outs.append(whole(*shape))
    fixed = [whole(*o.shape) if s is VMEM else s for o, s in zip(operands, specs)]
    for n, kind in enumerate(k for k in kinds if k != "down"):
        fixed[5 + n] = of_layer(layer, weights[kind])
    results = call(
        partial(final_kernel, layer, kinds),
        shapes,
        (1,),
        fixed,
        outs,
        2,
        scratch=[pltpu.VMEM((TALL, width), F32)],
        scalars=1,
        aliases=aliases,
        after=after,
    )(order, *operands)
    vectors, results = results[0], list(results[1:])
    grads = {}
    for kind in kinds:
        n = len(GRADS[kind])
        grads[kind], results = results[:n], results[n:]
    return (results if layer == 0 else vectors), grads


def across(array):
    return lax.ppermute(array, "core", [(0, 1), (1, 0)])


def around(array, axes, step):
    return lax.ppermute(array, axes, [(i, (i + step) % 4) for i in range(4)])


def exchanged(array, axes):
    return lax.ppermute(array, axes, [(0, 0), (1, 2), (2, 1), (3, 3)])


def gather_ring(own, axes):
    return [own] + [around(own, axes, k) for k in STEPS[1:]]


def gather_line(own, after=()):
    pieces = gather_ring(own, LINE)
    if after:
        pieces = pieces[:1] + list(gate(pieces[1:], after))
    return pieces + [across(p) for p in pieces]


def scatter_line(order, other, mine, early=(), own=sds):
    own, *sent, mark = combine(order, [mine, across(other), *early], own)
    return [own] + [around(s, LINE, k) for s, k in zip(sent, STEPS[1:])], mark


def outward_pairs(step):
    pairs = []
    for q in range(4):
        for zh in range(2):
            for core in range(2):
                z = (q - step) % 4
                pairs.append(((zh * 2 + core) * 4 + z, q * 4 + zh * 2 + core))
    return pairs


def outward(pieces):
    axes = ("yh", "core", "zh", "zl")
    return [lax.ppermute(p, axes, outward_pairs(k)) for k, p in enumerate(pieces)]


def tiny(array):
    return array[:16, :128]


def fetch(core, both, after):
    (both,) = far(both)
    got = across(pick(core, both, after))
    return settle_weights(core, both, got), got


def reduce_ring(array):
    return lax.psum_scatter(array, RING, scatter_dimension=0, tiled=True)


def crossed(step):
    return [
        ((x * 2 + core) * 2 + yl, ((x + step) % 4 * 2 + yl) * 2 + core)
        for x in range(4)
        for core in range(2)
        for yl in range(2)
    ]


def reduce_x(x, part, after=()):
    mine, *sent = share(x.reshape(1), far(part)[0], after)
    total, mark = last_sum([mine] + far(*[around(s, "x", k) for s, k in zip(sent, STEPS[1:])]))
    return far(*[lax.ppermute(total, ("x", "core", "yl"), crossed(k)) for k in STEPS]), mark


def shards(
    inputs, scales, shifts, triples, offsets, merger, expand, uplift, shrink, closing, cotangent
):
    core, y, z = lax.axis_index("core"), lax.axis_index(RING), lax.axis_index(LINE)
    x_at, q_at = lax.axis_index("x"), lax.axis_index(("yh", "core"))
    here, there = core.reshape(1), (1 - core).reshape(1)
    chunk = core * 4 + z
    sources = [(z - k + 4) % 4 for k in STEPS]
    tokens = jnp.stack([core * 4 + s for s in sources] + [(1 - core) * 4 + s for s in sources])
    blocks = [(s % 2) * 4 + (s // 2) * 2 for s in sources]
    features = jnp.stack([b + core for b in blocks] + [b + 1 - core for b in blocks] + [chunk])
    z_one, x_one, q_one = z.reshape(1), x_at.reshape(1), q_at.reshape(1)

    moved = exchanged(jnp.concatenate([inputs, cotangent], 0), ("yh", "zh"))
    marker = [tiny(moved)]
    triples, offsets = jnp.transpose(triples, (0, 2, 1, 3)), jnp.transpose(offsets, (1, 0, 2))
    wide_args = (triples, expand, scales, shifts, offsets, uplift, closing)
    down_args = (merger, shrink)
    packs = gate([pack(l, wide_args, down_args) for l in range(LAYERS)], marker, hbm)
    sent, sent1 = [lax.all_gather(p, RING, axis=0, tiled=False) for p in packs]
    pieces = gather_line(moved)
    first_pieces = pieces
    tables = rotary_tables()
    (wide, down, norms, bias), got = fetch(here, sent, [tiny(p) for p in pieces[1:4]])

    full0, slope0, query0, keys0, values0, hidden0, x0, *kept = project(
        True, features, far(*pieces), wide, norms, bias, tables
    )
    mixed0, logs0, mixed_kept = attend(query0, keys0, values0, 1)
    other = merge(there, mixed0, hidden0, down)
    mine = merge(here, mixed0, hidden0, down)
    query0, keys0, values0, hidden0, mixed0 = far(*kept, mixed_kept)
    parts, combined = scatter_line(z_one, other, mine)
    wide_kept, down_kept, kept_mark = keep_weights(here, *far(sent, got), [combined])
    late, arrived = marked_gate(parts[1:], [kept_mark])
    parts, marker = parts[:1] + late, [arrived]
    (wide1, down1, norms1, bias1), _ = fetch(here, sent1, marker)
    top, dmixed1, dhidden1, close_sum1 = branch_first(features, far(*first_pieces), down1)
    x1, xhat = finish(parts[:1] + far(*parts[1:]), x0, norms)
    pieces = gather_line(xhat, [close_sum1])

    full1, dupper1, query1, keys1, values1, hidden1, up_sum1 = project(
        False, tokens, far(pieces[0]) + pieces[1:], wide1, norms1, *far(bias1), tables, *far(dhidden1)
    )
    mixed1, logs1 = attend(query1, keys1, values1, 0)
    dqkv1, qkv_sum1 = attend_back(query1, keys1, values1, dmixed1, logs1, tables)
    other = spread(there, dqkv1, dupper1, wide1, norms1)
    mine = spread(here, dqkv1, dupper1, wide1, norms1)
    parts, combined = scatter_line(z_one, other, mine, own=hbm)
    grad1, done1 = payload(
        [(far(full1)[0], [dqkv1, dupper1]), (far(top)[0], [mixed1, hidden1])],
        [(2, 0, qkv_sum1, False), (0, QKV, up_sum1, False), (1, 0, close_sum1, True)],
        [combined],
    )
    late, arrived = marked_gate(parts[1:], [done1])
    gradient, lowered, mark = finish_back(
        chunk.reshape(1), far(parts[0], *late), *far(x1, top)
    )
    (grad1,) = gate([grad1], [arrived], hbm)
    grad1 = reduce_ring(grad1)

    other = merge(there, mixed1, hidden1, down1, [mark])
    mine = merge(here, mixed1, hidden1, down1, [mark])
    front = [mine, across(other)]
    pieces = gather_line(lowered, [tiny(mine)])

    dmixed0, dupper0, up_sum0, close_sum0, dy0 = branch(
        tokens, pieces, *far(down_kept, slope0)
    )
    dqkv0, qkv_sum0 = attend_back(query0, keys0, values0, dmixed0, logs0, far(*tables))
    grad0, done0 = payload(
        [(far(full0)[0], [dupper0]), (dy0, [mixed0, hidden0]), (far(full0)[0], [dqkv0])],
        [(0, 0, up_sum0, False), (1, 0, close_sum0, True), (2, HID + DOWN, qkv_sum0, False)],
    )
    grad0 = reduce_ring(grad0)

    reduced1, summed1 = reduce_x(x_at, grad1, [tiny(dqkv0)])
    rest = (dqkv0, dupper0, far(wide_kept)[0], norms, [done0])
    other = spread(there, *rest)
    mine = spread(here, *rest)
    parts, _ = scatter_line(z_one, other, mine, front)
    *pieces, finished = finish_last(
        z_one, parts[:1] + far(*parts[1:]), *far(x0, gradient, x1), norms1, [summed1])
    inputs_grad, outputs, landed = land(q_one, far(*outward(pieces)))
    cols = [
        jnp.concatenate([scales[l], shifts[l]], 0).astype(F32).T for l in range(LAYERS)
    ]
    weights = {"triples": triples, "expand": expand}
    upper, stacks = final(
        1, ("triples", "expand", "down"), x_one, reduced1, cols[1], weights, None
    )
    reduced, _ = reduce_x(x_at, grad0, [finished])
    (offsets_grad, uplift_grad, closing_grad, stats), stacks = final(
        0, ("expand", "down", "triples"), x_one, reduced, cols[0], weights, stacks, upper, [landed]
    )
    stats = stats + lax.ppermute(stats, "yl", [(0, 1), (1, 0)])
    scales_grad, shifts_grad = stats_sum(gather_ring(stats, LINE))
    return (
        outputs,
        inputs_grad,
        scales_grad,
        shifts_grad,
        jnp.transpose(stacks["triples"][0], (0, 2, 1, 3)),
        jnp.transpose(offsets_grad, (1, 0, 2)),
        stacks["down"][0],
        stacks["expand"][0],
        uplift_grad,
        stacks["down"][1],
        closing_grad,
    )


def solution(mesh):
    grid = Mesh(mesh.devices.reshape(4, 2, 2, 2, 2, 2), AXES)
    row, col = ("yh", "core"), ("yl", "zh", "zl")
    tokens = P(("x",) + col, row)
    weights = (
        P(None, None, row),
        P(None, None, row),
        P(None, row, None, col),
        P(None, None, col),
        P(None, col, row),
        P(None, row, col),
        P(None, col),
        P(None, col, row),
        P(None, row),
    )
    return jax.shard_map(
        shards,
        mesh=grid,
        in_specs=(tokens,) + weights + (tokens,),
        out_specs=(tokens, tokens) + weights,
        check_vma=False,
    )
```

```python
from functools import partial

import jax
import jax.numpy as jnp
import numpy as np
from jax import lax
from jax.experimental import pallas as pl
from jax.experimental.pallas import tpu as pltpu
from jax.sharding import Mesh
from jax.sharding import PartitionSpec as P

D = 1024
QUARTER = D // 4
HEAD = 64
ROT = 16
LAYERS = 2
LEN = 1024
OWN = LEN // 8
HEADS = 2
INNER = HEADS * HEAD
QKV = 3 * INNER
HID = 512
WIDE = QKV + HID
DOWN = INNER + HID
EXTRA = 16
TALL = QUARTER + EXTRA
SHARE = (WIDE + DOWN) // 4
NORM_EPSILON = 1e-05
BF = jnp.bfloat16
F32 = jnp.float32
NN = (((1,), (0,)), ((), ()))
NT = (((1,), (1,)), ((), ()))
TN = (((0,), (0,)), ((), ()))
AXES = ("x", "yh", "core", "yl", "zh", "zl")
LINE = ("zh", "zl")
RING = ("yh", "yl")
STEPS = (0, 1, 3, 2)
ANY = pl.BlockSpec(memory_space=pl.ANY)
HBM = pltpu.MemorySpace.HBM
VMEM = pl.BlockSpec(memory_space=pltpu.VMEM)


def dot(a, b, dims=NN):
    return lax.dot_general(a, b, dims, preferred_element_type=F32)


def sds(shape, dtype=BF):
    return jax.ShapeDtypeStruct(shape, dtype)


def hbm(shape, dtype=BF):
    return HBM(shape, dtype)


def call(
    kernel, out_shape, grid, in_specs, out_specs, micros, scratch=(), scalars=0, aliases={}, after=()
):
    count, extra = scalars + len(in_specs), len(after)

    def body(*refs):
        kernel(*refs[:count], *refs[count + extra :])

    run = pl.pallas_call(
        body,
        out_shape=out_shape,
        grid_spec=pltpu.PrefetchScalarGridSpec(
            num_scalar_prefetch=scalars,
            grid=grid,
            in_specs=list(in_specs) + [ANY] * extra,
            out_specs=out_specs,
            scratch_shapes=scratch,
        ),
        input_output_aliases=aliases,
        compiler_params=pltpu.CompilerParams(vmem_limit_bytes=12 * 2**20),
        cost_estimate=pl.CostEstimate(
            flops=int(micros * 1e6), bytes_accessed=1024, transcendentals=0
        ),
    )
    return lambda *operands: run(*operands, *after)


def far(*arrays):
    return [pltpu.with_memory_space_constraint(a, HBM) for a in arrays]


def block(rows, width):
    return pl.BlockSpec((rows, width), lambda i, *s: (i, 0))


def whole(*shape):
    return pl.BlockSpec(shape, lambda i, *s: (0,) * len(shape))


def rotary_tables():
    lane = jnp.arange(INNER) % (ROT // 2)
    inverse = 10000.0 ** (-(2 * lane).astype(F32) / ROT)
    angles = jnp.arange(LEN).astype(F32)[:, None] * inverse[None, :]
    return lax.optimization_barrier((jnp.cos(angles), jnp.sin(angles)))


def turn(u, cosine, sine, sign):
    half = ROT // 2
    lane = lax.broadcasted_iota(jnp.int32, u.shape, 1) % HEAD
    back = pltpu.roll(u, INNER - half, 1)
    ahead = pltpu.roll(u, half, 1)
    turned = jnp.where(lane < half, -back, ahead)
    return jnp.where(lane < ROT, u * cosine + sign * (turned * sine), u)


def normalized(x):
    mean = jnp.mean(x, 1, keepdims=True)
    r = lax.rsqrt(jnp.mean(x * x, 1, keepdims=True) - mean * mean + NORM_EPSILON)
    return (x - mean) * r, r


def token_copies(order, pieces, held, sems):
    return [
        pltpu.make_async_copy(p, held.at[pl.ds(order[j] * OWN, OWN)], sems.at[order[j]])
        for j, p in enumerate(pieces)
    ]


def feature_copies(order, pieces, held, sems, part=0):
    return [
        pltpu.make_async_copy(
            p.at[pl.ds(part * 512, 512)],
            held.at[
                pl.ds((order[j] // 4) * 512, 512), pl.ds(lax.rem(order[j], 4) * QUARTER, QUARTER)
            ],
            sems.at[order[j]],
        )
        for j, p in enumerate(pieces)
    ]


ROWS = 256


def project_kernel(first, last, order, *refs):
    pieces, refs = refs[:8], refs[8:]
    wide, norms, bias, cosine, sine, *refs = refs
    if last:
        down_grad, *refs = refs
    full, slope, query, keys, values, hidden, *rest = refs
    held, sems = refs[-2:]
    step = pl.program_id(0)

    @pl.when(step == 0)
    def _():
        copies = (feature_copies if first else token_copies)(order, pieces, held, sems)
        for c in copies:
            c.start()

    if first:

        @pl.when(lax.rem(step, 2) == 0)
        def _():
            for j in range(4):
                part = held.at[pl.ds(0, 512), pl.ds(0, QUARTER)]
                pltpu.make_async_copy(part, part, sems.at[step * 2 + j]).wait()

        @pl.when(step == order[8] // 2)
        def _():
            rest[0][...] = held[pl.ds(order[8] * OWN, OWN), :].astype(F32)
    else:
        for j in range(2):
            part = held.at[pl.ds(0, OWN)]
            pltpu.make_async_copy(pieces[0], part, sems.at[step * 2 + j]).wait()
    rows = held[pl.ds(step * ROWS, ROWS), :]
    xh = rows.astype(F32)
    if first:
        xh, _ = normalized(xh)
        rows = xh.astype(BF)
        xh = rows.astype(F32)
    full[...] = rows
    n_a = (xh * norms[0:1] + norms[2:3]).astype(BF)
    n_f = (xh * norms[1:2] + norms[3:4]).astype(BF)
    qkv = dot(n_a, wide[:, :QKV]) + bias[0:1, :QKV]
    table = (cosine[...], sine[...])
    query[...] = (turn(qkv[:, :INNER], *table, 1.0).astype(BF) * 0.125).astype(BF)
    keys[...] = turn(qkv[:, INNER : 2 * INNER], *table, 1.0).astype(BF)
    values[...] = qkv[:, 2 * INNER :].astype(BF)
    u = dot(n_f, wide[:, QKV:]) + bias[0:1, QKV:]
    cdf = 0.5 + 0.5 * lax.erf(u * (0.5**0.5))
    hidden[...] = (u * cdf).astype(BF)
    if first:
        for now, later in zip((query, keys, values, hidden), rest[1:5]):
            later[...] = now[...]
    steep = cdf + u * (jnp.exp(u * u * -0.5) * (1.0 / (2.0 * np.pi) ** 0.5))
    if last:
        du = (down_grad[...].astype(F32) * steep).astype(BF)
        slope[...] = du

        @pl.when(step == 0)
        def _():
            rest[0][...] = jnp.zeros_like(rest[0])

        rest[0][0:1] += jnp.sum(du.astype(F32), 0, keepdims=True)
    else:
        slope[...] = steep.astype(BF)


def project(first, order, pieces, wide, norms, bias, tables, down_grad=None):
    heads = [block(ROWS, INNER)] * 3 + [block(ROWS, HID)]
    shapes = [hbm((LEN, D)), hbm((LEN, HID)) if first else sds((LEN, HID))]
    shapes += [sds((LEN, INNER))] * 3 + [sds((LEN, HID))]
    outs = [block(ROWS, D), block(ROWS, HID)] + heads
    if first:
        shapes += [hbm((OWN, D), F32)] + [hbm((LEN, INNER))] * 3 + [hbm((LEN, HID))]
        outs += [whole(OWN, D)] + heads
    given = []
    if down_grad is not None:
        shapes.append(sds((8, HID), F32))
        outs.append(whole(8, HID))
        given = [down_grad]
    return call(
        partial(project_kernel, first, down_grad is not None),
        shapes,
        (LEN // ROWS,),
        [ANY] * 8
        + [whole(D, WIDE), whole(8, D), whole(8, WIDE)]
        + [block(ROWS, INNER)] * 2
        + [block(ROWS, HID)] * len(given),
        outs,
        7,
        scratch=[pltpu.VMEM((LEN, D), BF), pltpu.SemaphoreType.DMA((8,))],
        scalars=1,
    )(order, *pieces, wide, norms, bias, *tables, *given)


BLOCK = 256


def head_mask(h, rows):
    lane = lax.broadcasted_iota(jnp.int32, (rows, INNER), 1)
    return (lane // HEAD) == h


def causal():
    key = lax.broadcasted_iota(jnp.int32, (BLOCK, BLOCK), 0)
    query = lax.broadcasted_iota(jnp.int32, (BLOCK, BLOCK), 1)
    return key <= query


def attend_kernel(query, keys, values, mixed, logs, *kept):
    for i in range(LEN // BLOCK):
        n = (i + 1) * BLOCK
        here = pl.ds(i * BLOCK, BLOCK)
        q = query[here, :]
        out = jnp.zeros((BLOCK, INNER), F32)
        for h in range(HEADS):
            mask = head_mask(h, BLOCK)
            qh = jnp.where(mask, q, jnp.zeros_like(q))
            s = dot(keys[:n, :], qh, NT)
            tail = jnp.where(causal(), s[n - BLOCK :], -1e30)
            s = jnp.concatenate([s[: n - BLOCK], tail], 0) if i else tail
            top = jnp.max(s, 0, keepdims=True)
            p = jnp.exp(s - top)
            total = jnp.sum(p, 0, keepdims=True)
            logs[h : h + 1, here] = top + jnp.log(total)
            part = dot(values[:n, :], p.astype(BF), TN)
            part = jnp.transpose(part * (1.0 / total))
            out = jnp.where(mask, part, out)
        mixed[here, :] = out.astype(BF)
        for ref in kept:
            ref[here, :] = out.astype(BF)


def attend(query, keys, values, keep):
    return call(
        attend_kernel,
        [sds((LEN, INNER)), sds((8, LEN), F32)] + [hbm((LEN, INNER))] * keep,
        (),
        [VMEM] * 3,
        [VMEM] * (2 + keep),
        5,
    )(query, keys, values)


def attend_back_kernel(
    query, keys, values, dmixed, logs, cosine, sine, dqkv, sums, dkeys, dvalues
):
    dkeys[...] = jnp.zeros_like(dkeys)
    dvalues[...] = jnp.zeros_like(dvalues)
    count = jnp.zeros((1, INNER), F32)
    for i in range(LEN // BLOCK):
        n = (i + 1) * BLOCK
        here = pl.ds(i * BLOCK, BLOCK)
        q, do = query[here, :], dmixed[here, :]
        dq = jnp.zeros((BLOCK, INNER), F32)
        for h in range(HEADS):
            mask = head_mask(h, BLOCK)
            qh = jnp.where(mask, q, jnp.zeros_like(q))
            doh = jnp.where(mask, do, jnp.zeros_like(do))
            s = dot(keys[:n, :], qh, NT)
            p = jnp.exp(s - logs[h : h + 1, here])
            tail = jnp.where(causal(), p[n - BLOCK :], 0.0)
            p = jnp.concatenate([p[: n - BLOCK], tail], 0) if i else tail
            dp = dot(values[:n, :], doh, NT)
            w = p * dp
            delta = jnp.sum(w, 0, keepdims=True)
            ds = (w - p * delta).astype(BF)
            dvalues[:n, :] += dot(p.astype(BF), doh)
            dkeys[:n, :] += dot(ds, qh)
            dq = jnp.where(mask, jnp.transpose(dot(keys[:n, :], ds, TN)), dq)
        dq = turn(dq * 0.125, cosine[here, :], sine[here, :], -1.0).astype(BF)
        dqkv[here, :INNER] = dq
        count += jnp.sum(dq.astype(F32), 0, keepdims=True)
    sums[0:1, :INNER] = count
    dk = turn(dkeys[...], cosine[...], sine[...], -1.0).astype(BF)
    dv = dvalues[...].astype(BF)
    dqkv[:, INNER : 2 * INNER] = dk
    dqkv[:, 2 * INNER :] = dv
    sums[0:1, INNER : 2 * INNER] = jnp.sum(dk.astype(F32), 0, keepdims=True)
    sums[0:1, 2 * INNER :] = jnp.sum(dv.astype(F32), 0, keepdims=True)


def attend_back(query, keys, values, dmixed, logs, tables, after=()):
    return call(
        attend_back_kernel,
        [sds((LEN, QKV)), sds((8, QKV), F32)],
        (),
        [VMEM] * 7,
        [VMEM] * 2,
        6,
        scratch=[pltpu.VMEM((LEN, INNER), F32)] * 2,
        after=after,
    )(query, keys, values, dmixed, logs, *tables)


def merge_kernel(side, mixed, hidden, down, out):
    first = dot(mixed[...], down[:, :INNER], NT)
    out[...] = (first + dot(hidden[...], down[:, INNER:], NT)).astype(BF)


def half_block(width):
    return pl.BlockSpec((ROWS, width), lambda i, s: (s[0] * 2 + i, 0))


def merge(side, mixed, hidden, down, after=()):
    return call(
        merge_kernel,
        sds((LEN // 2, D)),
        (2,),
        [half_block(INNER), half_block(HID), whole(D, DOWN)],
        block(ROWS, D),
        2,
        scalars=1,
        after=after,
    )(side, mixed, hidden, down)


def spread_kernel(side, dqkv, dupper, wide, norms, out):
    first = dot(dqkv[...], wide[:, :QKV], NT) * norms[0:1]
    out[...] = (first + dot(dupper[...], wide[:, QKV:], NT) * norms[1:2]).astype(BF)


def spread(side, dqkv, dupper, wide, norms, after=()):
    return call(
        spread_kernel,
        sds((LEN // 2, D)),
        (2,),
        [half_block(QKV), half_block(HID), whole(D, WIDE), whole(8, D)],
        block(ROWS, D),
        2.2,
        scalars=1,
        after=after,
    )(side, dqkv, dupper, wide, norms)


def branch_first_kernel(order, *refs):
    pieces, refs = refs[:8], refs[8:]
    down, full, dmixed, dhidden, total, held, sems = refs
    step = pl.program_id(0)

    @pl.when(step == 0)
    def _():
        total[...] = jnp.zeros_like(total)
        for c in feature_copies(order, pieces, held, sems, 1):
            c.start()

    @pl.when(lax.rem(step, 2) == 0)
    def _():
        for j in range(4):
            part = held.at[pl.ds(0, 512), pl.ds(0, QUARTER)]
            pltpu.make_async_copy(part, part, sems.at[step * 2 + j]).wait()

    g = held[pl.ds(step * ROWS, ROWS), :]
    full[...] = g
    total[0:1] += jnp.sum(g.astype(F32), 0, keepdims=True)
    both = dot(g, down[...])
    dmixed[...] = both[:, :INNER].astype(BF)
    dhidden[...] = both[:, INNER:].astype(BF)


def branch_first(order, pieces, down):
    return call(
        branch_first_kernel,
        [hbm((LEN, D)), sds((LEN, INNER)), hbm((LEN, HID)), sds((8, D), F32)],
        (LEN // ROWS,),
        [ANY] * 8 + [whole(D, DOWN)],
        [block(ROWS, D), block(ROWS, INNER), block(ROWS, HID), whole(8, D)],
        4,
        scratch=[pltpu.VMEM((LEN, D), BF), pltpu.SemaphoreType.DMA((8,))],
        scalars=1,
    )(order, *pieces, down)


def branch_kernel(order, *refs):
    pieces, refs = refs[:8], refs[8:]
    down, slope, dmixed, dupper, sums, total, full, held, sems = refs
    step = pl.program_id(0)

    @pl.when(step == 0)
    def _():
        sums[...] = jnp.zeros_like(sums)
        total[...] = jnp.zeros_like(total)
        for c in token_copies(order, pieces, held, sems):
            c.start()

    for j in range(2):
        part = held.at[pl.ds(0, OWN)]
        pltpu.make_async_copy(pieces[0], part, sems.at[step * 2 + j]).wait()
    g = held[pl.ds(step * ROWS, ROWS), :]
    full[...] = g
    total[0:1] += jnp.sum(g.astype(F32), 0, keepdims=True)
    both = dot(g, down[...])
    dmixed[...] = both[:, :INNER].astype(BF)
    du = (both[:, INNER:] * slope[...].astype(F32)).astype(BF)
    dupper[...] = du
    sums[0:1] += jnp.sum(du.astype(F32), 0, keepdims=True)


def branch(order, pieces, down, slope, after=()):
    return call(
        branch_kernel,
        [
            sds((LEN, INNER)),
            sds((LEN, HID)),
            sds((8, HID), F32),
            sds((8, D), F32),
            sds((LEN, D)),
        ],
        (LEN // ROWS,),
        [ANY] * 8 + [whole(D, DOWN), block(ROWS, HID)],
        [block(ROWS, INNER), block(ROWS, HID), whole(8, HID), whole(8, D), block(ROWS, D)],
        4,
        scratch=[pltpu.VMEM((LEN, D), BF), pltpu.SemaphoreType.DMA((8,))],
        scalars=1,
        after=after,
    )(order, *pieces, down, slope)


def pack_kernel(has_wide, has_down, layer, *refs):
    refs, out = list(refs[:-1]), refs[-1]
    start = 0
    if has_wide:
        out[QUARTER:, :] = jnp.zeros_like(out[QUARTER:, :])
        triples, expand, scales, shifts, offsets, uplift, closing = refs[:7]
        refs = refs[7:]
        for i in range(3):
            at = slice(i * INNER, (i + 1) * INNER)
            out[:QUARTER, at] = triples[0, i]
            out[QUARTER : QUARTER + 1, at] = offsets[i, layer : layer + 1, :]
        out[:QUARTER, QKV:WIDE] = expand[0]
        out[QUARTER : QUARTER + 1, QKV:WIDE] = uplift[layer : layer + 1, :]
        for i in range(2):
            at = slice(i * QUARTER, (i + 1) * QUARTER)
            out[QUARTER + 1 : QUARTER + 2, at] = scales[layer, i : i + 1, :]
            out[QUARTER + 2 : QUARTER + 3, at] = shifts[layer, i : i + 1, :]
        out[QUARTER + 3 : QUARTER + 4, :QUARTER] = closing[layer : layer + 1, :]
        start = WIDE
    if has_down:
        merger, shrink = refs
        out[:QUARTER, start : start + INNER] = merger[0].T
        out[:QUARTER, start + INNER :] = shrink[0].T


def of_layer(layer, array):
    shape = array.shape[1:]
    return pl.BlockSpec((1,) + shape, lambda i, *s: (layer,) + (0,) * len(shape))


def pack(layer, wide, down, after=()):
    specs = []
    if wide:
        specs += [of_layer(layer, a) for a in wide[:2]] + [whole(*a.shape) for a in wide[2:]]
    specs += [of_layer(layer, a) for a in down]
    width = (WIDE if wide else 0) + (DOWN if down else 0)
    rows = QUARTER + EXTRA if wide else QUARTER
    return call(
        partial(pack_kernel, bool(wide), bool(down), layer),
        hbm((rows, width)),
        (1,),
        specs,
        whole(rows, width),
        1,
        after=after,
    )(*far(*wide), *far(*down))


def pick_kernel(order, both, out, sems):
    copies = [
        pltpu.make_async_copy(both.at[2 * i + 1 - order[0]], out.at[i], sems.at[i])
        for i in range(2)
    ]
    for c in copies:
        c.start()
    for c in copies:
        c.wait()


def pick(order, both, after=()):
    return call(
        pick_kernel,
        sds((2,) + both.shape[1:]),
        (),
        [ANY],
        VMEM,
        1,
        scratch=[pltpu.SemaphoreType.DMA((2,))],
        scalars=1,
        after=after,
    )(order, both)


def halves(core, both, got, sems, places):
    copies = []
    for i in range(2):
        for j, (source, at) in enumerate(
            ((both.at[2 * i + core], 2 * i + core), (got.at[i], 2 * i + 1 - core))
        ):
            for n, (a, b) in enumerate(places(source, at)):
                copies.append(pltpu.make_async_copy(a, b, sems.at[2 * i + j, n]))
    for c in copies:
        c.start()
    for c in copies:
        c.wait()


def wide_places(wide, extra):
    def places(source, at):
        rows = pl.ds(at * QUARTER, QUARTER)
        return (
            (source.at[pl.ds(0, QUARTER), pl.ds(0, WIDE)], wide.at[rows]),
            (source.at[pl.ds(QUARTER, EXTRA), pl.ds(0, WIDE)], extra.at[at]),
        )

    return places


def down_places(down, start):
    def places(source, at):
        rows = pl.ds(at * QUARTER, QUARTER)
        return ((source.at[pl.ds(0, QUARTER), pl.ds(start, DOWN)], down.at[rows]),)

    return places


def vectors(extra, norms, bias):
    bias[...] = jnp.zeros_like(bias)
    norms[...] = jnp.zeros_like(norms)
    bias[0:1] = extra[0, 0:1].astype(F32)
    for q in range(4):
        cols = slice(q * QUARTER, (q + 1) * QUARTER)
        for n in range(5):
            row, at = 1 + n // 2, (n % 2) * QUARTER
            norms[n : n + 1, cols] = extra[q, row : row + 1, at : at + QUARTER].astype(F32)


def weights_kernel(order, both, got, wide, down, norms, bias, extra, sems):
    def places(source, at):
        return wide_places(wide, extra)(source, at) + down_places(down, WIDE)(source, at)

    halves(order[0], both, got, sems, places)
    vectors(extra, norms, bias)


def settle_weights(order, both, got):
    return call(
        weights_kernel,
        [sds((D, WIDE)), sds((D, DOWN)), sds((8, D), F32), hbm((8, WIDE), F32)],
        (),
        [ANY] * 2,
        [VMEM] * 4,
        2,
        scratch=[pltpu.VMEM((4, EXTRA, WIDE), BF), pltpu.SemaphoreType.DMA((4, 3))],
        scalars=1,
    )(order, both, got)


def keep_kernel(order, both, got, wide, down, mark, sems):
    mark[...] = jnp.zeros_like(mark)

    def places(source, at):
        rows = pl.ds(at * QUARTER, QUARTER)
        return (
            (source.at[pl.ds(0, QUARTER), pl.ds(0, WIDE)], wide.at[rows]),
        ) + down_places(down, WIDE)(source, at)

    halves(order[0], both, got, sems, places)


def keep_weights(order, both, got, after):
    return call(
        keep_kernel,
        [hbm((D, WIDE)), hbm((D, DOWN)), sds((8, 128), F32)],
        (),
        [ANY] * 2,
        [VMEM] * 3,
        2,
        scratch=[pltpu.SemaphoreType.DMA((4, 3))],
        scalars=1,
        after=after,
    )(order, both, got)


def gate_kernel(*refs):
    pass


def gate(arrays, after, shape=sds):
    return call(
        gate_kernel,
        [shape(a.shape, a.dtype) for a in arrays],
        (),
        [ANY] * len(arrays),
        [ANY] * len(arrays),
        0.1,
        aliases={i: i for i in range(len(arrays))},
        after=after,
    )(*(arrays if shape is sds else far(*arrays)))


def marked_gate_kernel(*refs):
    refs[-1][...] = jnp.zeros_like(refs[-1])


def marked_gate(arrays, after):
    *same, mark = call(
        marked_gate_kernel,
        [hbm(a.shape, a.dtype) for a in arrays] + [sds((8, 128), F32)],
        (),
        [ANY] * len(arrays),
        [ANY] * len(arrays) + [VMEM],
        0.1,
        aliases={i: i for i in range(len(arrays))},
        after=after,
    )(*far(*arrays))
    return same, mark


def combine_kernel(count, order, *refs):
    halves, (own, *sent), mark = refs[: 2 * count], refs[2 * count : -1], refs[-1]
    mark[...] = jnp.zeros_like(mark)
    for k, ref in zip(STEPS, [own] + sent):
        at = pl.ds(pl.multiple_of(lax.rem(order[0] + k, 4) * OWN, OWN), OWN)
        for part in range(count):
            mine, got = halves[2 * part : 2 * part + 2]
            total = mine[at, :].astype(F32) + got[at, :].astype(F32)
            ref[part * OWN : (part + 1) * OWN, :] = total.astype(ref.dtype)


def combine(order, halves, own=sds):
    count = len(halves) // 2
    rows = count * OWN
    return call(
        partial(combine_kernel, count),
        [own((rows, D), F32)] + [hbm((rows, D))] * 3 + [sds((8, 128), F32)],
        (),
        [VMEM] * len(halves),
        [VMEM] * 5,
        1.5,
        scalars=1,
    )(order, *halves)


def summed(own, others, rows):
    total = own[rows, :]
    for ref in others:
        total = total + ref[rows, :].astype(F32)
    return total


def back_through_norm(dxhat, x):
    xhat, r = normalized(x)
    mean = jnp.mean(dxhat, 1, keepdims=True)
    return r * (dxhat - mean - xhat * jnp.mean(dxhat * xhat, 1, keepdims=True))


EVERY = slice(0, OWN)


def finish_kernel(own, a, b, c, x, norms, new, xhat):
    value = x[...] + (summed(own, (a, b, c), EVERY) + norms[4:5])
    new[...] = value
    xhat[...] = normalized(value)[0].astype(BF)


def finish(parts, x, norms):
    return call(
        finish_kernel,
        [hbm((OWN, D), F32), hbm((OWN, D))],
        (),
        [VMEM] * 6,
        [VMEM] * 2,
        1.5,
    )(*parts, x, norms)


def finish_back_kernel(order, own, a, b, c, x, gradient, new, lowered, mark):
    mark[...] = jnp.zeros_like(mark)
    value = gradient[...].astype(F32) + back_through_norm(summed(own, (a, b, c), EVERY), x[...])
    new[...] = value
    lowered[...] = value.astype(BF)


def finish_back(order, parts, x, gradient):
    return call(
        finish_back_kernel,
        [hbm((OWN, D), F32), sds((OWN, D)), sds((8, 128), F32)],
        (1,),
        [whole(OWN, D)] * 5 + [pl.BlockSpec((OWN, D), lambda i, s: (s[0], 0))],
        [whole(OWN, D)] * 2 + [whole(8, 128)],
        1.5,
        scalars=1,
    )(order, *parts, x, gradient)


def finish_last_kernel(order, own, a, b, c, x_back, gradient, x_front, norms, *refs):
    outs, mark, held = refs[:4], refs[4], refs[5]
    mark[...] = jnp.zeros_like(mark)
    others = (a, b, c)
    held[EVERY, :] = gradient[...] + back_through_norm(summed(own, others, EVERY), x_back[...])
    held[OWN:, :] = x_front[...] + (summed(own, others, slice(OWN, 2 * OWN)) + norms[4:5])
    for k, ref in enumerate(outs):
        q = lax.rem(order[0] + k, 4)
        ref[...] = held[:, pl.ds(pl.multiple_of(q * QUARTER, QUARTER), QUARTER)].astype(BF)


def finish_last(order, parts, x_back, gradient, x_front, norms, after):
    return call(
        finish_last_kernel,
        [hbm((2 * OWN, QUARTER))] * 4 + [sds((8, 128), F32)],
        (),
        [VMEM] * 8,
        [VMEM] * 5,
        2,
        scratch=[pltpu.VMEM((2 * OWN, D), F32)],
        scalars=1,
        after=after,
    )(order, *parts, x_back, gradient, x_front, norms)


def land_kernel(order, *refs):
    pieces, (back, front, mark) = refs[:4], refs[4:]
    mark[...] = jnp.zeros_like(mark)
    for k, p in enumerate(pieces):
        at = pl.ds(pl.multiple_of(lax.rem(order[0] - k + 4, 4) * OWN, OWN), OWN)
        back[at, :] = p[:OWN, :].astype(F32)
        front[at, :] = p[OWN:, :]


def land(order, pieces):
    shape = (4 * OWN, QUARTER)
    return call(
        land_kernel,
        [sds(shape, F32), sds(shape), sds((8, 128), F32)],
        (),
        [VMEM] * 4,
        [VMEM] * 3,
        1,
        scalars=1,
    )(order, *pieces)


def payload_kernel(pairs, marks, *refs):
    out, mark = refs[-2:]
    mark[...] = jnp.zeros_like(mark)
    at, width = 0, 0
    out[QUARTER:, :] = jnp.zeros_like(out[QUARTER:, :])
    for rights in pairs:
        lhs = refs[at][...]
        at += 1
        for w in rights:
            out[:QUARTER, width : width + w] = dot(lhs, refs[at][...], TN).astype(BF)
            at += 1
            width += w
    for row, start, w in marks:
        out[QUARTER + row : QUARTER + row + 1, start : start + w] = refs[at][0:1, :].astype(BF)
        at += 1


def payload(pairs, extras, after=()):
    operands, specs, shape, width = [], [], [], 0
    for left, rights in pairs:
        operands.append(left)
        specs.append(pl.BlockSpec((LEN, QUARTER), lambda i: (0, i)))
        for r in rights:
            operands.append(r)
            specs.append(whole(*r.shape))
            width += r.shape[1]
        shape.append(tuple(r.shape[1] for r in rights))
    marks = []
    for row, start, vector, sliced in extras:
        operands.append(vector)
        w = QUARTER if sliced else vector.shape[1]
        specs.append(pl.BlockSpec((8, w), lambda i: (0, i)) if sliced else whole(8, w))
        marks.append((row, start, w))
    return call(
        partial(payload_kernel, tuple(shape), tuple(marks)),
        [hbm((4 * TALL, width)), sds((8, 128), F32)],
        (4,),
        specs,
        [block(TALL, width), whole(8, 128)],
        4 * (0.3 + width / 1536),
        after=after,
    )(*operands)


def share_kernel(order, part, mine, *sent):
    for k, ref in zip(STEPS, (mine,) + sent):
        at = pl.multiple_of(lax.rem(order[0] + k, 4) * SHARE, SHARE)
        ref[...] = part[:, pl.ds(at, SHARE)]


def share(order, part, after=()):
    return call(
        share_kernel,
        [sds((TALL, SHARE))] + [hbm((TALL, SHARE))] * 3,
        (),
        [VMEM],
        [VMEM] * 4,
        1.5,
        scalars=1,
        after=after,
    )(order, part)


def last_sum_kernel(own, a, b, c, out, mark):
    mark[...] = jnp.zeros_like(mark)
    total = own[...].astype(F32) + a[...].astype(F32) + b[...].astype(F32) + c[...].astype(F32)
    out[...] = total.astype(BF)


def last_sum(parts):
    return call(
        last_sum_kernel,
        [hbm((TALL, SHARE)), sds((8, 128), F32)],
        (),
        [VMEM] * 4,
        [VMEM] * 2,
        1,
    )(*parts)


def stats_kernel(a, b, c, d, scales, shifts):
    total = a[...] + b[...] + c[...] + d[...]
    for n, ref in enumerate((scales, shifts)):
        for l in range(LAYERS):
            ref[l] = total[4 * n + 2 * l : 4 * n + 2 * l + 2]


def stats_sum(parts):
    return call(
        stats_kernel,
        [sds((LAYERS, 2, QUARTER), F32)] * 2,
        (),
        [VMEM] * 4,
        [VMEM] * 2,
        1,
    )(*parts)


WIDTHS = {"triples": QKV, "expand": HID, "down": DOWN}
ROW = {"triples": 2, "expand": 0, "down": 1}


def final_kernel(layer, kinds, order, *refs):
    pieces, cols, refs = refs[:4], refs[4], refs[5:]
    shards_in = {}
    for kind in kinds:
        if kind != "down":
            shards_in[kind], refs = refs[0], refs[1:]
    if layer == 0:
        upper, refs = refs[0], refs[1 + sum(2 if k == "down" else 1 for k in kinds) :]
    held = refs[-1]
    for k, ref in zip(STEPS, pieces):
        at = pl.ds(pl.multiple_of(lax.rem(order[0] - k + 4, 4) * SHARE, SHARE), SHARE)
        held[:, at] = ref[...].astype(F32)
    start, lane = 0, lax.broadcasted_iota(jnp.int32, (QUARTER, 128), 1)
    stats = jnp.zeros((QUARTER, 128), F32)
    vectors, refs = refs[0], refs[1:]
    vectors[...] = jnp.zeros_like(vectors)
    for kind in kinds:
        w, row = WIDTHS[kind], ROW[kind]
        product = held[:QUARTER, start : start + w]
        if kind == "down":
            turned = jnp.transpose(product)
            refs[0][0] = turned[:INNER]
            refs[1][0] = turned[INNER:]
            refs = refs[2:]
            vectors[row : row + 1, :QUARTER] = held[QUARTER + row : QUARTER + row + 1, :QUARTER]
        else:
            sums = held[QUARTER + row : QUARTER + row + 1, start : start + w]
            vectors[row : row + 1, :w] = sums
            own = shards_in[kind]
            if kind == "triples":
                own = jnp.concatenate([own[0, i] for i in range(3)], 1)
            else:
                own = own[0]
            own = own.astype(F32)
            at = 0 if kind == "triples" else 1
            stats = jnp.where(lane == at, jnp.sum(own * product, 1, keepdims=True), stats)
            stats = jnp.where(lane == 2 + at, jnp.sum(own * sums, 1, keepdims=True), stats)
            value = cols[:, at : at + 1] * product + cols[:, 2 + at : 3 + at] * sums
            if kind == "triples":
                for i in range(3):
                    refs[0][0, i] = value[:, i * INNER : (i + 1) * INNER]
            else:
                refs[0][0] = value
            refs = refs[1:]
        start += w
    vectors[4:8, :QUARTER] = jnp.transpose(stats)[:4]
    if layer == 0:
        offsets, uplift, closing, joint_stats = refs[:4]
        for l, source in enumerate((vectors, upper)):
            for i in range(3):
                offsets[i, l : l + 1, :] = source[2:3, i * INNER : (i + 1) * INNER]
            uplift[l : l + 1] = source[0:1]
            closing[l : l + 1] = source[1:2, :QUARTER]
            for n in range(2):
                at = 4 * n + 2 * l
                joint_stats[at : at + 2] = source[4 + 2 * n : 6 + 2 * n, :QUARTER]


GRADS = {
    "triples": [(LAYERS, 3, QUARTER, INNER)],
    "expand": [(LAYERS, QUARTER, HID)],
    "down": [(LAYERS, INNER, QUARTER), (LAYERS, HID, QUARTER)],
}


def final(layer, kinds, order, pieces, cols, weights, stacks, upper=None):
    width = WIDE + DOWN
    operands = list(pieces) + [cols] + [weights[k] for k in kinds if k != "down"]
    if layer == 0:
        operands.append(upper)
    specs = [VMEM] * len(operands)
    shapes, outs, aliases = [sds((8, HID), F32)], [VMEM], {}
    for kind in kinds:
        for place, shape in enumerate(GRADS[kind]):
            if layer == 0:
                aliases[1 + len(operands)] = len(shapes)
                operands.append(stacks[kind][place])
                specs.append(ANY)
            shapes.append(sds(shape, F32))
            outs.append(
                pl.BlockSpec(
                    (1,) + shape[1:], lambda i, s, n=len(shape) - 1: (layer,) + (0,) * n
                )
            )
    outs[0] = whole(8, HID)
    if layer == 0:
        for shape in ((3, LAYERS, INNER), (LAYERS, HID), (LAYERS, QUARTER), (8, QUARTER)):
            shapes.append(sds(shape, F32))
            outs.append(whole(*shape))
    fixed = [whole(*o.shape) if s is VMEM else s for o, s in zip(operands, specs)]
    for n, kind in enumerate(k for k in kinds if k != "down"):
        fixed[5 + n] = of_layer(layer, weights[kind])
    results = call(
        partial(final_kernel, layer, kinds),
        shapes,
        (1,),
        fixed,
        outs,
        2,
        scratch=[pltpu.VMEM((TALL, width), F32)],
        scalars=1,
        aliases=aliases,
    )(order, *operands)
    vectors, results = results[0], list(results[1:])
    grads = {}
    for kind in kinds:
        n = len(GRADS[kind])
        grads[kind], results = results[:n], results[n:]
    return (results if layer == 0 else vectors), grads


def across(array):
    return lax.ppermute(array, "core", [(0, 1), (1, 0)])


def around(array, axes, step):
    return lax.ppermute(array, axes, [(i, (i + step) % 4) for i in range(4)])


def exchanged(array, axes):
    return lax.ppermute(array, axes, [(0, 0), (1, 2), (2, 1), (3, 3)])


def gather_ring(own, axes):
    return [own] + [around(own, axes, k) for k in STEPS[1:]]


def gather_line(own, after=()):
    pieces = gather_ring(own, LINE)
    if after:
        pieces = pieces[:1] + list(gate(pieces[1:], after))
    return pieces + [across(p) for p in pieces]


def scatter_line(order, other, mine, early=(), own=sds):
    own, *sent, mark = combine(order, [mine, across(other), *early], own)
    return [own] + [around(s, LINE, k) for s, k in zip(sent, STEPS[1:])], mark


def outward_pairs(step):
    pairs = []
    for q in range(4):
        for zh in range(2):
            for core in range(2):
                z = (q - step) % 4
                pairs.append(((zh * 2 + core) * 4 + z, q * 4 + zh * 2 + core))
    return pairs


def outward(pieces):
    axes = ("yh", "core", "zh", "zl")
    return [lax.ppermute(p, axes, outward_pairs(k)) for k, p in enumerate(pieces)]


def tiny(array):
    return array[:16, :128]


def fetch(core, both, after):
    (both,) = far(both)
    got = across(pick(core, both, after))
    return settle_weights(core, both, got), got


def reduce_ring(array):
    return lax.psum_scatter(array, RING, scatter_dimension=0, tiled=True)


def crossed(step):
    return [
        ((x * 2 + core) * 2 + yl, ((x + step) % 4 * 2 + yl) * 2 + core)
        for x in range(4)
        for core in range(2)
        for yl in range(2)
    ]


def reduce_x(x, part, after=()):
    mine, *sent = share(x.reshape(1), far(part)[0], after)
    total, mark = last_sum([mine] + far(*[around(s, "x", k) for s, k in zip(sent, STEPS[1:])]))
    return far(*[lax.ppermute(total, ("x", "core", "yl"), crossed(k)) for k in STEPS]), mark


def shards(
    inputs, scales, shifts, triples, offsets, merger, expand, uplift, shrink, closing, cotangent
):
    core, y, z = lax.axis_index("core"), lax.axis_index(RING), lax.axis_index(LINE)
    x_at, q_at = lax.axis_index("x"), lax.axis_index(("yh", "core"))
    here, there = core.reshape(1), (1 - core).reshape(1)
    chunk = core * 4 + z
    sources = [(z - k + 4) % 4 for k in STEPS]
    tokens = jnp.stack([core * 4 + s for s in sources] + [(1 - core) * 4 + s for s in sources])
    blocks = [(s % 2) * 4 + (s // 2) * 2 for s in sources]
    features = jnp.stack([b + core for b in blocks] + [b + 1 - core for b in blocks] + [chunk])
    z_one, x_one, q_one = z.reshape(1), x_at.reshape(1), q_at.reshape(1)

    moved = exchanged(jnp.concatenate([inputs, cotangent], 0), ("yh", "zh"))
    marker = [tiny(moved)]
    triples, offsets = jnp.transpose(triples, (0, 2, 1, 3)), jnp.transpose(offsets, (1, 0, 2))
    wide_args = (triples, expand, scales, shifts, offsets, uplift, closing)
    down_args = (merger, shrink)
    packs = gate([pack(l, wide_args, down_args) for l in range(LAYERS)], marker, hbm)
    sent, sent1 = [lax.all_gather(p, RING, axis=0, tiled=False) for p in packs]
    pieces = gather_line(moved)
    first_pieces = pieces
    tables = rotary_tables()
    (wide, down, norms, bias), got = fetch(here, sent, [tiny(p) for p in pieces[1:4]])

    full0, slope0, query0, keys0, values0, hidden0, x0, *kept = project(
        True, features, far(*pieces), wide, norms, bias, tables
    )
    mixed0, logs0, mixed_kept = attend(query0, keys0, values0, 1)
    other = merge(there, mixed0, hidden0, down)
    mine = merge(here, mixed0, hidden0, down)
    query0, keys0, values0, hidden0, mixed0 = far(*kept, mixed_kept)
    parts, combined = scatter_line(z_one, other, mine)
    wide_kept, down_kept, kept_mark = keep_weights(here, *far(sent, got), [combined])
    late, arrived = marked_gate(parts[1:], [kept_mark])
    parts, marker = parts[:1] + late, [arrived]
    (wide1, down1, norms1, bias1), _ = fetch(here, sent1, marker)
    top, dmixed1, dhidden1, close_sum1 = branch_first(features, far(*first_pieces), down1)
    x1, xhat = finish(parts[:1] + far(*parts[1:]), x0, norms)
    pieces = gather_line(xhat, [close_sum1])

    full1, dupper1, query1, keys1, values1, hidden1, up_sum1 = project(
        False, tokens, far(pieces[0]) + pieces[1:], wide1, norms1, *far(bias1), tables, *far(dhidden1)
    )
    mixed1, logs1 = attend(query1, keys1, values1, 0)
    dqkv1, qkv_sum1 = attend_back(query1, keys1, values1, dmixed1, logs1, tables)
    other = spread(there, dqkv1, dupper1, wide1, norms1)
    mine = spread(here, dqkv1, dupper1, wide1, norms1)
    parts, combined = scatter_line(z_one, other, mine, own=hbm)
    grad1, done1 = payload(
        [(far(full1)[0], [dqkv1, dupper1]), (far(top)[0], [mixed1, hidden1])],
        [(2, 0, qkv_sum1, False), (0, QKV, up_sum1, False), (1, 0, close_sum1, True)],
        [combined],
    )
    late, arrived = marked_gate(parts[1:], [done1])
    gradient, lowered, mark = finish_back(
        chunk.reshape(1), far(parts[0], *late), *far(x1, top)
    )
    (grad1,) = gate([grad1], [arrived], hbm)
    grad1 = reduce_ring(grad1)

    other = merge(there, mixed1, hidden1, down1, [mark])
    mine = merge(here, mixed1, hidden1, down1, [mark])
    front = [mine, across(other)]
    pieces = gather_line(lowered, [tiny(mine)])

    dmixed0, dupper0, up_sum0, close_sum0, dy0 = branch(
        tokens, pieces, *far(down_kept, slope0)
    )
    dqkv0, qkv_sum0 = attend_back(query0, keys0, values0, dmixed0, logs0, far(*tables))
    grad0, done0 = payload(
        [(far(full0)[0], [dqkv0, dupper0]), (dy0, [mixed0, hidden0])],
        [(2, 0, qkv_sum0, False), (0, QKV, up_sum0, False), (1, 0, close_sum0, True)],
    )
    grad0 = reduce_ring(grad0)

    reduced1, summed1 = reduce_x(x_at, grad1, [tiny(dqkv0)])
    rest = (dqkv0, dupper0, far(wide_kept)[0], norms, [done0])
    other = spread(there, *rest)
    mine = spread(here, *rest)
    parts, _ = scatter_line(z_one, other, mine, front)
    *pieces, finished = finish_last(
        z_one, parts[:1] + far(*parts[1:]), *far(x0, gradient, x1), norms1, [summed1])
    inputs_grad, outputs, landed = land(q_one, far(*outward(pieces)))
    cols = [
        jnp.concatenate([scales[l], shifts[l]], 0).astype(F32).T for l in range(LAYERS)
    ]
    weights = {"triples": triples, "expand": expand}
    upper, stacks = final(
        1, ("triples", "expand", "down"), x_one, reduced1, cols[1], weights, None
    )
    reduced, _ = reduce_x(x_at, grad0, [finished])
    (offsets_grad, uplift_grad, closing_grad, stats), stacks = final(
        0, ("triples", "expand", "down"), x_one, reduced, cols[0], weights, stacks, upper
    )
    stats = stats + lax.ppermute(stats, "yl", [(0, 1), (1, 0)])
    scales_grad, shifts_grad = stats_sum(gather_ring(stats, LINE))
    return (
        outputs,
        inputs_grad,
        scales_grad,
        shifts_grad,
        jnp.transpose(stacks["triples"][0], (0, 2, 1, 3)),
        jnp.transpose(offsets_grad, (1, 0, 2)),
        stacks["down"][0],
        stacks["expand"][0],
        uplift_grad,
        stacks["down"][1],
        closing_grad,
    )


def solution(mesh):
    grid = Mesh(mesh.devices.reshape(4, 2, 2, 2, 2, 2), AXES)
    row, col = ("yh", "core"), ("yl", "zh", "zl")
    tokens = P(("x",) + col, row)
    weights = (
        P(None, None, row),
        P(None, None, row),
        P(None, row, None, col),
        P(None, None, col),
        P(None, col, row),
        P(None, row, col),
        P(None, col),
        P(None, col, row),
        P(None, row),
    )
    return jax.shard_map(
        shards,
        mesh=grid,
        in_specs=(tokens,) + weights + (tokens,),
        out_specs=(tokens, tokens) + weights,
        check_vma=False,
    )
```

```python
from functools import partial

import jax
import jax.numpy as jnp
import numpy as np
from jax import lax
from jax.experimental import pallas as pl
from jax.experimental.pallas import tpu as pltpu
from jax.sharding import Mesh
from jax.sharding import PartitionSpec as P

D = 1024
QUARTER = D // 4
HEAD = 64
ROT = 16
LAYERS = 2
LEN = 1024
OWN = LEN // 8
HEADS = 2
INNER = HEADS * HEAD
QKV = 3 * INNER
HID = 512
WIDE = QKV + HID
DOWN = INNER + HID
EXTRA = 16
TALL = QUARTER + EXTRA
SHARE = (WIDE + DOWN) // 4
NORM_EPSILON = 1e-05
BF = jnp.bfloat16
F32 = jnp.float32
NN = (((1,), (0,)), ((), ()))
NT = (((1,), (1,)), ((), ()))
TN = (((0,), (0,)), ((), ()))
AXES = ("x", "yh", "core", "yl", "zh", "zl")
LINE = ("zh", "zl")
RING = ("yh", "yl")
STEPS = (0, 1, 3, 2)
ANY = pl.BlockSpec(memory_space=pl.ANY)
HBM = pltpu.MemorySpace.HBM
VMEM = pl.BlockSpec(memory_space=pltpu.VMEM)


def dot(a, b, dims=NN):
    return lax.dot_general(a, b, dims, preferred_element_type=F32)


def sds(shape, dtype=BF):
    return jax.ShapeDtypeStruct(shape, dtype)


def hbm(shape, dtype=BF):
    return HBM(shape, dtype)


def call(
    kernel, out_shape, grid, in_specs, out_specs, micros, scratch=(), scalars=0, aliases={}, after=()
):
    count, extra = scalars + len(in_specs), len(after)

    def body(*refs):
        kernel(*refs[:count], *refs[count + extra :])

    run = pl.pallas_call(
        body,
        out_shape=out_shape,
        grid_spec=pltpu.PrefetchScalarGridSpec(
            num_scalar_prefetch=scalars,
            grid=grid,
            in_specs=list(in_specs) + [ANY] * extra,
            out_specs=out_specs,
            scratch_shapes=scratch,
        ),
        input_output_aliases=aliases,
        compiler_params=pltpu.CompilerParams(vmem_limit_bytes=12 * 2**20),
        cost_estimate=pl.CostEstimate(
            flops=int(micros * 1e6), bytes_accessed=1024, transcendentals=0
        ),
    )
    return lambda *operands: run(*operands, *after)


def far(*arrays):
    return [pltpu.with_memory_space_constraint(a, HBM) for a in arrays]


def block(rows, width):
    return pl.BlockSpec((rows, width), lambda i, *s: (i, 0))


def whole(*shape):
    return pl.BlockSpec(shape, lambda i, *s: (0,) * len(shape))


def rotary_tables():
    lane = jnp.arange(INNER) % (ROT // 2)
    inverse = 10000.0 ** (-(2 * lane).astype(F32) / ROT)
    angles = jnp.arange(LEN).astype(F32)[:, None] * inverse[None, :]
    return lax.optimization_barrier((jnp.cos(angles), jnp.sin(angles)))


def turn(u, cosine, sine, sign):
    half = ROT // 2
    lane = lax.broadcasted_iota(jnp.int32, u.shape, 1) % HEAD
    back = pltpu.roll(u, INNER - half, 1)
    ahead = pltpu.roll(u, half, 1)
    turned = jnp.where(lane < half, -back, ahead)
    return jnp.where(lane < ROT, u * cosine + sign * (turned * sine), u)


def normalized(x):
    mean = jnp.mean(x, 1, keepdims=True)
    r = lax.rsqrt(jnp.mean(x * x, 1, keepdims=True) - mean * mean + NORM_EPSILON)
    return (x - mean) * r, r


def token_copies(order, pieces, held, sems):
    return [
        pltpu.make_async_copy(p, held.at[pl.ds(order[j] * OWN, OWN)], sems.at[order[j]])
        for j, p in enumerate(pieces)
    ]


def feature_copies(order, pieces, held, sems, part=0):
    return [
        pltpu.make_async_copy(
            p.at[pl.ds(part * 512, 512)],
            held.at[
                pl.ds((order[j] // 4) * 512, 512), pl.ds(lax.rem(order[j], 4) * QUARTER, QUARTER)
            ],
            sems.at[order[j]],
        )
        for j, p in enumerate(pieces)
    ]


ROWS = 256


def project_kernel(first, last, order, *refs):
    pieces, refs = refs[:8], refs[8:]
    wide, norms, bias, cosine, sine, *refs = refs
    if last:
        down_grad, *refs = refs
    full, slope, query, keys, values, hidden, *rest = refs
    held, sems = refs[-2:]
    step = pl.program_id(0)

    @pl.when(step == 0)
    def _():
        copies = (feature_copies if first else token_copies)(order, pieces, held, sems)
        for c in copies:
            c.start()

    if first:

        @pl.when(lax.rem(step, 2) == 0)
        def _():
            for j in range(4):
                part = held.at[pl.ds(0, 512), pl.ds(0, QUARTER)]
                pltpu.make_async_copy(part, part, sems.at[step * 2 + j]).wait()

        @pl.when(step == order[8] // 2)
        def _():
            rest[0][...] = held[pl.ds(order[8] * OWN, OWN), :].astype(F32)
    else:
        for j in range(2):
            part = held.at[pl.ds(0, OWN)]
            pltpu.make_async_copy(pieces[0], part, sems.at[step * 2 + j]).wait()
    rows = held[pl.ds(step * ROWS, ROWS), :]
    xh = rows.astype(F32)
    if first:
        xh, _ = normalized(xh)
        rows = xh.astype(BF)
        xh = rows.astype(F32)
    full[...] = rows
    n_a = (xh * norms[0:1] + norms[2:3]).astype(BF)
    n_f = (xh * norms[1:2] + norms[3:4]).astype(BF)
    qkv = dot(n_a, wide[:, :QKV]) + bias[0:1, :QKV]
    table = (cosine[...], sine[...])
    query[...] = (turn(qkv[:, :INNER], *table, 1.0).astype(BF) * 0.125).astype(BF)
    keys[...] = turn(qkv[:, INNER : 2 * INNER], *table, 1.0).astype(BF)
    values[...] = qkv[:, 2 * INNER :].astype(BF)
    u = dot(n_f, wide[:, QKV:]) + bias[0:1, QKV:]
    cdf = 0.5 + 0.5 * lax.erf(u * (0.5**0.5))
    hidden[...] = (u * cdf).astype(BF)
    if first:
        for now, later in zip((query, keys, values, hidden), rest[1:5]):
            later[...] = now[...]
    steep = cdf + u * (jnp.exp(u * u * -0.5) * (1.0 / (2.0 * np.pi) ** 0.5))
    if last:
        du = (down_grad[...].astype(F32) * steep).astype(BF)
        slope[...] = du

        @pl.when(step == 0)
        def _():
            rest[0][...] = jnp.zeros_like(rest[0])

        rest[0][0:1] += jnp.sum(du.astype(F32), 0, keepdims=True)
    else:
        slope[...] = steep.astype(BF)


def project(first, order, pieces, wide, norms, bias, tables, down_grad=None):
    heads = [block(ROWS, INNER)] * 3 + [block(ROWS, HID)]
    shapes = [hbm((LEN, D)), hbm((LEN, HID)) if first else sds((LEN, HID))]
    shapes += [sds((LEN, INNER))] * 3 + [sds((LEN, HID))]
    outs = [block(ROWS, D), block(ROWS, HID)] + heads
    if first:
        shapes += [hbm((OWN, D), F32)] + [hbm((LEN, INNER))] * 3 + [hbm((LEN, HID))]
        outs += [whole(OWN, D)] + heads
    given = []
    if down_grad is not None:
        shapes.append(sds((8, HID), F32))
        outs.append(whole(8, HID))
        given = [down_grad]
    return call(
        partial(project_kernel, first, down_grad is not None),
        shapes,
        (LEN // ROWS,),
        [ANY] * 8
        + [whole(D, WIDE), whole(8, D), whole(8, WIDE)]
        + [block(ROWS, INNER)] * 2
        + [block(ROWS, HID)] * len(given),
        outs,
        7,
        scratch=[pltpu.VMEM((LEN, D), BF), pltpu.SemaphoreType.DMA((8,))],
        scalars=1,
    )(order, *pieces, wide, norms, bias, *tables, *given)


BLOCK = 256


def head_mask(h, rows):
    lane = lax.broadcasted_iota(jnp.int32, (rows, INNER), 1)
    return (lane // HEAD) == h


def causal():
    key = lax.broadcasted_iota(jnp.int32, (BLOCK, BLOCK), 0)
    query = lax.broadcasted_iota(jnp.int32, (BLOCK, BLOCK), 1)
    return key <= query


def attend_kernel(query, keys, values, mixed, logs, *kept):
    for i in range(LEN // BLOCK):
        n = (i + 1) * BLOCK
        here = pl.ds(i * BLOCK, BLOCK)
        q = query[here, :]
        out = jnp.zeros((BLOCK, INNER), F32)
        for h in range(HEADS):
            mask = head_mask(h, BLOCK)
            qh = jnp.where(mask, q, jnp.zeros_like(q))
            s = dot(keys[:n, :], qh, NT)
            tail = jnp.where(causal(), s[n - BLOCK :], -1e30)
            s = jnp.concatenate([s[: n - BLOCK], tail], 0) if i else tail
            top = jnp.max(s, 0, keepdims=True)
            p = jnp.exp(s - top)
            total = jnp.sum(p, 0, keepdims=True)
            logs[h : h + 1, here] = top + jnp.log(total)
            part = dot(values[:n, :], p.astype(BF), TN)
            part = jnp.transpose(part * (1.0 / total))
            out = jnp.where(mask, part, out)
        mixed[here, :] = out.astype(BF)
        for ref in kept:
            ref[here, :] = out.astype(BF)


def attend(query, keys, values, keep):
    return call(
        attend_kernel,
        [sds((LEN, INNER)), sds((8, LEN), F32)] + [hbm((LEN, INNER))] * keep,
        (),
        [VMEM] * 3,
        [VMEM] * (2 + keep),
        5,
    )(query, keys, values)


def attend_back_kernel(
    query, keys, values, dmixed, logs, cosine, sine, dqkv, sums, dkeys, dvalues
):
    dkeys[...] = jnp.zeros_like(dkeys)
    dvalues[...] = jnp.zeros_like(dvalues)
    count = jnp.zeros((1, INNER), F32)
    for i in range(LEN // BLOCK):
        n = (i + 1) * BLOCK
        here = pl.ds(i * BLOCK, BLOCK)
        q, do = query[here, :], dmixed[here, :]
        dq = jnp.zeros((BLOCK, INNER), F32)
        for h in range(HEADS):
            mask = head_mask(h, BLOCK)
            qh = jnp.where(mask, q, jnp.zeros_like(q))
            doh = jnp.where(mask, do, jnp.zeros_like(do))
            s = dot(keys[:n, :], qh, NT)
            p = jnp.exp(s - logs[h : h + 1, here])
            tail = jnp.where(causal(), p[n - BLOCK :], 0.0)
            p = jnp.concatenate([p[: n - BLOCK], tail], 0) if i else tail
            dp = dot(values[:n, :], doh, NT)
            w = p * dp
            delta = jnp.sum(w, 0, keepdims=True)
            ds = (w - p * delta).astype(BF)
            dvalues[:n, :] += dot(p.astype(BF), doh)
            dkeys[:n, :] += dot(ds, qh)
            dq = jnp.where(mask, jnp.transpose(dot(keys[:n, :], ds, TN)), dq)
        dq = turn(dq * 0.125, cosine[here, :], sine[here, :], -1.0).astype(BF)
        dqkv[here, :INNER] = dq
        count += jnp.sum(dq.astype(F32), 0, keepdims=True)
    sums[0:1, :INNER] = count
    dk = turn(dkeys[...], cosine[...], sine[...], -1.0).astype(BF)
    dv = dvalues[...].astype(BF)
    dqkv[:, INNER : 2 * INNER] = dk
    dqkv[:, 2 * INNER :] = dv
    sums[0:1, INNER : 2 * INNER] = jnp.sum(dk.astype(F32), 0, keepdims=True)
    sums[0:1, 2 * INNER :] = jnp.sum(dv.astype(F32), 0, keepdims=True)


def attend_back(query, keys, values, dmixed, logs, tables, after=()):
    return call(
        attend_back_kernel,
        [sds((LEN, QKV)), sds((8, QKV), F32)],
        (),
        [VMEM] * 7,
        [VMEM] * 2,
        6,
        scratch=[pltpu.VMEM((LEN, INNER), F32)] * 2,
        after=after,
    )(query, keys, values, dmixed, logs, *tables)


def merge_kernel(side, mixed, hidden, down, out):
    first = dot(mixed[...], down[:, :INNER], NT)
    out[...] = (first + dot(hidden[...], down[:, INNER:], NT)).astype(BF)


def half_block(width):
    return pl.BlockSpec((ROWS, width), lambda i, s: (s[0] * 2 + i, 0))


def merge(side, mixed, hidden, down, after=()):
    return call(
        merge_kernel,
        sds((LEN // 2, D)),
        (2,),
        [half_block(INNER), half_block(HID), whole(D, DOWN)],
        block(ROWS, D),
        2,
        scalars=1,
        after=after,
    )(side, mixed, hidden, down)


def spread_kernel(side, dqkv, dupper, wide, norms, out):
    first = dot(dqkv[...], wide[:, :QKV], NT) * norms[0:1]
    out[...] = (first + dot(dupper[...], wide[:, QKV:], NT) * norms[1:2]).astype(BF)


def spread(side, dqkv, dupper, wide, norms, after=()):
    return call(
        spread_kernel,
        sds((LEN // 2, D)),
        (2,),
        [half_block(QKV), half_block(HID), whole(D, WIDE), whole(8, D)],
        block(ROWS, D),
        2.2,
        scalars=1,
        after=after,
    )(side, dqkv, dupper, wide, norms)


def branch_first_kernel(order, *refs):
    pieces, refs = refs[:8], refs[8:]
    down, full, dmixed, dhidden, total, held, sems = refs
    step = pl.program_id(0)

    @pl.when(step == 0)
    def _():
        total[...] = jnp.zeros_like(total)
        for c in feature_copies(order, pieces, held, sems, 1):
            c.start()

    @pl.when(lax.rem(step, 2) == 0)
    def _():
        for j in range(4):
            part = held.at[pl.ds(0, 512), pl.ds(0, QUARTER)]
            pltpu.make_async_copy(part, part, sems.at[step * 2 + j]).wait()

    g = held[pl.ds(step * ROWS, ROWS), :]
    full[...] = g
    total[0:1] += jnp.sum(g.astype(F32), 0, keepdims=True)
    both = dot(g, down[...])
    dmixed[...] = both[:, :INNER].astype(BF)
    dhidden[...] = both[:, INNER:].astype(BF)


def branch_first(order, pieces, down):
    return call(
        branch_first_kernel,
        [hbm((LEN, D)), sds((LEN, INNER)), hbm((LEN, HID)), sds((8, D), F32)],
        (LEN // ROWS,),
        [ANY] * 8 + [whole(D, DOWN)],
        [block(ROWS, D), block(ROWS, INNER), block(ROWS, HID), whole(8, D)],
        4,
        scratch=[pltpu.VMEM((LEN, D), BF), pltpu.SemaphoreType.DMA((8,))],
        scalars=1,
    )(order, *pieces, down)


def branch_kernel(order, *refs):
    pieces, refs = refs[:8], refs[8:]
    down, slope, dmixed, dupper, sums, total, full, held, sems = refs
    step = pl.program_id(0)

    @pl.when(step == 0)
    def _():
        sums[...] = jnp.zeros_like(sums)
        total[...] = jnp.zeros_like(total)
        for c in token_copies(order, pieces, held, sems):
            c.start()

    for j in range(2):
        part = held.at[pl.ds(0, OWN)]
        pltpu.make_async_copy(pieces[0], part, sems.at[step * 2 + j]).wait()
    g = held[pl.ds(step * ROWS, ROWS), :]
    full[...] = g
    total[0:1] += jnp.sum(g.astype(F32), 0, keepdims=True)
    both = dot(g, down[...])
    dmixed[...] = both[:, :INNER].astype(BF)
    du = (both[:, INNER:] * slope[...].astype(F32)).astype(BF)
    dupper[...] = du
    sums[0:1] += jnp.sum(du.astype(F32), 0, keepdims=True)


def branch(order, pieces, down, slope, after=()):
    return call(
        branch_kernel,
        [
            sds((LEN, INNER)),
            sds((LEN, HID)),
            sds((8, HID), F32),
            sds((8, D), F32),
            sds((LEN, D)),
        ],
        (LEN // ROWS,),
        [ANY] * 8 + [whole(D, DOWN), block(ROWS, HID)],
        [block(ROWS, INNER), block(ROWS, HID), whole(8, HID), whole(8, D), block(ROWS, D)],
        4,
        scratch=[pltpu.VMEM((LEN, D), BF), pltpu.SemaphoreType.DMA((8,))],
        scalars=1,
        after=after,
    )(order, *pieces, down, slope)


def pack_kernel(has_wide, has_down, layer, *refs):
    refs, out = list(refs[:-1]), refs[-1]
    start = 0
    if has_wide:
        out[QUARTER:, :] = jnp.zeros_like(out[QUARTER:, :])
        triples, expand, scales, shifts, offsets, uplift, closing = refs[:7]
        refs = refs[7:]
        for i in range(3):
            at = slice(i * INNER, (i + 1) * INNER)
            out[:QUARTER, at] = triples[0, :, i, :]
            out[QUARTER : QUARTER + 1, at] = offsets[layer, i : i + 1, :]
        out[:QUARTER, QKV:WIDE] = expand[0]
        out[QUARTER : QUARTER + 1, QKV:WIDE] = uplift[layer : layer + 1, :]
        for i in range(2):
            at = slice(i * QUARTER, (i + 1) * QUARTER)
            out[QUARTER + 1 : QUARTER + 2, at] = scales[layer, i : i + 1, :]
            out[QUARTER + 2 : QUARTER + 3, at] = shifts[layer, i : i + 1, :]
        out[QUARTER + 3 : QUARTER + 4, :QUARTER] = closing[layer : layer + 1, :]
        start = WIDE
    if has_down:
        merger, shrink = refs
        out[:QUARTER, start : start + INNER] = merger[0].T
        out[:QUARTER, start + INNER :] = shrink[0].T


def of_layer(layer, array):
    shape = array.shape[1:]
    return pl.BlockSpec((1,) + shape, lambda i, *s: (layer,) + (0,) * len(shape))


def pack(layer, wide, down, after=()):
    specs = []
    if wide:
        specs += [of_layer(layer, a) for a in wide[:2]] + [whole(*a.shape) for a in wide[2:]]
    specs += [of_layer(layer, a) for a in down]
    width = (WIDE if wide else 0) + (DOWN if down else 0)
    rows = QUARTER + EXTRA if wide else QUARTER
    return call(
        partial(pack_kernel, bool(wide), bool(down), layer),
        hbm((rows, width)),
        (1,),
        specs,
        whole(rows, width),
        1,
        after=after,
    )(*wide, *down)


def pick_kernel(order, both, out, sems):
    copies = [
        pltpu.make_async_copy(both.at[2 * i + 1 - order[0]], out.at[i], sems.at[i])
        for i in range(2)
    ]
    for c in copies:
        c.start()
    for c in copies:
        c.wait()


def pick(order, both, after=()):
    return call(
        pick_kernel,
        sds((2,) + both.shape[1:]),
        (),
        [ANY],
        VMEM,
        1,
        scratch=[pltpu.SemaphoreType.DMA((2,))],
        scalars=1,
        after=after,
    )(order, both)


def halves(core, both, got, sems, places):
    copies = []
    for i in range(2):
        for j, (source, at) in enumerate(
            ((both.at[2 * i + core], 2 * i + core), (got.at[i], 2 * i + 1 - core))
        ):
            for n, (a, b) in enumerate(places(source, at)):
                copies.append(pltpu.make_async_copy(a, b, sems.at[2 * i + j, n]))
    for c in copies:
        c.start()
    for c in copies:
        c.wait()


def wide_places(wide, extra):
    def places(source, at):
        rows = pl.ds(at * QUARTER, QUARTER)
        return (
            (source.at[pl.ds(0, QUARTER), pl.ds(0, WIDE)], wide.at[rows]),
            (source.at[pl.ds(QUARTER, EXTRA), pl.ds(0, WIDE)], extra.at[at]),
        )

    return places


def down_places(down, start):
    def places(source, at):
        rows = pl.ds(at * QUARTER, QUARTER)
        return ((source.at[pl.ds(0, QUARTER), pl.ds(start, DOWN)], down.at[rows]),)

    return places


def vectors(extra, norms, bias):
    bias[...] = jnp.zeros_like(bias)
    norms[...] = jnp.zeros_like(norms)
    bias[0:1] = extra[0, 0:1].astype(F32)
    for q in range(4):
        cols = slice(q * QUARTER, (q + 1) * QUARTER)
        for n in range(5):
            row, at = 1 + n // 2, (n % 2) * QUARTER
            norms[n : n + 1, cols] = extra[q, row : row + 1, at : at + QUARTER].astype(F32)


def weights_kernel(order, both, got, wide, down, norms, bias, extra, sems):
    def places(source, at):
        return wide_places(wide, extra)(source, at) + down_places(down, WIDE)(source, at)

    halves(order[0], both, got, sems, places)
    vectors(extra, norms, bias)


def settle_weights(order, both, got):
    return call(
        weights_kernel,
        [sds((D, WIDE)), sds((D, DOWN)), sds((8, D), F32), hbm((8, WIDE), F32)],
        (),
        [ANY] * 2,
        [VMEM] * 4,
        2,
        scratch=[pltpu.VMEM((4, EXTRA, WIDE), BF), pltpu.SemaphoreType.DMA((4, 3))],
        scalars=1,
    )(order, both, got)


def keep_kernel(order, both, got, wide, down, mark, sems):
    mark[...] = jnp.zeros_like(mark)

    def places(source, at):
        rows = pl.ds(at * QUARTER, QUARTER)
        return (
            (source.at[pl.ds(0, QUARTER), pl.ds(0, WIDE)], wide.at[rows]),
        ) + down_places(down, WIDE)(source, at)

    halves(order[0], both, got, sems, places)


def keep_weights(order, both, got, after):
    return call(
        keep_kernel,
        [hbm((D, WIDE)), hbm((D, DOWN)), sds((8, 128), F32)],
        (),
        [ANY] * 2,
        [VMEM] * 3,
        2,
        scratch=[pltpu.SemaphoreType.DMA((4, 3))],
        scalars=1,
        after=after,
    )(order, both, got)


def gate_kernel(*refs):
    pass


def gate(arrays, after, shape=sds):
    return call(
        gate_kernel,
        [shape(a.shape, a.dtype) for a in arrays],
        (),
        [ANY] * len(arrays),
        [ANY] * len(arrays),
        0.1,
        aliases={i: i for i in range(len(arrays))},
        after=after,
    )(*(arrays if shape is sds else far(*arrays)))


def marked_gate_kernel(*refs):
    refs[-1][...] = jnp.zeros_like(refs[-1])


def marked_gate(arrays, after):
    *same, mark = call(
        marked_gate_kernel,
        [hbm(a.shape, a.dtype) for a in arrays] + [sds((8, 128), F32)],
        (),
        [ANY] * len(arrays),
        [ANY] * len(arrays) + [VMEM],
        0.1,
        aliases={i: i for i in range(len(arrays))},
        after=after,
    )(*far(*arrays))
    return same, mark


def combine_kernel(count, order, *refs):
    halves, (own, *sent), mark = refs[: 2 * count], refs[2 * count : -1], refs[-1]
    mark[...] = jnp.zeros_like(mark)
    for k, ref in zip(STEPS, [own] + sent):
        at = pl.ds(pl.multiple_of(lax.rem(order[0] + k, 4) * OWN, OWN), OWN)
        for part in range(count):
            mine, got = halves[2 * part : 2 * part + 2]
            total = mine[at, :].astype(F32) + got[at, :].astype(F32)
            ref[part * OWN : (part + 1) * OWN, :] = total.astype(ref.dtype)


def combine(order, halves, own=sds):
    count = len(halves) // 2
    rows = count * OWN
    return call(
        partial(combine_kernel, count),
        [own((rows, D), F32)] + [hbm((rows, D))] * 3 + [sds((8, 128), F32)],
        (),
        [VMEM] * len(halves),
        [VMEM] * 5,
        1.5,
        scalars=1,
    )(order, *halves)


def summed(own, others, rows):
    total = own[rows, :]
    for ref in others:
        total = total + ref[rows, :].astype(F32)
    return total


def back_through_norm(dxhat, x):
    xhat, r = normalized(x)
    mean = jnp.mean(dxhat, 1, keepdims=True)
    return r * (dxhat - mean - xhat * jnp.mean(dxhat * xhat, 1, keepdims=True))


EVERY = slice(0, OWN)


def finish_kernel(own, a, b, c, x, norms, new, xhat):
    value = x[...] + (summed(own, (a, b, c), EVERY) + norms[4:5])
    new[...] = value
    xhat[...] = normalized(value)[0].astype(BF)


def finish(parts, x, norms):
    return call(
        finish_kernel,
        [hbm((OWN, D), F32), hbm((OWN, D))],
        (),
        [VMEM] * 6,
        [VMEM] * 2,
        1.5,
    )(*parts, x, norms)


def finish_back_kernel(order, own, a, b, c, x, gradient, new, lowered, mark):
    mark[...] = jnp.zeros_like(mark)
    value = gradient[...].astype(F32) + back_through_norm(summed(own, (a, b, c), EVERY), x[...])
    new[...] = value
    lowered[...] = value.astype(BF)


def finish_back(order, parts, x, gradient):
    return call(
        finish_back_kernel,
        [hbm((OWN, D), F32), sds((OWN, D)), sds((8, 128), F32)],
        (1,),
        [whole(OWN, D)] * 5 + [pl.BlockSpec((OWN, D), lambda i, s: (s[0], 0))],
        [whole(OWN, D)] * 2 + [whole(8, 128)],
        1.5,
        scalars=1,
    )(order, *parts, x, gradient)


def finish_last_kernel(order, own, a, b, c, x_back, gradient, x_front, norms, *refs):
    outs, mark, held = refs[:4], refs[4], refs[5]
    mark[...] = jnp.zeros_like(mark)
    others = (a, b, c)
    held[EVERY, :] = gradient[...] + back_through_norm(summed(own, others, EVERY), x_back[...])
    held[OWN:, :] = x_front[...] + (summed(own, others, slice(OWN, 2 * OWN)) + norms[4:5])
    for k, ref in enumerate(outs):
        q = lax.rem(order[0] + k, 4)
        ref[...] = held[:, pl.ds(pl.multiple_of(q * QUARTER, QUARTER), QUARTER)].astype(BF)


def finish_last(order, parts, x_back, gradient, x_front, norms, after):
    return call(
        finish_last_kernel,
        [hbm((2 * OWN, QUARTER))] * 4 + [sds((8, 128), F32)],
        (),
        [VMEM] * 8,
        [VMEM] * 5,
        2,
        scratch=[pltpu.VMEM((2 * OWN, D), F32)],
        scalars=1,
        after=after,
    )(order, *parts, x_back, gradient, x_front, norms)


def land_kernel(order, *refs):
    pieces, (back, front, mark) = refs[:4], refs[4:]
    mark[...] = jnp.zeros_like(mark)
    for k, p in enumerate(pieces):
        at = pl.ds(pl.multiple_of(lax.rem(order[0] - k + 4, 4) * OWN, OWN), OWN)
        back[at, :] = p[:OWN, :].astype(F32)
        front[at, :] = p[OWN:, :]


def land(order, pieces):
    shape = (4 * OWN, QUARTER)
    return call(
        land_kernel,
        [sds(shape, F32), sds(shape), sds((8, 128), F32)],
        (),
        [VMEM] * 4,
        [VMEM] * 3,
        1,
        scalars=1,
    )(order, *pieces)


def payload_kernel(pairs, marks, *refs):
    out, mark = refs[-2:]
    mark[...] = jnp.zeros_like(mark)
    at, width = 0, 0
    out[QUARTER:, :] = jnp.zeros_like(out[QUARTER:, :])
    for rights in pairs:
        lhs = refs[at][...]
        at += 1
        for w in rights:
            out[:QUARTER, width : width + w] = dot(lhs, refs[at][...], TN).astype(BF)
            at += 1
            width += w
    for row, start, w in marks:
        out[QUARTER + row : QUARTER + row + 1, start : start + w] = refs[at][0:1, :].astype(BF)
        at += 1


def payload(pairs, extras, after=()):
    operands, specs, shape, width = [], [], [], 0
    for left, rights in pairs:
        operands.append(left)
        specs.append(pl.BlockSpec((LEN, QUARTER), lambda i: (0, i)))
        for r in rights:
            operands.append(r)
            specs.append(whole(*r.shape))
            width += r.shape[1]
        shape.append(tuple(r.shape[1] for r in rights))
    marks = []
    for row, start, vector, sliced in extras:
        operands.append(vector)
        w = QUARTER if sliced else vector.shape[1]
        specs.append(pl.BlockSpec((8, w), lambda i: (0, i)) if sliced else whole(8, w))
        marks.append((row, start, w))
    return call(
        partial(payload_kernel, tuple(shape), tuple(marks)),
        [hbm((4 * TALL, width)), sds((8, 128), F32)],
        (4,),
        specs,
        [block(TALL, width), whole(8, 128)],
        4 * (0.3 + width / 1536),
        after=after,
    )(*operands)


def share_kernel(order, part, mine, *sent):
    for k, ref in zip(STEPS, (mine,) + sent):
        at = pl.multiple_of(lax.rem(order[0] + k, 4) * SHARE, SHARE)
        ref[...] = part[:, pl.ds(at, SHARE)]


def share(order, part, after=()):
    return call(
        share_kernel,
        [sds((TALL, SHARE))] + [hbm((TALL, SHARE))] * 3,
        (),
        [VMEM],
        [VMEM] * 4,
        1.5,
        scalars=1,
        after=after,
    )(order, part)


def last_sum_kernel(own, a, b, c, out, mark):
    mark[...] = jnp.zeros_like(mark)
    total = own[...].astype(F32) + a[...].astype(F32) + b[...].astype(F32) + c[...].astype(F32)
    out[...] = total.astype(BF)


def last_sum(parts):
    return call(
        last_sum_kernel,
        [hbm((TALL, SHARE)), sds((8, 128), F32)],
        (),
        [VMEM] * 4,
        [VMEM] * 2,
        1,
    )(*parts)


def stats_kernel(a, b, c, d, scales, shifts):
    total = a[...] + b[...] + c[...] + d[...]
    for n, ref in enumerate((scales, shifts)):
        for l in range(LAYERS):
            ref[l] = total[4 * n + 2 * l : 4 * n + 2 * l + 2]


def stats_sum(parts):
    return call(
        stats_kernel,
        [sds((LAYERS, 2, QUARTER), F32)] * 2,
        (),
        [VMEM] * 4,
        [VMEM] * 2,
        1,
    )(*parts)


WIDTHS = {"triples": QKV, "expand": HID, "down": DOWN}
ROW = {"triples": 2, "expand": 0, "down": 1}


def final_kernel(layer, kinds, order, *refs):
    pieces, cols, refs = refs[:4], refs[4], refs[5:]
    shards_in = {}
    for kind in kinds:
        if kind != "down":
            shards_in[kind], refs = refs[0], refs[1:]
    if layer == 0:
        upper, refs = refs[0], refs[1 + sum(2 if k == "down" else 1 for k in kinds) :]
    held = refs[-1]
    for k, ref in zip(STEPS, pieces):
        at = pl.ds(pl.multiple_of(lax.rem(order[0] - k + 4, 4) * SHARE, SHARE), SHARE)
        held[:, at] = ref[...].astype(F32)
    start, lane = 0, lax.broadcasted_iota(jnp.int32, (QUARTER, 128), 1)
    stats = jnp.zeros((QUARTER, 128), F32)
    vectors, refs = refs[0], refs[1:]
    vectors[...] = jnp.zeros_like(vectors)
    for kind in kinds:
        w, row = WIDTHS[kind], ROW[kind]
        product = held[:QUARTER, start : start + w]
        if kind == "down":
            turned = jnp.transpose(product)
            refs[0][0] = turned[:INNER]
            refs[1][0] = turned[INNER:]
            refs = refs[2:]
            vectors[row : row + 1, :QUARTER] = held[QUARTER + row : QUARTER + row + 1, :QUARTER]
        else:
            sums = held[QUARTER + row : QUARTER + row + 1, start : start + w]
            vectors[row : row + 1, :w] = sums
            own = shards_in[kind]
            if kind == "triples":
                own = jnp.concatenate([own[0, :, i, :] for i in range(3)], 1)
            else:
                own = own[0]
            own = own.astype(F32)
            at = 0 if kind == "triples" else 1
            stats = jnp.where(lane == at, jnp.sum(own * product, 1, keepdims=True), stats)
            stats = jnp.where(lane == 2 + at, jnp.sum(own * sums, 1, keepdims=True), stats)
            value = cols[:, at : at + 1] * product + cols[:, 2 + at : 3 + at] * sums
            if kind == "triples":
                for i in range(3):
                    refs[0][0, :, i, :] = value[:, i * INNER : (i + 1) * INNER]
            else:
                refs[0][0] = value
            refs = refs[1:]
        start += w
    vectors[4:8, :QUARTER] = jnp.transpose(stats)[:4]
    if layer == 0:
        offsets, uplift, closing, joint_stats = refs[:4]
        for l, source in enumerate((vectors, upper)):
            for i in range(3):
                offsets[l, i : i + 1, :] = source[2:3, i * INNER : (i + 1) * INNER]
            uplift[l : l + 1] = source[0:1]
            closing[l : l + 1] = source[1:2, :QUARTER]
            for n in range(2):
                at = 4 * n + 2 * l
                joint_stats[at : at + 2] = source[4 + 2 * n : 6 + 2 * n, :QUARTER]


GRADS = {
    "triples": [(LAYERS, QUARTER, 3, INNER)],
    "expand": [(LAYERS, QUARTER, HID)],
    "down": [(LAYERS, INNER, QUARTER), (LAYERS, HID, QUARTER)],
}


def final(layer, kinds, order, pieces, cols, weights, stacks, upper=None):
    width = WIDE + DOWN
    operands = list(pieces) + [cols] + [weights[k] for k in kinds if k != "down"]
    if layer == 0:
        operands.append(upper)
    specs = [VMEM] * len(operands)
    shapes, outs, aliases = [sds((8, HID), F32)], [VMEM], {}
    for kind in kinds:
        for place, shape in enumerate(GRADS[kind]):
            if layer == 0:
                aliases[1 + len(operands)] = len(shapes)
                operands.append(stacks[kind][place])
                specs.append(ANY)
            shapes.append(sds(shape, F32))
            outs.append(
                pl.BlockSpec(
                    (1,) + shape[1:], lambda i, s, n=len(shape) - 1: (layer,) + (0,) * n
                )
            )
    outs[0] = whole(8, HID)
    if layer == 0:
        for shape in ((LAYERS, 3, INNER), (LAYERS, HID), (LAYERS, QUARTER), (8, QUARTER)):
            shapes.append(sds(shape, F32))
            outs.append(whole(*shape))
    fixed = [whole(*o.shape) if s is VMEM else s for o, s in zip(operands, specs)]
    for n, kind in enumerate(k for k in kinds if k != "down"):
        fixed[5 + n] = of_layer(layer, weights[kind])
    results = call(
        partial(final_kernel, layer, kinds),
        shapes,
        (1,),
        fixed,
        outs,
        2,
        scratch=[pltpu.VMEM((TALL, width), F32)],
        scalars=1,
        aliases=aliases,
    )(order, *operands)
    vectors, results = results[0], list(results[1:])
    grads = {}
    for kind in kinds:
        n = len(GRADS[kind])
        grads[kind], results = results[:n], results[n:]
    return (results if layer == 0 else vectors), grads


def across(array):
    return lax.ppermute(array, "core", [(0, 1), (1, 0)])


def around(array, axes, step):
    return lax.ppermute(array, axes, [(i, (i + step) % 4) for i in range(4)])


def exchanged(array, axes):
    return lax.ppermute(array, axes, [(0, 0), (1, 2), (2, 1), (3, 3)])


def gather_ring(own, axes):
    return [own] + [around(own, axes, k) for k in STEPS[1:]]


def gather_line(own, after=()):
    pieces = gather_ring(own, LINE)
    if after:
        pieces = pieces[:1] + list(gate(pieces[1:], after))
    return pieces + [across(p) for p in pieces]


def scatter_line(order, other, mine, early=(), own=sds):
    own, *sent, mark = combine(order, [mine, across(other), *early], own)
    return [own] + [around(s, LINE, k) for s, k in zip(sent, STEPS[1:])], mark


def outward_pairs(step):
    pairs = []
    for q in range(4):
        for zh in range(2):
            for core in range(2):
                z = (q - step) % 4
                pairs.append(((zh * 2 + core) * 4 + z, q * 4 + zh * 2 + core))
    return pairs


def outward(pieces):
    axes = ("yh", "core", "zh", "zl")
    return [lax.ppermute(p, axes, outward_pairs(k)) for k, p in enumerate(pieces)]


def tiny(array):
    return array[:16, :128]


def fetch(core, both, after):
    (both,) = far(both)
    got = across(pick(core, both, after))
    return settle_weights(core, both, got), got


def reduce_ring(array):
    return lax.psum_scatter(array, RING, scatter_dimension=0, tiled=True)


def crossed(step):
    return [
        ((x * 2 + core) * 2 + yl, ((x + step) % 4 * 2 + yl) * 2 + core)
        for x in range(4)
        for core in range(2)
        for yl in range(2)
    ]


def reduce_x(x, part, after=()):
    mine, *sent = share(x.reshape(1), far(part)[0], after)
    total, mark = last_sum([mine] + far(*[around(s, "x", k) for s, k in zip(sent, STEPS[1:])]))
    return far(*[lax.ppermute(total, ("x", "core", "yl"), crossed(k)) for k in STEPS]), mark


def shards(
    inputs, scales, shifts, triples, offsets, merger, expand, uplift, shrink, closing, cotangent
):
    core, y, z = lax.axis_index("core"), lax.axis_index(RING), lax.axis_index(LINE)
    x_at, q_at = lax.axis_index("x"), lax.axis_index(("yh", "core"))
    here, there = core.reshape(1), (1 - core).reshape(1)
    chunk = core * 4 + z
    sources = [(z - k + 4) % 4 for k in STEPS]
    tokens = jnp.stack([core * 4 + s for s in sources] + [(1 - core) * 4 + s for s in sources])
    blocks = [(s % 2) * 4 + (s // 2) * 2 for s in sources]
    features = jnp.stack([b + core for b in blocks] + [b + 1 - core for b in blocks] + [chunk])
    z_one, x_one, q_one = z.reshape(1), x_at.reshape(1), q_at.reshape(1)

    moved = exchanged(jnp.concatenate([inputs, cotangent], 0), ("yh", "zh"))
    marker = [tiny(moved)]
    wide_args = (triples, expand, scales, shifts, offsets, uplift, closing)
    down_args = (merger, shrink)
    packs = gate([pack(l, wide_args, down_args) for l in range(LAYERS)], marker)
    sent, sent1 = [lax.all_gather(p, RING, axis=0, tiled=False) for p in packs]
    pieces = gather_line(moved)
    first_pieces = pieces
    tables = rotary_tables()
    (wide, down, norms, bias), got = fetch(here, sent, [tiny(p) for p in pieces[1:4]])

    full0, slope0, query0, keys0, values0, hidden0, x0, *kept = project(
        True, features, far(*pieces), wide, norms, bias, tables
    )
    mixed0, logs0, mixed_kept = attend(query0, keys0, values0, 1)
    other = merge(there, mixed0, hidden0, down)
    mine = merge(here, mixed0, hidden0, down)
    query0, keys0, values0, hidden0, mixed0 = far(*kept, mixed_kept)
    parts, combined = scatter_line(z_one, other, mine)
    wide_kept, down_kept, kept_mark = keep_weights(here, *far(sent, got), [combined])
    late, arrived = marked_gate(parts[1:], [kept_mark])
    parts, marker = parts[:1] + late, [arrived]
    (wide1, down1, norms1, bias1), _ = fetch(here, sent1, marker)
    top, dmixed1, dhidden1, close_sum1 = branch_first(features, far(*first_pieces), down1)
    x1, xhat = finish(parts[:1] + far(*parts[1:]), x0, norms)
    pieces = gather_line(xhat, [close_sum1])

    full1, dupper1, query1, keys1, values1, hidden1, up_sum1 = project(
        False, tokens, far(pieces[0]) + pieces[1:], wide1, norms1, *far(bias1), tables, *far(dhidden1)
    )
    mixed1, logs1 = attend(query1, keys1, values1, 0)
    dqkv1, qkv_sum1 = attend_back(query1, keys1, values1, dmixed1, logs1, tables)
    other = spread(there, dqkv1, dupper1, wide1, norms1)
    mine = spread(here, dqkv1, dupper1, wide1, norms1)
    parts, combined = scatter_line(z_one, other, mine, own=hbm)
    grad1, done1 = payload(
        [(far(full1)[0], [dqkv1, dupper1]), (far(top)[0], [mixed1, hidden1])],
        [(2, 0, qkv_sum1, False), (0, QKV, up_sum1, False), (1, 0, close_sum1, True)],
        [combined],
    )
    late, arrived = marked_gate(parts[1:], [done1])
    gradient, lowered, mark = finish_back(
        chunk.reshape(1), far(parts[0], *late), *far(x1, top)
    )
    (grad1,) = gate([grad1], [arrived], hbm)
    grad1 = reduce_ring(grad1)

    other = merge(there, mixed1, hidden1, down1, [mark])
    mine = merge(here, mixed1, hidden1, down1, [mark])
    front = [mine, across(other)]
    pieces = gather_line(lowered, [tiny(mine)])

    dmixed0, dupper0, up_sum0, close_sum0, dy0 = branch(
        tokens, pieces, *far(down_kept, slope0)
    )
    dqkv0, qkv_sum0 = attend_back(query0, keys0, values0, dmixed0, logs0, far(*tables))
    grad0, done0 = payload(
        [(far(full0)[0], [dqkv0, dupper0]), (dy0, [mixed0, hidden0])],
        [(2, 0, qkv_sum0, False), (0, QKV, up_sum0, False), (1, 0, close_sum0, True)],
    )
    grad0 = reduce_ring(grad0)

    reduced1, summed1 = reduce_x(x_at, grad1, [done0])
    rest = (dqkv0, dupper0, far(wide_kept)[0], norms, [done0])
    other = spread(there, *rest)
    mine = spread(here, *rest)
    parts, _ = scatter_line(z_one, other, mine, front)
    *pieces, finished = finish_last(
        z_one, parts[:1] + far(*parts[1:]), *far(x0, gradient, x1), norms1, [summed1])
    inputs_grad, outputs, landed = land(q_one, far(*outward(pieces)))
    cols = [
        jnp.concatenate([scales[l], shifts[l]], 0).astype(F32).T for l in range(LAYERS)
    ]
    weights = {"triples": triples, "expand": expand}
    upper, stacks = final(
        1, ("triples", "expand", "down"), x_one, reduced1, cols[1], weights, None
    )
    reduced, _ = reduce_x(x_at, grad0, [finished])
    (offsets_grad, uplift_grad, closing_grad, stats), stacks = final(
        0, ("triples", "expand", "down"), x_one, reduced, cols[0], weights, stacks, upper
    )
    stats = stats + lax.ppermute(stats, "yl", [(0, 1), (1, 0)])
    scales_grad, shifts_grad = stats_sum(gather_ring(stats, LINE))
    return (
        outputs,
        inputs_grad,
        scales_grad,
        shifts_grad,
        stacks["triples"][0],
        offsets_grad,
        stacks["down"][0],
        stacks["expand"][0],
        uplift_grad,
        stacks["down"][1],
        closing_grad,
    )


def solution(mesh):
    grid = Mesh(mesh.devices.reshape(4, 2, 2, 2, 2, 2), AXES)
    row, col = ("yh", "core"), ("yl", "zh", "zl")
    tokens = P(("x",) + col, row)
    weights = (
        P(None, None, row),
        P(None, None, row),
        P(None, row, None, col),
        P(None, None, col),
        P(None, col, row),
        P(None, row, col),
        P(None, col),
        P(None, col, row),
        P(None, row),
    )
    return jax.shard_map(
        shards,
        mesh=grid,
        in_specs=(tokens,) + weights + (tokens,),
        out_specs=(tokens, tokens) + weights,
        check_vma=False,
    )
```
